128 devices in a mesh: orb: 64 (over z, y, x), grid: 2 (over core).
Axes of the slice: x: 4, y: 4, z: 4, core: 2. Of those that a mesh axis runs over, the one named last changes fastest.
Arguments:
- coefficients: bfloat16 [192, 128, 128, 128], P('orb', None, 'grid'), may hold values from -8 to 8
- occupations: int32 [192], replicated, may hold values from 0 to 2
- slot_orbital: int32 [192], replicated, may hold values from 0 to 191, each once
Outputs:
- updated: bfloat16 [192, 128, 128, 128], P('orb', None, 'grid')
- orbital_energies: float32 [192], P('orb')
- potential: float32 [128, 128, 128], P('orb', 'grid')
The draws below stay inside these ranges and needn't reach their ends.
Inputs may be any that keep to these rules, and one draw needn't show every extreme that they name: `slot_orbital`: every orbital number appears once.
All inputs are finite; a program needn't handle non-finite values.
Results may differ from the reference program's by a relative error of at most 0.0008.
The reference program's roundings to bfloat16 on the way count: a program that leaves them out, or rounds other values in their place, can miss the bound.
Values may be sent and summed in bfloat16 or wider, within the bound.
No kernel may reach another device: no remote copies, remote signals or barrier semaphores. Data moves between devices by JAX's collectives and lax.ppermute only.
A program may use at most 192 MiB of HBM per device.

```python
import math
import jax
import jax.numpy as jnp
from jax import lax

G = 128
ORBS = 192


def smooth_profile(key, noise_scale, smooth_scale, noise):
    phase_key, wave_key, shift_key = jax.random.split(key, 3)
    phases = jax.random.uniform(phase_key, (ORBS, 1, 1, 1), jnp.float32, 0.0, 1.0)
    waves = jax.random.randint(wave_key, (3, ORBS, 1, 1, 1), 1, 4).astype(jnp.float32)
    shifts = jax.random.uniform(shift_key, (3, ORBS, 1, 1, 1), jnp.float32, 0.0, 2.0 * math.pi)
    cells = jnp.arange(G, dtype=jnp.int32).astype(jnp.float32) / G
    depth_pos = cells[None, :, None, None]
    width_pos = cells[None, None, :, None]
    last_pos = cells[None, None, None, :]
    rough_amp = 0.55 + 0.45 * jnp.cos(2.0 * math.pi * (width_pos + phases))
    smooth = jnp.cos(2.0 * math.pi * waves[0] * depth_pos + shifts[0])
    smooth = smooth * jnp.cos(2.0 * math.pi * waves[1] * width_pos + shifts[1])
    smooth = smooth * jnp.cos(2.0 * math.pi * waves[2] * last_pos + shifts[2])
    return noise * noise_scale * rough_amp + smooth_scale * smooth


def draw_coefficients(key, part):
    key = jax.random.fold_in(key, 11)
    noise_key, shape_key = jax.random.split(key)
    shape_all = (ORBS, G, G, G)
    noise = jax.random.truncated_normal(noise_key, -4.0, 4.0, shape_all, jnp.float32)
    values = smooth_profile(shape_key, 1.5, 1.5, noise)
    return values.astype(jnp.bfloat16)


def plant(drawn, key, least, high):
    index_at = [jax.random.randint(jax.random.fold_in(key, axis), (), 0, length) for axis, length in enumerate(drawn.shape)]
    main_axis = drawn.shape.index(max(drawn.shape))
    neighbour = index_at[:main_axis] + [(index_at[main_axis] + 1) % drawn.shape[main_axis]] + index_at[main_axis + 1:]
    return drawn.at[tuple(index_at)].set(least).at[tuple(neighbour)].set(high)


def setup_inputs(seed: int = 0) -> dict:
    key_list = jax.random.split(jax.random.key(seed), 4)
    return {
        "coefficients": draw_coefficients(jax.random.fold_in(key_list[3], 71), 0),
        "occupations": plant(jax.random.randint(key_list[1], (ORBS,), 0, 3), jax.random.fold_in(key_list[1], 1), 0, 2).astype(jnp.int32),
        "slot_orbital": jax.random.permutation(key_list[2], ORBS).astype(jnp.int32),
    }


MAGIC = (8.4334247333529341094733325815816e-7, -1.290557201342060969516786758559028e-5, 8.762984476210559564689161894116397e-5, -3.0158038132690463167163703826169879e-4, 1.74723713672993903449447812749852942e-3, -9.42047030201080385922711540948195075e-3, 2.373821463724942397566389712597274535e-2, 6.12625895831207982195380597e-2, 9.940415697834003993178616713e-1, -6.04895289196983516002834636e-2, -2.103025160930381434955489412839065067e-2, 1.337263414854794752733423467013220997e-2, -3.44128144493493857280881509686821861e-3, 4.9443227688689919192282259476750972e-4, -5.185986881173432922848639136911487e-5, 2.72734492911979659657715313017228e-6)
STEP_SIZE = 0.1
COULOMB = 4.0 * math.pi


def magic_pairs():
    return [(position - 8, MAGIC[position]) for position in range(16)]


def transposed_pairs():
    return [(8 - position, MAGIC[position]) for position in range(16)]


def kinetic_pairs():
    spread = 14
    weights = []
    for distance in range(1, spread + 1):
        numerator = 2.0 * (-1.0) ** (distance + 1) * math.factorial(spread) ** 2
        weights.append(numerator / (distance * distance * math.factorial(spread - distance) * math.factorial(spread + distance)))
    result = [(0, -2.0 * sum(weights))]
    for distance in range(1, spread + 1):
        result.append((distance, weights[distance - 1]))
        result.append((-distance, weights[distance - 1]))
    return result


def band_matrix(length, pairs):
    rows_in = lax.broadcasted_iota(jnp.int32, (length, length), 0)
    cols_out = lax.broadcasted_iota(jnp.int32, (length, length), 1)
    distance = rows_in - cols_out
    matrix = jnp.zeros((length, length), jnp.float32)
    for offset_cells, weight in pairs:
        rounded = jnp.asarray(weight, jnp.float32).astype(jnp.bfloat16).astype(jnp.float32)
        matches = jnp.mod(distance - offset_cells, length) == 0
        matrix = matrix + jnp.where(matches, rounded, jnp.float32(0.0))
    return matrix


def along(field, matrix, axis_number):
    values = field.astype(jnp.float32)
    highest = lax.Precision.HIGHEST
    if axis_number == 0:
        return jnp.einsum("ji,jxy->ixy", matrix, values, precision=highest)
    if axis_number == 1:
        return jnp.einsum("ji,zjy->ziy", matrix, values, precision=highest)
    return jnp.einsum("zxj,ji->zxi", values, matrix, precision=highest)


def real_orbital(coeff, magic):
    first_pass = along(coeff, magic, 2).astype(jnp.bfloat16)
    second_pass = along(first_pass, magic, 1).astype(jnp.bfloat16)
    return along(second_pass, magic, 0).astype(jnp.bfloat16)


def coulomb_kernel(length):
    waves = jnp.arange(length, dtype=jnp.int32).astype(jnp.float32)
    curve = 2.0 - 2.0 * jnp.cos(waves * (2.0 * math.pi / length))
    summed = curve[:, None, None] + curve[None, :, None] + curve[None, None, :]
    grid_index = jnp.arange(length, dtype=jnp.int32)
    anchor = (grid_index[:, None, None] == 0) & (grid_index[None, :, None] == 0) & (grid_index[None, None, :] == 0)
    return jnp.where(anchor, jnp.float32(0.0), COULOMB / jnp.where(anchor, jnp.float32(1.0), summed))


def reference(coefficients, occupations, slot_orbital):
    total_slots = coefficients.shape[0]
    length = coefficients.shape[1]
    magic = band_matrix(length, magic_pairs())
    transposed = band_matrix(length, transposed_pairs())
    kinetic = band_matrix(length, kinetic_pairs())
    catalog = jnp.arange(total_slots, dtype=jnp.int32)
    occupancy = jnp.sum(jnp.where(slot_orbital[:, None] == catalog[None, :], occupations[None, :], 0), axis=1)
    weights = occupancy.astype(jnp.float32) / total_slots

    def accumulate(density, inputs):
        coeff, weight = inputs
        psi_values = real_orbital(coeff, magic).astype(jnp.float32)
        return density + weight * psi_values * psi_values, None

    density, _ = lax.scan(accumulate, jnp.zeros((length, length, length), jnp.float32), (coefficients, weights))
    spectrum = jnp.fft.fftn(density)
    potential = jnp.real(jnp.fft.ifftn(spectrum * coulomb_kernel(length))).astype(jnp.float32)

    def apply_one(coeff):
        psi_values = real_orbital(coeff, magic)
        product = (potential * psi_values.astype(jnp.float32)).astype(jnp.bfloat16)
        back_z = along(product, transposed, 0).astype(jnp.bfloat16)
        back_zx = along(back_z, transposed, 1).astype(jnp.bfloat16)
        second = along(coeff, kinetic, 0) + along(coeff, kinetic, 1) + along(coeff, kinetic, 2)
        applied = -0.5 * second + along(back_zx, transposed, 2)
        coeff_wide = coeff.astype(jnp.float32)
        energy = jnp.sum(coeff_wide * applied) / jnp.sum(coeff_wide * coeff_wide)
        updated = (coeff_wide - STEP_SIZE * (applied - energy * coeff_wide)).astype(jnp.bfloat16)
        return updated, energy

    updated, energies = lax.map(apply_one, coefficients)
    return updated, energies, potential
```

```python
import functools
import math

import jax
import jax.numpy as jnp
import ml_dtypes
import numpy as np
from jax import lax
from jax.experimental import pallas as pl
from jax.experimental.pallas import tpu as pltpu
from jax.sharding import PartitionSpec as P

MAGIC = (
    8.433424733352934e-07,
    -1.290557201342061e-05,
    8.76298447621056e-05,
    -0.00030158038132690465,
    0.001747237136729939,
    -0.009420470302010804,
    0.023738214637249424,
    0.0612625895831208,
    0.9940415697834004,
    -0.06048952891969835,
    -0.021030251609303816,
    0.013372634148547948,
    -0.0034412814449349387,
    0.0004944322768868992,
    -5.185986881173433e-05,
    2.7273449291197967e-06,
)
STEP_SIZE = 0.1
COULOMB = 4.0 * math.pi
LEVELS = 32000.0
FINE = 16384.0
F32 = jnp.float32
BF16 = jnp.bfloat16
HIGHEST = lax.Precision.HIGHEST
VMEM_LIMIT = 56 * 1024 * 1024


def magic_pairs():
    return [(position - 8, MAGIC[position]) for position in range(16)]


def transposed_pairs():
    return [(8 - position, MAGIC[position]) for position in range(16)]


def kinetic_pairs():
    spread = 14
    weights = []
    for distance in range(1, spread + 1):
        numerator = 2.0 * (-1.0) ** (distance + 1) * math.factorial(spread) ** 2
        weights.append(
            numerator
            / (
                distance
                * distance
                * math.factorial(spread - distance)
                * math.factorial(spread + distance)
            )
        )
    result = [(0, -2.0 * sum(weights))]
    for distance in range(1, spread + 1):
        result.append((distance, weights[distance - 1]))
        result.append((-distance, weights[distance - 1]))
    return result


def rounded(weight):
    return np.float32(np.float32(weight).astype(ml_dtypes.bfloat16))


def band_periodic(length, pairs, scale=1.0):
    matrix = np.zeros((length, length), np.float32)
    for offset, weight in pairs:
        for i in range(length):
            matrix[i, (i + offset) % length] += scale * rounded(weight)
    return matrix.astype(ml_dtypes.bfloat16)


def band_open(length, margin, pairs, scale=1.0):
    matrix = np.zeros((length, length + 2 * margin), np.float32)
    for offset, weight in pairs:
        for i in range(length):
            matrix[i, i + offset + margin] += scale * rounded(weight)
    return matrix.astype(ml_dtypes.bfloat16)


def hartley(length):
    index = np.arange(length)
    angle = 2.0 * np.pi * ((index[:, None] * index[None, :]) % length) / length
    return ((np.cos(angle) + np.sin(angle)) / math.sqrt(length)).astype(np.float32)


def curve(length):
    return 2.0 - 2.0 * np.cos(2.0 * np.pi * np.arange(length) / length)


def dot(a, b):
    return jnp.dot(a, b, preferred_element_type=F32)


def dot_exact(a, b):
    return jnp.dot(a, b, preferred_element_type=F32, precision=HIGHEST)


def params(count):
    return pltpu.CompilerParams(
        dimension_semantics=("arbitrary",) * count, vmem_limit_bytes=VMEM_LIMIT
    )


def whole(array):
    zeros = (0,) * array.ndim
    return pl.BlockSpec(array.shape, lambda *_: zeros)


def scale_of(largest):
    largest = jnp.maximum(largest, 1e-30)
    code = jnp.ceil(jnp.log2(largest))
    power = jnp.exp2(code)
    units = jnp.ceil(largest / power * FINE) + 1.0
    return code, units, units * (1.0 / FINE) * power


def coded_rows(cells_y, codes):
    row = lax.broadcasted_iota(jnp.int32, (16, cells_y), 0)
    values = jnp.zeros((16, cells_y), F32)
    for k, code in enumerate(codes):
        values = jnp.where(row == k, code, values)
    return values.astype(jnp.int32).astype(jnp.int16)


def density_kernel(
    occ_ref, slot_ref, c_ref, h_ref, my_ref, ax_ref, mz_ref, dht_ref, psi_ref, q_ref, mid, dens
):
    orbital = pl.program_id(0)
    chunk = pl.program_id(1)
    orbitals = pl.num_programs(0)
    chunks = pl.num_programs(1)
    cells_z, cells_x, cells_y = c_ref.shape[1], c_ref.shape[2], c_ref.shape[3]
    length = cells_z * chunks
    block = 8
    first = lax.axis_index("orb") * orbitals
    weight = occ_ref[slot_ref[first + orbital]].astype(F32) / slot_ref.shape[0]
    my = my_ref[...]
    ax = ax_ref[...]
    mz = mz_ref[...]

    def planes(i, carry):
        z0 = i * block
        ext = jnp.concatenate(
            [
                h_ref[0, pl.ds(z0, block), 0:16, :],
                c_ref[0, pl.ds(z0, block)],
                h_ref[0, pl.ds(z0, block), 16:32, :],
            ],
            axis=1,
        )
        wide = ext.shape[1]
        mag_y = dot(ext.reshape(block * wide, cells_y), my).astype(BF16)
        mag_y = mag_y.reshape(block, wide, cells_y)
        for p in range(0, block, 2):
            both = dot(ax, jnp.concatenate([mag_y[p], mag_y[p + 1]], axis=1))
            row = (chunk * cells_z + z0 + p) * cells_x
            mid[pl.ds(pl.multiple_of(row, cells_x), cells_x), :] = both[:, :cells_y]
            mid[pl.ds(pl.multiple_of(row + cells_x, cells_x), cells_x), :] = both[:, cells_y:]
        return carry

    lax.fori_loop(0, cells_z // block, planes, 0)

    @pl.when((orbital == 0) & (chunk == 0))
    def _():
        dens[...] = jnp.zeros_like(dens)

    @pl.when(chunk == chunks - 1)
    def _():
        def columns(i, carry):
            x = 2 * i
            pair = jnp.concatenate(
                [
                    mid[pl.ds(x, length, stride=cells_x), :].astype(BF16),
                    mid[pl.ds(x + 1, length, stride=cells_x), :].astype(BF16),
                ],
                axis=1,
            )
            values = dot(mz, pair).astype(BF16)
            for k in range(2):
                psi = values[:, k * cells_y : (k + 1) * cells_y]
                psi_ref[0, x + k] = psi
                psi = psi.astype(F32)
                dens[x + k] = dens[x + k] + weight * (psi * psi)
            return carry

        lax.fori_loop(0, cells_x // 2, columns, 0, unroll=2)

    @pl.when((orbital == orbitals - 1) & (chunk == chunks - 1))
    def _():
        dht = dht_ref[...]

        def total(x, acc):
            return acc + dens[x]

        summed = lax.fori_loop(0, cells_x, total, jnp.zeros((length, cells_y), F32), unroll=4)
        mean = jnp.sum(summed) / (length * cells_x * cells_y)
        mean_code, mean_fine, mean_step = scale_of(mean)
        mean_units = jnp.round(mean * (LEVELS / mean_step))
        mean = mean_units * (mean_step * (1.0 / LEVELS))

        def transform(i, largest):
            x = 2 * i
            pair = jnp.concatenate([dens[x] - mean, dens[x + 1] - mean], axis=1)
            waves = dot_exact(dht, pair)
            for k in range(2):
                part = waves[:, k * cells_y : (k + 1) * cells_y]
                mid[pl.ds(x + k, length, stride=cells_x), :] = part
                largest = jnp.maximum(largest, jnp.abs(part))
            return largest

        largest = lax.fori_loop(
            0, cells_x // 2, transform, jnp.zeros((length, cells_y), F32), unroll=2
        )
        code, fine, top = scale_of(jnp.max(largest))
        factor = LEVELS / top
        code_rows = coded_rows(cells_y, (code, fine, mean_code, mean_fine, mean_units))
        per = length // q_ref.shape[0]

        def quantise(i, carry):
            rows = per * cells_x
            values = mid[pl.ds(pl.multiple_of(i * rows, rows), rows), :] * factor
            q_ref[i, 0:rows, :] = jnp.round(values).astype(jnp.int32).astype(jnp.int16)
            q_ref[i, rows : rows + 16, :] = code_rows
            return carry

        lax.fori_loop(0, q_ref.shape[0], quantise, 0, unroll=2)


def density(occupations, slot_orbital, c, halo, my, ax, mz, dht, owners):
    orbitals, length, cells_x, cells_y = c.shape
    chunks = 4
    part = length // chunks
    smem = pl.BlockSpec(memory_space=pltpu.SMEM)
    rows = (length // owners) * cells_x + 16
    return pl.pallas_call(
        density_kernel,
        grid=(orbitals, chunks),
        in_specs=[
            smem,
            smem,
            pl.BlockSpec((1, part, cells_x, cells_y), lambda o, j: (o, j, 0, 0)),
            pl.BlockSpec((1, part, halo.shape[2], cells_y), lambda o, j: (o, j, 0, 0)),
            whole(my),
            whole(ax),
            whole(mz),
            whole(dht),
        ],
        out_specs=[
            pl.BlockSpec((1, cells_x, length, cells_y), lambda o, j: (o, 0, 0, 0)),
            pl.BlockSpec((owners, rows, cells_y), lambda o, j: (0, 0, 0)),
        ],
        out_shape=[
            jax.ShapeDtypeStruct((orbitals, cells_x, length, cells_y), BF16),
            jax.ShapeDtypeStruct((owners, rows, cells_y), jnp.int16),
        ],
        scratch_shapes=[
            pltpu.VMEM((length * cells_x, cells_y), F32),
            pltpu.VMEM((cells_x, length, cells_y), F32),
        ],
        compiler_params=params(2),
        name="density",
    )(occupations, slot_orbital, c, halo, my, ax, mz, dht)


def kinetic_kernel(c_ref, h_ref, dy_ref, dx_ref, dz_ref, kin_ref, sums_ref, wide_c, acc):
    length, cells_x, cells_y = c_ref.shape[1], c_ref.shape[2], c_ref.shape[3]
    block = 8
    dy = dy_ref[...]
    dx = dx_ref[...]
    dz = dz_ref[...]

    def widen(i, carry):
        rows = block * cells_x
        values = c_ref[0, pl.ds(i * block, block)].reshape(rows, cells_y)
        wide_c[pl.ds(pl.multiple_of(i * rows, rows), rows), :] = values.astype(F32)
        return carry

    lax.fori_loop(0, length // block, widen, 0)

    def columns(i, carry):
        x = 2 * i
        pair = jnp.concatenate(
            [
                wide_c[pl.ds(x, length, stride=cells_x), :].astype(BF16),
                wide_c[pl.ds(x + 1, length, stride=cells_x), :].astype(BF16),
            ],
            axis=1,
        )
        values = dot(dz, pair)
        acc[pl.ds(x, length, stride=cells_x), :] = values[:, :cells_y]
        acc[pl.ds(x + 1, length, stride=cells_x), :] = values[:, cells_y:]
        return carry

    lax.fori_loop(0, cells_x // 2, columns, 0, unroll=2)

    def planes(i, carry):
        energy, norm = carry
        z0 = i * block
        own = c_ref[0, pl.ds(z0, block)]
        ext = jnp.concatenate(
            [h_ref[0, pl.ds(z0, block), 0:16, :], own, h_ref[0, pl.ds(z0, block), 16:32, :]],
            axis=1,
        )
        rows = block * cells_x
        along_y = dot(own.reshape(rows, cells_y), dy)
        for p in range(0, block, 2):
            along_x = dot(dx, jnp.concatenate([ext[p], ext[p + 1]], axis=1))
            for k in range(2):
                z = z0 + p + k
                at = pl.ds(pl.multiple_of(z * cells_x, cells_x), cells_x)
                value = (
                    acc[at, :]
                    + along_x[:, k * cells_y : (k + 1) * cells_y]
                    + along_y[(p + k) * cells_x : (p + k + 1) * cells_x]
                )
                kin_ref[0, z] = value
                coeff = own[p + k].astype(F32)
                energy = energy + coeff * value
                norm = norm + coeff * coeff
        return energy, norm

    zeros = jnp.zeros((cells_x, cells_y), F32)
    energy, norm = lax.fori_loop(0, length // block, planes, (zeros, zeros))
    sums_ref[0, 0] = jnp.sum(energy.reshape(cells_x // 8, 8, cells_y), axis=0)
    sums_ref[0, 1] = jnp.sum(norm.reshape(cells_x // 8, 8, cells_y), axis=0)


def kinetic(c, halo, dy, dx, dz):
    orbitals, length, cells_x, cells_y = c.shape
    cells = orbitals * length * cells_x * cells_y
    return pl.pallas_call(
        kinetic_kernel,
        grid=(orbitals,),
        in_specs=[
            pl.BlockSpec((1, length, cells_x, cells_y), lambda o: (o, 0, 0, 0)),
            pl.BlockSpec((1, length, halo.shape[2], cells_y), lambda o: (o, 0, 0, 0)),
            whole(dy),
            whole(dx),
            whole(dz),
        ],
        out_specs=[
            pl.BlockSpec((1, length, cells_x, cells_y), lambda o: (o, 0, 0, 0)),
            pl.BlockSpec((1, 2, 8, cells_y), lambda o: (o, 0, 0, 0)),
        ],
        out_shape=[
            jax.ShapeDtypeStruct((orbitals, length, cells_x, cells_y), F32),
            jax.ShapeDtypeStruct((orbitals, 2, 8, cells_y), F32),
        ],
        scratch_shapes=[
            pltpu.VMEM((length * cells_x, cells_y), F32),
            pltpu.VMEM((length * cells_x, cells_y), F32),
        ],
        compiler_params=params(1),
        cost_estimate=pl.CostEstimate(
            flops=cells * 768 * 4, bytes_accessed=cells * 7, transcendentals=0
        ),
        name="kinetic",
    )(c, halo, dy, dx, dz)


def unpacked(ref, source, rows):
    codes = ref[source, rows : rows + 16, :].astype(jnp.int32).astype(F32)
    powers = jnp.exp2(codes) * (1.0 / (LEVELS * FINE))
    step = codes[1:2] * powers[0:1]
    mean = codes[4:5] * (codes[3:4] * powers[2:3])
    return ref[source, 0:rows, :].astype(jnp.int32).astype(F32) * step, mean


def sum_kernel(per, got_ref, out_ref):
    rows = out_ref.shape[0]
    cells_y = out_ref.shape[1]

    def body(source, carry):
        total, means = carry
        values, mean = unpacked(got_ref, source, rows)
        return total + values, means + mean

    total, means = lax.fori_loop(
        0,
        got_ref.shape[0],
        body,
        (jnp.zeros((rows, cells_y), F32), jnp.zeros((1, cells_y), F32)),
        unroll=2,
    )
    length = got_ref.shape[0] * per
    row = lax.broadcasted_iota(jnp.int32, (rows, cells_y), 0)
    flat = (lax.axis_index("orb") == 0) & (row < rows // per)
    out_ref[...] = total + jnp.where(flat, means * math.sqrt(length), 0.0)


def slab_sum(got, rows, per):
    return pl.pallas_call(
        functools.partial(sum_kernel, per),
        out_shape=jax.ShapeDtypeStruct((rows, got.shape[2]), F32),
        compiler_params=pltpu.CompilerParams(vmem_limit_bytes=VMEM_LIMIT),
        name="slab_sum",
    )(got)


def solve_kernel(curve_z_ref, slab_ref, dht_ref, curve_x_ref, curve_y_ref, q_ref):
    per, length, cells_y = slab_ref.shape
    cells_x = length // 2
    orb = lax.axis_index("orb")
    corner = pl.multiple_of(lax.axis_index("grid") * cells_x, cells_x)
    dht = dht_ref[...]
    own = dht_ref[pl.ds(corner, cells_x), :]
    row = lax.broadcasted_iota(jnp.int32, (length, cells_y), 0)
    col = lax.broadcasted_iota(jnp.int32, (length, cells_y), 1)
    plane_curve = curve_x_ref[...] + curve_y_ref[...]
    parts = []
    for k in range(per):
        wave = orb * per + k
        anchor = (row == 0) & (col == 0) & (wave == 0)
        bent = plane_curve + curve_z_ref[wave]
        factor = jnp.where(anchor, 0.0, COULOMB / jnp.where(anchor, 1.0, bent))
        spectrum = dot_exact(dot_exact(dht, slab_ref[k]), dht) * factor
        parts.append(dot_exact(dot_exact(own, spectrum), dht))
    field = jnp.concatenate(parts, axis=0)
    code, fine, top = scale_of(jnp.max(jnp.abs(field)))
    coded = jnp.round(field * (LEVELS / top)).astype(jnp.int32).astype(jnp.int16)
    code_rows = coded_rows(cells_y, (code, fine))
    rows = per * cells_x

    def spread(i, carry):
        q_ref[i, 0:rows, :] = coded
        q_ref[i, rows : rows + 16, :] = code_rows
        return carry

    lax.fori_loop(0, q_ref.shape[0], spread, 0)


def solve(curve_z, slab, dht, curve_x, curve_y, owners):
    per, length, cells_y = slab.shape
    vmem = pl.BlockSpec(memory_space=pltpu.VMEM)
    return pl.pallas_call(
        solve_kernel,
        in_specs=[pl.BlockSpec(memory_space=pltpu.SMEM), vmem, vmem, vmem, vmem],
        out_shape=jax.ShapeDtypeStruct((owners, per * (length // 2) + 16, cells_y), jnp.int16),
        compiler_params=pltpu.CompilerParams(vmem_limit_bytes=VMEM_LIMIT),
        name="solve",
    )(curve_z, slab, dht, curve_x, curve_y)


def field_kernel(got_ref, psi_ref, dht_ref, tz_ref, back_ref, slab_ref, sums_ref, waves):
    step = pl.program_id(0)
    orbitals, some_x, length, cells_y = psi_ref.shape
    owners = got_ref.shape[0]
    cells_x = waves.shape[0] // length
    per = length // owners
    rows = per * cells_x
    dht = dht_ref[...]
    tz = tz_ref[...]
    first = lax.axis_index("orb") * per

    @pl.when(step == 0)
    def _():
        def unpack(source, carry):
            at = pl.ds(pl.multiple_of(source * rows, rows), rows)
            waves[at, :] = unpacked(got_ref, source, rows)[0]
            return carry

        lax.fori_loop(0, owners, unpack, 0, unroll=2)
        sums_ref[...] = jnp.zeros_like(sums_ref)

    def columns(i, carry):
        local = 2 * i
        x = step * some_x + local
        pair = jnp.concatenate(
            [
                waves[pl.ds(x, length, stride=cells_x), :],
                waves[pl.ds(x + 1, length, stride=cells_x), :],
            ],
            axis=1,
        )
        field = dot_exact(dht, pair)
        slab_ref[local] = field[:, :cells_y]
        slab_ref[local + 1] = field[:, cells_y:]
        new = []
        for o in range(orbitals):
            psi = jnp.concatenate([psi_ref[o, local], psi_ref[o, local + 1]], axis=1).astype(F32)
            product = field * psi
            squares = product * psi
            squares = squares[:, :cells_y] + squares[:, cells_y:]
            new.append(carry[o] + jnp.sum(squares.reshape(length // 8, 8, cells_y), axis=0))
            back = dot(tz, product.astype(BF16)).astype(BF16)
            back_ref[o, local] = back[:, :cells_y]
            back_ref[o, local + 1] = back[:, cells_y:]
        return tuple(new)

    zeros = jnp.zeros((8, cells_y), F32)
    energy = lax.fori_loop(0, some_x // 2, columns, (zeros,) * orbitals, unroll=2)
    for o in range(orbitals):
        sums_ref[o] = sums_ref[o] + energy[o]


def field(got, psi, dht, tz):
    orbitals, cells_x, length, cells_y = psi.shape
    chunks = 8
    part = cells_x // chunks
    return pl.pallas_call(
        field_kernel,
        grid=(chunks,),
        in_specs=[
            whole(got),
            pl.BlockSpec((orbitals, part, length, cells_y), lambda i: (0, i, 0, 0)),
            whole(dht),
            whole(tz),
        ],
        out_specs=[
            pl.BlockSpec((orbitals, part, length, cells_y), lambda i: (0, i, 0, 0)),
            pl.BlockSpec((part, length, cells_y), lambda i: (i, 0, 0)),
            pl.BlockSpec((orbitals, 8, cells_y), lambda i: (0, 0, 0)),
        ],
        out_shape=[
            jax.ShapeDtypeStruct((orbitals, cells_x, length, cells_y), BF16),
            jax.ShapeDtypeStruct((cells_x, length, cells_y), F32),
            jax.ShapeDtypeStruct((orbitals, 8, cells_y), F32),
        ],
        scratch_shapes=[pltpu.VMEM((length * cells_x, cells_y), F32)],
        compiler_params=params(1),
        name="field",
    )(got, psi, dht, tz)


def update_kernel(
    energy_ref, back_ref, low_ref, high_ref, c_ref, kin_ref, tx_ref, ty_ref, out_ref, wide
):
    orbital = pl.program_id(0)
    cells_x, some_z, cells_y = back_ref.shape[1], back_ref.shape[2], back_ref.shape[3]
    margin = low_ref.shape[1]
    energy = energy_ref[orbital]
    tx = tx_ref[...]
    ty = ty_ref[...]

    def put(row, values):
        count = values.shape[0] * some_z
        wide[pl.ds(pl.multiple_of(row, some_z), count), :] = values.reshape(count, cells_y).astype(
            F32
        )

    put(0, low_ref[0])
    put((margin + cells_x) * some_z, high_ref[0])

    def widen(i, carry):
        put((margin + 8 * i) * some_z, back_ref[0, pl.ds(8 * i, 8)])
        return carry

    lax.fori_loop(0, cells_x // 8, widen, 0)
    total = cells_x + 2 * margin
    block = 4

    def planes(i, carry):
        z0 = i * block
        crossed = []
        for p in range(0, block, 2):
            pair = jnp.concatenate(
                [
                    wide[pl.ds(z0 + p, total, stride=some_z), :].astype(BF16),
                    wide[pl.ds(z0 + p + 1, total, stride=some_z), :].astype(BF16),
                ],
                axis=1,
            )
            both = dot(tx, pair).astype(BF16)
            crossed += [both[:, :cells_y], both[:, cells_y:]]
        potential = dot(jnp.concatenate(crossed, axis=0), ty)
        for p in range(block):
            z = z0 + p
            applied = potential[p * cells_x : (p + 1) * cells_x] + kin_ref[0, z]
            coeff = c_ref[0, z].astype(F32)
            out_ref[0, z] = (coeff - STEP_SIZE * (applied - energy * coeff)).astype(BF16)
        return carry

    lax.fori_loop(0, some_z // block, planes, 0, unroll=2)


def update(energies, back, low, high, c, kin, tx, ty):
    orbitals, length, cells_x, cells_y = c.shape
    chunks = 4
    part = length // chunks
    margin = low.shape[1]

    def x_major(count):
        return pl.BlockSpec((1, count, part, cells_y), lambda o, j: (o, 0, j, 0))

    z_major = pl.BlockSpec((1, part, cells_x, cells_y), lambda o, j: (o, j, 0, 0))
    return pl.pallas_call(
        update_kernel,
        grid=(orbitals, chunks),
        in_specs=[
            pl.BlockSpec(memory_space=pltpu.SMEM),
            x_major(cells_x),
            x_major(margin),
            x_major(margin),
            z_major,
            z_major,
            whole(tx),
            whole(ty),
        ],
        out_specs=z_major,
        out_shape=jax.ShapeDtypeStruct(c.shape, BF16),
        scratch_shapes=[pltpu.VMEM(((cells_x + 2 * margin) * part, cells_y), F32)],
        compiler_params=params(2),
        name="update",
    )(energies, back, low, high, c, kin, tx, ty)


def to_other(array):
    return lax.ppermute(array, "grid", [(0, 1), (1, 0)])


def to_all(blocks):
    return lax.all_to_all(blocks, "orb", split_axis=0, concat_axis=0, tiled=True)


def on_device(coefficients, occupations, slot_orbital):
    orbitals, length, cells_x, cells_y = coefficients.shape
    owners = slot_orbital.shape[0] // orbitals
    per = length // owners
    magic, trans, kin_taps = magic_pairs(), transposed_pairs(), kinetic_pairs()
    magic_line = band_periodic(length, magic)
    trans_line = band_periodic(length, trans)
    kin_line = band_periodic(length, kin_taps, -0.5)
    dht = hartley(length)
    waves = curve(length).astype(np.float32)

    rims = jnp.concatenate(
        [coefficients[:, :, cells_x - 16 :], coefficients[:, :, :16]], axis=2
    )
    halo = to_other(rims)
    psi, coded = density(
        occupations,
        slot_orbital,
        coefficients,
        halo,
        jnp.asarray(magic_line.T),
        jnp.asarray(band_open(cells_x, 16, magic)),
        jnp.asarray(magic_line),
        jnp.asarray(dht),
        owners,
    )
    got = to_all(coded)
    kin, kin_sums = kinetic(
        coefficients,
        halo,
        jnp.asarray(kin_line.T),
        jnp.asarray(band_open(cells_x, 16, kin_taps, -0.5)),
        jnp.asarray(kin_line),
    )
    half = slab_sum(got, per * cells_x, per).reshape(per, cells_x, cells_y)
    slab = lax.all_gather(half, "grid", axis=1, tiled=True)
    spread = solve(
        jnp.asarray(waves),
        slab,
        jnp.asarray(dht),
        jnp.asarray(np.broadcast_to(waves[:, None], (length, cells_y))),
        jnp.asarray(np.broadcast_to(waves[None, :], (length, cells_y))),
        owners,
    )
    back, full_field, field_sums = field(
        to_all(spread), psi, jnp.asarray(dht), jnp.asarray(trans_line)
    )
    low = to_other(back[:, cells_x - 8 :])
    high = to_other(back[:, :8])
    sums = jnp.stack(
        [
            jnp.sum(kin_sums[:, 0], axis=(1, 2)) + jnp.sum(field_sums, axis=(1, 2)),
            jnp.sum(kin_sums[:, 1], axis=(1, 2)),
        ]
    )
    sums = sums + to_other(sums)
    energies = sums[0] / sums[1]
    updated = update(
        energies,
        back,
        low,
        high,
        coefficients,
        kin,
        jnp.asarray(band_open(cells_x, 8, trans)),
        jnp.asarray(trans_line.T),
    )
    first = lax.axis_index("orb") * per
    potential = lax.dynamic_slice_in_dim(full_field, first, per, 1).transpose(1, 0, 2)
    return (updated, energies, potential)


def solution(mesh):
    return jax.shard_map(
        on_device,
        mesh=mesh,
        in_specs=(P("orb", None, "grid", None), P(), P()),
        out_specs=(P("orb", None, "grid", None), P("orb"), P("orb", "grid", None)),
        check_vma=False,
    )
```

```python
import functools
import math

import jax
import jax.numpy as jnp
import ml_dtypes
import numpy as np
from jax import lax
from jax.experimental import pallas as pl
from jax.experimental.pallas import tpu as pltpu
from jax.sharding import PartitionSpec as P

MAGIC = (
    8.433424733352934e-07,
    -1.290557201342061e-05,
    8.76298447621056e-05,
    -0.00030158038132690465,
    0.001747237136729939,
    -0.009420470302010804,
    0.023738214637249424,
    0.0612625895831208,
    0.9940415697834004,
    -0.06048952891969835,
    -0.021030251609303816,
    0.013372634148547948,
    -0.0034412814449349387,
    0.0004944322768868992,
    -5.185986881173433e-05,
    2.7273449291197967e-06,
)
STEP_SIZE = 0.1
COULOMB = 4.0 * math.pi
LEVELS = 32000.0
FINE = 16384.0
F32 = jnp.float32
BF16 = jnp.bfloat16
HIGHEST = lax.Precision.HIGHEST
MIB = 1024 * 1024


def magic_pairs():
    return [(position - 8, MAGIC[position]) for position in range(16)]


def transposed_pairs():
    return [(8 - position, MAGIC[position]) for position in range(16)]


def kinetic_pairs():
    spread = 14
    weights = []
    for distance in range(1, spread + 1):
        numerator = 2.0 * (-1.0) ** (distance + 1) * math.factorial(spread) ** 2
        weights.append(
            numerator
            / (
                distance
                * distance
                * math.factorial(spread - distance)
                * math.factorial(spread + distance)
            )
        )
    result = [(0, -2.0 * sum(weights))]
    for distance in range(1, spread + 1):
        result.append((distance, weights[distance - 1]))
        result.append((-distance, weights[distance - 1]))
    return result


def rounded(weight):
    return np.float32(np.float32(weight).astype(ml_dtypes.bfloat16))


def band_periodic(length, pairs, scale=1.0):
    matrix = np.zeros((length, length), np.float32)
    for offset, weight in pairs:
        for i in range(length):
            matrix[i, (i + offset) % length] += scale * rounded(weight)
    return matrix.astype(ml_dtypes.bfloat16)


def band_columns(length, columns, pairs, scale=1.0):
    matrix = np.zeros((length, len(columns)), np.float32)
    place = {cell: k for k, cell in enumerate(columns)}
    for offset, weight in pairs:
        for i in range(length):
            matrix[i, place[i + offset]] += scale * rounded(weight)
    return matrix.astype(ml_dtypes.bfloat16)


def with_rims(length, inner, outer):
    return [*range(-outer, -inner), *range(length + inner, length + outer)]


def hartley(length):
    index = np.arange(length)
    angle = 2.0 * np.pi * ((index[:, None] * index[None, :]) % length) / length
    return ((np.cos(angle) + np.sin(angle)) / math.sqrt(length)).astype(np.float32)


def split_table(table):
    high = table.astype(ml_dtypes.bfloat16)
    low = (table - high.astype(np.float32)).astype(ml_dtypes.bfloat16)
    return np.concatenate([high, low], axis=1)


def curve(length):
    return 2.0 - 2.0 * np.cos(2.0 * np.pi * np.arange(length) / length)


def dot(a, b):
    return jnp.dot(a, b, preferred_element_type=F32)


def dot_exact(a, b):
    return jnp.dot(a, b, preferred_element_type=F32, precision=HIGHEST)


def params(count, mebibytes):
    return pltpu.CompilerParams(
        dimension_semantics=("arbitrary",) * count, vmem_limit_bytes=mebibytes * MIB
    )


def whole(array):
    zeros = (0,) * array.ndim
    return pl.BlockSpec(array.shape, lambda *_: zeros)


def scale_of(largest):
    largest = jnp.maximum(largest, 1e-30)
    code = jnp.ceil(jnp.log2(largest))
    power = jnp.exp2(code)
    units = jnp.ceil(largest / power * FINE) + 1.0
    return code, units, units * (1.0 / FINE) * power


def coded_rows(cells_y, codes):
    row = lax.broadcasted_iota(jnp.int32, (16, cells_y), 0)
    values = jnp.zeros((16, cells_y), F32)
    for k, code in enumerate(codes):
        values = jnp.where(row == k, code, values)
    return values.astype(jnp.int32).astype(jnp.int16)


def side_by_side(first, second):
    return jnp.concatenate([first, second], axis=1)


def hartley_pair(table, pair):
    high = pair.astype(BF16)
    low = (pair - high.astype(F32)).astype(BF16)
    return dot(table, jnp.concatenate([high, high], axis=0)) + dot(
        table, jnp.concatenate([low, low], axis=0)
    )


def rims_kernel(inner, outer, low_ref, high_ref, after_ref, out_ref):
    tile = low_ref.shape[2]
    low = low_ref[0].astype(F32)[:, tile - outer : tile - inner]
    high = high_ref[0].astype(F32)[:, inner:outer]
    out_ref[0] = jnp.concatenate([low, high], axis=1).astype(BF16)


def own_rims(c, inner, outer, after):
    orbitals, length, cells_x, cells_y = c.shape
    tile = 16
    chunks = 2
    part = length // chunks

    def at(k):
        return pl.BlockSpec((1, part, tile, cells_y), lambda o, j: (o, j, k, 0))

    return pl.pallas_call(
        functools.partial(rims_kernel, inner, outer),
        grid=(orbitals, chunks),
        in_specs=[at(cells_x // tile - 1), at(0), pl.BlockSpec(memory_space=pl.ANY)],
        out_specs=at(0),
        out_shape=jax.ShapeDtypeStruct((orbitals, length, 2 * (outer - inner), cells_y), BF16),
        compiler_params=params(2, 8),
        name="own_rims",
    )(c, c, after)


def density_kernel(
    first_steps,
    pitch,
    occ_ref,
    slot_ref,
    c_ref,
    h_ref,
    my_ref,
    ax_ref,
    mz_ref,
    dht_ref,
    psi_ref,
    q_ref,
    mid,
    waves,
    peak,
    level,
):
    step = pl.program_id(0)
    cells_z, cells_x, cells_y = c_ref.shape[1], c_ref.shape[2], c_ref.shape[3]
    rim = h_ref.shape[2]
    orbitals, some_x, length = psi_ref.shape[0], psi_ref.shape[1], psi_ref.shape[2]
    block = 8

    @pl.when(step < first_steps)
    def _():
        my = my_ref[...]
        ax = ax_ref[...]

        def planes(i, carry):
            z0 = i * block
            own = dot(c_ref[0, pl.ds(z0, block)].reshape(block * cells_x, cells_y), my)
            own = own.astype(BF16).reshape(block, cells_x, cells_y)
            far = dot(h_ref[0, pl.ds(z0, block)].reshape(block * rim, cells_y), my)
            far = far.astype(BF16).reshape(block, rim, cells_y)
            for p in range(0, block, 2):
                pair = jnp.concatenate(
                    [side_by_side(own[p], own[p + 1]), side_by_side(far[p], far[p + 1])], axis=0
                )
                both = dot(ax, pair)
                row = pl.multiple_of((step * cells_z + z0 + p) * pitch, 8)
                mid[pl.ds(row, cells_x), :] = both[:, :cells_y]
                mid[pl.ds(row + pitch, cells_x), :] = both[:, cells_y:]
            return carry

        lax.fori_loop(0, cells_z // block, planes, 0, unroll=4)

    def grid_values(x):
        first = lax.axis_index("orb") * orbitals
        total = jnp.zeros((length, 2 * cells_y), F32)
        kept = []
        for o in range(orbitals):
            weight = occ_ref[slot_ref[first + o]].astype(F32) / slot_ref.shape[0]
            row = o * length * pitch + x
            pair = side_by_side(
                mid[pl.ds(row, length, stride=pitch), :].astype(BF16),
                mid[pl.ds(row + 1, length, stride=pitch), :].astype(BF16),
            )
            values = dot(mz_ref[...], pair).astype(BF16)
            kept.append(values)
            wide = values.astype(F32)
            total = total + weight * (wide * wide)
        return kept, total

    @pl.when(step == first_steps)
    def _():
        _, total = grid_values(0)
        code, fine, top = scale_of(jnp.sum(total) / total.size)
        level[0] = code
        level[1] = fine
        level[2] = top
        peak[...] = jnp.zeros_like(peak)

    @pl.when(step >= first_steps)
    def _():
        x0 = (step - first_steps) * some_x
        mean = level[2]
        table = dht_ref[...]
        largest = peak[...]
        for local in range(0, some_x, 2):
            kept, total = grid_values(x0 + local)
            for o in range(orbitals):
                psi_ref[o, local] = kept[o][:, :cells_y]
                psi_ref[o, local + 1] = kept[o][:, cells_y:]
            result = hartley_pair(table, total - mean)
            waves[pl.ds(x0 + local, length, stride=pitch), :] = result[:, :cells_y]
            waves[pl.ds(x0 + local + 1, length, stride=pitch), :] = result[:, cells_y:]
            size = jnp.abs(result)
            size = jnp.maximum(size[:, :cells_y], size[:, cells_y:])
            largest = jnp.maximum(largest, jnp.max(size.reshape(length // 8, 8, cells_y), axis=0))
        peak[...] = largest

    @pl.when(step == pl.num_programs(0) - 1)
    def _():
        code, fine, top = scale_of(jnp.max(peak[...]))
        factor = LEVELS / top
        code_rows = coded_rows(cells_y, (code, fine, level[0], level[1], LEVELS))
        per = length // q_ref.shape[0]
        rows = per * cells_x

        def quantise(i, carry):
            for k in range(per):
                row = pl.multiple_of((i * per + k) * pitch, 8)
                values = jnp.round(waves[pl.ds(row, cells_x), :] * factor)
                at = pl.ds(k * cells_x, cells_x)
                q_ref[i, at, :] = values.astype(jnp.int32).astype(jnp.int16)
            q_ref[i, rows : rows + 16, :] = code_rows
            return carry

        lax.fori_loop(0, q_ref.shape[0], quantise, 0, unroll=4)


def density(occupations, slot_orbital, c, halo, my, ax, mz, dht, owners):
    orbitals, length, cells_x, cells_y = c.shape
    chunks = 4
    part = length // chunks
    first_steps = orbitals * chunks
    some_x = 8
    pitch = cells_x + 8
    smem = pl.BlockSpec(memory_space=pltpu.SMEM)
    rows = (length // owners) * cells_x + 16

    def at_first(s):
        s = jnp.minimum(s, first_steps - 1)
        return (s // chunks, s % chunks, 0, 0)

    return pl.pallas_call(
        functools.partial(density_kernel, first_steps, pitch),
        grid=(first_steps + cells_x // some_x,),
        in_specs=[
            smem,
            smem,
            pl.BlockSpec((1, part, cells_x, cells_y), at_first),
            pl.BlockSpec((1, part, halo.shape[2], cells_y), at_first),
            whole(my),
            whole(ax),
            whole(mz),
            whole(dht),
        ],
        out_specs=[
            pl.BlockSpec(
                (orbitals, some_x, length, cells_y),
                lambda s: (0, jnp.maximum(s - first_steps, 0), 0, 0),
            ),
            pl.BlockSpec((owners, rows, cells_y), lambda s: (0, 0, 0)),
        ],
        out_shape=[
            jax.ShapeDtypeStruct((orbitals, cells_x, length, cells_y), BF16),
            jax.ShapeDtypeStruct((owners, rows, cells_y), jnp.int16),
        ],
        scratch_shapes=[
            pltpu.VMEM((orbitals * length * pitch, cells_y), F32),
            pltpu.VMEM((length * pitch, cells_y), F32),
            pltpu.VMEM((8, cells_y), F32),
            pltpu.SMEM((3,), F32),
        ],
        compiler_params=params(1, 34),
        name="density",
    )(occupations, slot_orbital, c, halo, my, ax, mz, dht)


def kinetic_kernel(
    pitch, c_ref, near_ref, far_ref, dy_ref, dx_ref, dz_ref, after_ref, kin_ref, sums_ref, wide, acc
):
    length, cells_x, cells_y = c_ref.shape[1], c_ref.shape[2], c_ref.shape[3]
    block = 8

    def widen(z, carry):
        row = pl.multiple_of(z * pitch, 8)
        wide[pl.ds(row, cells_x), :] = c_ref[0, z].astype(F32)
        return carry

    lax.fori_loop(0, length, widen, 0, unroll=8)

    def columns(i, carry):
        x = 2 * i
        pair = side_by_side(
            wide[pl.ds(x, length, stride=pitch), :].astype(BF16),
            wide[pl.ds(x + 1, length, stride=pitch), :].astype(BF16),
        )
        values = dot(dz_ref[...], pair)
        acc[pl.ds(x, length, stride=pitch), :] = values[:, :cells_y]
        acc[pl.ds(x + 1, length, stride=pitch), :] = values[:, cells_y:]
        return carry

    lax.fori_loop(0, cells_x // 2, columns, 0, unroll=4)

    def planes(i, carry):
        energy, norm = carry
        z0 = i * block
        own = c_ref[0, pl.ds(z0, block)]
        along_y = dot(own.reshape(block * cells_x, cells_y), dy_ref[...])
        for p in range(0, block, 2):
            z = z0 + p
            pair = jnp.concatenate(
                [
                    side_by_side(c_ref[0, z], c_ref[0, z + 1]),
                    side_by_side(near_ref[0, z], near_ref[0, z + 1]),
                    side_by_side(far_ref[0, z], far_ref[0, z + 1]),
                ],
                axis=0,
            )
            along_x = dot(dx_ref[...], pair)
            for k in range(2):
                at = pl.ds(pl.multiple_of((z + k) * pitch, 8), cells_x)
                value = (
                    acc[at, :]
                    + along_x[:, k * cells_y : (k + 1) * cells_y]
                    + along_y[(p + k) * cells_x : (p + k + 1) * cells_x]
                )
                kin_ref[0, z + k] = value
                coeff = own[p + k].astype(F32)
                tiles = (cells_x // 8, 8, cells_y)
                energy = energy + jnp.sum((coeff * value).reshape(tiles), axis=0)
                norm = norm + jnp.sum((coeff * coeff).reshape(tiles), axis=0)
        return energy, norm

    zeros = jnp.zeros((8, cells_y), F32)
    energy, norm = lax.fori_loop(0, length // block, planes, (zeros, zeros), unroll=2)
    sums_ref[0, 0:8] = energy
    sums_ref[0, 8:16] = norm


def kinetic(c, near, far, dy, dx, dz, after):
    orbitals, length, cells_x, cells_y = c.shape
    cells = orbitals * length * cells_x * cells_y
    pitch = cells_x + 8

    def block(array):
        return pl.BlockSpec((1, *array.shape[1:]), lambda o: (o, 0, 0, 0))

    return pl.pallas_call(
        functools.partial(kinetic_kernel, pitch),
        grid=(orbitals,),
        in_specs=[
            block(c),
            block(near),
            block(far),
            whole(dy),
            whole(dx),
            whole(dz),
            pl.BlockSpec(memory_space=pl.ANY),
        ],
        out_specs=[block(c), pl.BlockSpec((1, 16, cells_y), lambda o: (o, 0, 0))],
        out_shape=[
            jax.ShapeDtypeStruct(c.shape, F32),
            jax.ShapeDtypeStruct((orbitals, 16, cells_y), F32),
        ],
        scratch_shapes=[
            pltpu.VMEM((length * pitch, cells_y), F32),
            pltpu.VMEM((length * pitch, cells_y), F32),
        ],
        compiler_params=params(1, 30),
        cost_estimate=pl.CostEstimate(
            flops=cells * 768 * 4, bytes_accessed=cells * 7, transcendentals=0
        ),
        name="kinetic",
    )(c, near, far, dy, dx, dz, after)


def unpacked(ref, source, rows):
    codes = ref[source, rows : rows + 16, :].astype(jnp.int32).astype(F32)
    powers = jnp.exp2(codes) * (1.0 / (LEVELS * FINE))
    step = codes[1:2] * powers[0:1]
    mean = codes[4:5] * (codes[3:4] * powers[2:3])
    return ref[source, 0:rows, :].astype(jnp.int32).astype(F32) * step, mean


def sum_kernel(per, got_ref, after_ref, out_ref):
    rows = out_ref.shape[0]
    cells_y = out_ref.shape[1]

    def body(source, carry):
        total, means = carry
        values, mean = unpacked(got_ref, source, rows)
        return total + values, means + mean

    total, means = lax.fori_loop(
        0,
        got_ref.shape[0],
        body,
        (jnp.zeros((rows, cells_y), F32), jnp.zeros((1, cells_y), F32)),
        unroll=2,
    )
    length = got_ref.shape[0] * per
    row = lax.broadcasted_iota(jnp.int32, (rows, cells_y), 0)
    flat = (lax.axis_index("orb") == 0) & (row < rows // per)
    out_ref[...] = total + jnp.where(flat, means * math.sqrt(length), 0.0)


def slab_sum(got, rows, per, after):
    return pl.pallas_call(
        functools.partial(sum_kernel, per),
        in_specs=[pl.BlockSpec(memory_space=pltpu.VMEM), pl.BlockSpec(memory_space=pl.ANY)],
        out_shape=jax.ShapeDtypeStruct((rows, got.shape[2]), F32),
        compiler_params=params(0, 12),
        name="slab_sum",
    )(got, after)


def solve_kernel(curve_z_ref, slab_ref, dht_ref, curve_ref, q_ref):
    per, length, cells_y = slab_ref.shape
    cells_x = length // 2
    orb = lax.axis_index("orb")
    corner = pl.multiple_of(lax.axis_index("grid") * cells_x, cells_x)
    dht = dht_ref[...]
    own = dht_ref[pl.ds(corner, cells_x), :]
    row = lax.broadcasted_iota(jnp.int32, (length, cells_y), 0)
    col = lax.broadcasted_iota(jnp.int32, (length, cells_y), 1)
    waves = dot_exact(jnp.concatenate([slab_ref[k] for k in range(per)], axis=0), dht)
    waves = jnp.concatenate(
        [waves[k * length : (k + 1) * length] for k in range(per)], axis=1
    )
    waves = dot_exact(dht, waves)
    parts = []
    for k in range(per):
        wave = orb * per + k
        anchor = (row == 0) & (col == 0) & (wave == 0)
        bent = curve_ref[...] + curve_z_ref[wave]
        factor = jnp.where(anchor, 0.0, COULOMB / jnp.where(anchor, 1.0, bent))
        parts.append(waves[:, k * cells_y : (k + 1) * cells_y] * factor)
    field = dot_exact(own, jnp.concatenate(parts, axis=1))
    field = jnp.concatenate(
        [field[:, k * cells_y : (k + 1) * cells_y] for k in range(per)], axis=0
    )
    field = dot_exact(field, dht)
    code, fine, top = scale_of(jnp.max(jnp.abs(field)))
    coded = jnp.round(field * (LEVELS / top)).astype(jnp.int32).astype(jnp.int16)
    code_rows = coded_rows(cells_y, (code, fine))
    rows = per * cells_x

    def spread(i, carry):
        q_ref[i, 0:rows, :] = coded
        q_ref[i, rows : rows + 16, :] = code_rows
        return carry

    lax.fori_loop(0, q_ref.shape[0], spread, 0, unroll=4)


def solve(curve_z, slab, dht, plane_curve, owners):
    per, length, cells_y = slab.shape
    vmem = pl.BlockSpec(memory_space=pltpu.VMEM)
    return pl.pallas_call(
        solve_kernel,
        in_specs=[pl.BlockSpec(memory_space=pltpu.SMEM), vmem, vmem, vmem],
        out_shape=jax.ShapeDtypeStruct((owners, per * (length // 2) + 16, cells_y), jnp.int16),
        compiler_params=params(0, 12),
        name="solve",
    )(curve_z, slab, dht, plane_curve)


def field_kernel(
    pitch,
    turn_pitch,
    got_ref,
    psi_ref,
    kin_ref,
    dht_ref,
    tz_ref,
    back_ref,
    rim_ref,
    slab_ref,
    sums_ref,
    waves,
    turn,
    head,
    values,
):
    step = pl.program_id(0)
    orbitals, some_x, length, cells_y = psi_ref.shape
    owners = got_ref.shape[0]
    per = length // owners
    cells_x = some_x * pl.num_programs(0)
    rim = rim_ref.shape[2] // 2
    first = pl.multiple_of((lax.axis_index("orb") * per) // 8 * 8, 8)

    @pl.when(step == 0)
    def _():
        def unpack(source, carry):
            found, _ = unpacked(got_ref, source, per * cells_x)
            for k in range(per):
                at = pl.ds(pl.multiple_of((source * per + k) * pitch, 8), cells_x)
                waves[at, :] = found[k * cells_x : (k + 1) * cells_x]
            return carry

        lax.fori_loop(0, owners, unpack, 0, unroll=4)
        sums_ref[...] = kin_ref[...]

    def columns(i, carry):
        new = list(carry)
        for pair in range(2):
            local = 4 * i + 2 * pair
            x = step * some_x + local
            field = hartley_pair(
                dht_ref[...],
                side_by_side(
                    waves[pl.ds(x, length, stride=pitch), :],
                    waves[pl.ds(x + 1, length, stride=pitch), :],
                ),
            )
            values[pair] = field
            own = values[pair, pl.ds(first, 8), :]
            slab_ref[local] = own[:, :cells_y]
            slab_ref[local + 1] = own[:, cells_y:]
            for o in range(orbitals):
                psi = side_by_side(psi_ref[o, local], psi_ref[o, local + 1]).astype(F32)
                product = field * psi
                squares = product * psi
                squares = squares[:, :cells_y] + squares[:, cells_y:]
                new[o] = new[o] + jnp.sum(squares.reshape(length // 8, 8, cells_y), axis=0)
                back = dot(tz_ref[...], product.astype(BF16))
                row = o * length * turn_pitch + local
                turn[pl.ds(row, length, stride=turn_pitch), :] = back[:, :cells_y]
                turn[pl.ds(row + 1, length, stride=turn_pitch), :] = back[:, cells_y:]
        return tuple(new)

    zeros = jnp.zeros((8, cells_y), F32)
    energy = lax.fori_loop(0, some_x // 4, columns, (zeros,) * orbitals, unroll=2)
    for o in range(orbitals):
        sums_ref[o, 0:8] = sums_ref[o, 0:8] + energy[o]

    def turned(o, z, start, count):
        row = pl.multiple_of((o * length + z) * turn_pitch, 8) + start
        return turn[pl.ds(row, count), :]

    def rows(z, carry):
        for o in range(orbitals):
            back_ref[o, z] = turned(o, z, 0, some_x).astype(BF16)
        return carry

    lax.fori_loop(0, length, rows, 0, unroll=8)

    @pl.when(step == 0)
    def _():
        def keep(z, carry):
            for o in range(orbitals):
                head[o, z] = turned(o, z, 0, rim)
            return carry

        lax.fori_loop(0, length, keep, 0, unroll=8)

    @pl.when(step == pl.num_programs(0) - 1)
    def _():
        def send(z, carry):
            for o in range(orbitals):
                both = jnp.concatenate([turned(o, z, some_x - rim, rim), head[o, z]], axis=0)
                rim_ref[o, z] = both.astype(BF16)
            return carry

        lax.fori_loop(0, length, send, 0, unroll=8)


def field(got, psi, kin_sums, dht, tz):
    orbitals, cells_x, length, cells_y = psi.shape
    some_x = 16
    pitch = cells_x + 8
    turn_pitch = some_x + 8
    rim = 8
    return pl.pallas_call(
        functools.partial(field_kernel, pitch, turn_pitch),
        grid=(cells_x // some_x,),
        in_specs=[
            whole(got),
            pl.BlockSpec((orbitals, some_x, length, cells_y), lambda i: (0, i, 0, 0)),
            whole(kin_sums),
            whole(dht),
            whole(tz),
        ],
        out_specs=[
            pl.BlockSpec((orbitals, length, some_x, cells_y), lambda i: (0, 0, i, 0)),
            pl.BlockSpec((orbitals, length, 2 * rim, cells_y), lambda i: (0, 0, 0, 0)),
            pl.BlockSpec((some_x, 8, cells_y), lambda i: (i, 0, 0)),
            whole(kin_sums),
        ],
        out_shape=[
            jax.ShapeDtypeStruct((orbitals, length, cells_x, cells_y), BF16),
            jax.ShapeDtypeStruct((orbitals, length, 2 * rim, cells_y), BF16),
            jax.ShapeDtypeStruct((cells_x, 8, cells_y), F32),
            jax.ShapeDtypeStruct(kin_sums.shape, F32),
        ],
        scratch_shapes=[
            pltpu.VMEM((length * pitch, cells_y), F32),
            pltpu.VMEM((orbitals * length * turn_pitch, cells_y), F32),
            pltpu.VMEM((orbitals, length, rim, cells_y), F32),
            pltpu.VMEM((2, length, 2 * cells_y), F32),
        ],
        compiler_params=params(1, 30),
        name="field",
    )(got, psi, kin_sums, dht, tz)


def update_kernel(
    sums_ref, other_ref, back_ref, rim_ref, c_ref, kin_ref, tx_ref, ty_ref, out_ref, energy_ref
):
    orbital = pl.program_id(0)

    @pl.when(pl.program_id(1) == 0)
    def _():
        both = sums_ref[orbital] + other_ref[orbital]
        energy_ref[orbital] = jnp.sum(both[0:8]) / jnp.sum(both[8:16])

    energy = energy_ref[orbital]
    some_z, cells_x, cells_y = back_ref.shape[1], back_ref.shape[2], back_ref.shape[3]
    tx = tx_ref[...]
    ty = ty_ref[...]
    block = 8

    def planes(i, carry):
        z0 = i * block
        crossed = []
        for p in range(0, block, 2):
            z = z0 + p
            pair = jnp.concatenate(
                [
                    side_by_side(back_ref[0, z], back_ref[0, z + 1]),
                    side_by_side(rim_ref[0, z], rim_ref[0, z + 1]),
                ],
                axis=0,
            )
            both = dot(tx, pair).astype(BF16)
            crossed += [both[:, :cells_y], both[:, cells_y:]]
        potential = dot(jnp.concatenate(crossed, axis=0), ty)
        for p in range(block):
            z = z0 + p
            applied = potential[p * cells_x : (p + 1) * cells_x] + kin_ref[0, z]
            coeff = c_ref[0, z].astype(F32)
            out_ref[0, z] = (coeff - STEP_SIZE * (applied - energy * coeff)).astype(BF16)
        return carry

    lax.fori_loop(0, some_z // block, planes, 0, unroll=4)


def update(sums, other_sums, back, rim, c, kin, tx, ty):
    orbitals, length, cells_x, cells_y = c.shape
    chunks = 4
    part = length // chunks
    block = pl.BlockSpec((1, part, cells_x, cells_y), lambda o, j: (o, j, 0, 0))
    return pl.pallas_call(
        update_kernel,
        grid=(orbitals, chunks),
        in_specs=[
            whole(sums),
            whole(other_sums),
            block,
            pl.BlockSpec((1, part, rim.shape[2], cells_y), lambda o, j: (o, j, 0, 0)),
            block,
            block,
            whole(tx),
            whole(ty),
        ],
        out_specs=[block, pl.BlockSpec(memory_space=pltpu.SMEM)],
        out_shape=[
            jax.ShapeDtypeStruct(c.shape, BF16),
            jax.ShapeDtypeStruct((orbitals,), F32),
        ],
        compiler_params=params(2, 12),
        name="update",
    )(sums, other_sums, back, rim, c, kin, tx, ty)


def to_other(array):
    return lax.ppermute(array, "grid", [(0, 1), (1, 0)])


def to_all(blocks):
    return lax.all_to_all(blocks, "orb", split_axis=0, concat_axis=0, tiled=True)


def on_device(coefficients, occupations, slot_orbital):
    orbitals, length, cells_x, cells_y = coefficients.shape
    owners = slot_orbital.shape[0] // orbitals
    per = length // owners
    magic, trans, kin_taps = magic_pairs(), transposed_pairs(), kinetic_pairs()
    magic_line = band_periodic(length, magic)
    trans_line = band_periodic(length, trans)
    kin_line = band_periodic(length, kin_taps, -0.5)
    inside = list(range(cells_x))
    near_cells = inside + with_rims(cells_x, 0, 8)
    all_cells = near_cells + with_rims(cells_x, 8, 16)
    dht = hartley(length)
    table = jnp.asarray(split_table(dht))
    waves = curve(length)

    near = to_other(own_rims(coefficients, 0, 8, occupations))
    psi, coded = density(
        occupations,
        slot_orbital,
        coefficients,
        near,
        jnp.asarray(magic_line.T),
        jnp.asarray(band_columns(cells_x, near_cells, magic)),
        jnp.asarray(magic_line),
        table,
        owners,
    )
    got = to_all(coded)
    far = to_other(own_rims(coefficients, 8, 16, psi))
    kin, kin_sums = kinetic(
        coefficients,
        near,
        far,
        jnp.asarray(kin_line.T),
        jnp.asarray(band_columns(cells_x, all_cells, kin_taps, -0.5)),
        jnp.asarray(kin_line),
        psi,
    )
    half = slab_sum(got, per * cells_x, per, kin_sums).reshape(per, cells_x, cells_y)
    slab = lax.all_gather(half, "grid", axis=1, tiled=True)
    spread = solve(
        jnp.asarray(waves.astype(np.float32)),
        slab,
        jnp.asarray(dht),
        jnp.asarray((waves[:, None] + waves[None, :]).astype(np.float32)),
        owners,
    )
    back, back_rims, slab_field, sums = field(
        to_all(spread), psi, kin_sums, table, jnp.asarray(trans_line)
    )
    updated, energies = update(
        sums,
        to_other(sums),
        back,
        to_other(back_rims),
        coefficients,
        kin,
        jnp.asarray(band_columns(cells_x, near_cells, trans)),
        jnp.asarray(trans_line.T),
    )
    first = lax.rem(lax.axis_index("orb") * per, 8)
    potential = lax.dynamic_slice_in_dim(slab_field, first, per, 1).transpose(1, 0, 2)
    return (updated, energies, potential)


def solution(mesh):
    return jax.shard_map(
        on_device,
        mesh=mesh,
        in_specs=(P("orb", None, "grid", None), P(), P()),
        out_specs=(P("orb", None, "grid", None), P("orb"), P("orb", "grid", None)),
        check_vma=False,
    )
```

```python
import functools
import math

import jax
import jax.numpy as jnp
import ml_dtypes
import numpy as np
from jax import lax
from jax.experimental import pallas as pl
from jax.experimental.pallas import tpu as pltpu
from jax.sharding import PartitionSpec as P

MAGIC = (
    8.433424733352934e-07,
    -1.290557201342061e-05,
    8.76298447621056e-05,
    -0.00030158038132690465,
    0.001747237136729939,
    -0.009420470302010804,
    0.023738214637249424,
    0.0612625895831208,
    0.9940415697834004,
    -0.06048952891969835,
    -0.021030251609303816,
    0.013372634148547948,
    -0.0034412814449349387,
    0.0004944322768868992,
    -5.185986881173433e-05,
    2.7273449291197967e-06,
)
STEP_SIZE = 0.1
COULOMB = 4.0 * math.pi
LEVELS = 32000.0
FINE = 16384.0
F32 = jnp.float32
BF16 = jnp.bfloat16
HIGHEST = lax.Precision.HIGHEST
MIB = 1024 * 1024


def magic_pairs():
    return [(position - 8, MAGIC[position]) for position in range(16)]


def transposed_pairs():
    return [(8 - position, MAGIC[position]) for position in range(16)]


def kinetic_pairs():
    spread = 14
    weights = []
    for distance in range(1, spread + 1):
        numerator = 2.0 * (-1.0) ** (distance + 1) * math.factorial(spread) ** 2
        weights.append(
            numerator
            / (
                distance
                * distance
                * math.factorial(spread - distance)
                * math.factorial(spread + distance)
            )
        )
    result = [(0, -2.0 * sum(weights))]
    for distance in range(1, spread + 1):
        result.append((distance, weights[distance - 1]))
        result.append((-distance, weights[distance - 1]))
    return result


def rounded(weight):
    return np.float32(np.float32(weight).astype(ml_dtypes.bfloat16))


def band_periodic(length, pairs, scale=1.0):
    matrix = np.zeros((length, length), np.float32)
    for offset, weight in pairs:
        for i in range(length):
            matrix[i, (i + offset) % length] += scale * rounded(weight)
    return matrix.astype(ml_dtypes.bfloat16)


def band_columns(length, columns, pairs, scale=1.0):
    matrix = np.zeros((length, len(columns)), np.float32)
    place = {cell: k for k, cell in enumerate(columns)}
    for offset, weight in pairs:
        for i in range(length):
            matrix[i, place[i + offset]] += scale * rounded(weight)
    return matrix.astype(ml_dtypes.bfloat16)


def with_rims(length, inner, outer):
    return [*range(-outer, -inner), *range(length + inner, length + outer)]


def hartley(length):
    index = np.arange(length)
    angle = 2.0 * np.pi * ((index[:, None] * index[None, :]) % length) / length
    return ((np.cos(angle) + np.sin(angle)) / math.sqrt(length)).astype(np.float32)


def split_table(table):
    high = table.astype(ml_dtypes.bfloat16)
    low = (table - high.astype(np.float32)).astype(ml_dtypes.bfloat16)
    return np.concatenate([high, low], axis=1)


def curve(length):
    return 2.0 - 2.0 * np.cos(2.0 * np.pi * np.arange(length) / length)


def dot(a, b):
    return jnp.dot(a, b, preferred_element_type=F32)


def dot_exact(a, b):
    return jnp.dot(a, b, preferred_element_type=F32, precision=HIGHEST)


def params(count, mebibytes):
    return pltpu.CompilerParams(
        dimension_semantics=("arbitrary",) * count, vmem_limit_bytes=mebibytes * MIB
    )


def whole(array):
    zeros = (0,) * array.ndim
    return pl.BlockSpec(array.shape, lambda *_: zeros)


def scale_of(largest):
    largest = jnp.maximum(largest, 1e-30)
    code = jnp.ceil(jnp.log2(largest))
    power = jnp.exp2(code)
    units = jnp.ceil(largest / power * FINE) + 1.0
    return code, units, units * (1.0 / FINE) * power


def coded_rows(cells_y, codes):
    row = lax.broadcasted_iota(jnp.int32, (16, cells_y), 0)
    values = jnp.zeros((16, cells_y), F32)
    for k, code in enumerate(codes):
        values = jnp.where(row == k, code, values)
    return values.astype(jnp.int32).astype(jnp.int16)


def side_by_side(first, second):
    return jnp.concatenate([first, second], axis=1)


def hartley_pair(table, pair):
    high = pair.astype(BF16)
    low = (pair - high.astype(F32)).astype(BF16)
    return dot(table, jnp.concatenate([high, high], axis=0)) + dot(
        table, jnp.concatenate([low, low], axis=0)
    )


def rims_kernel(inner, outer, low_ref, high_ref, after_ref, out_ref):
    tile = low_ref.shape[2]
    low = low_ref[0].astype(F32)[:, tile - outer : tile - inner]
    high = high_ref[0].astype(F32)[:, inner:outer]
    out_ref[0] = jnp.concatenate([low, high], axis=1).astype(BF16)


def own_rims(c, inner, outer, after):
    orbitals, length, cells_x, cells_y = c.shape
    tile = 16
    chunks = 2
    part = length // chunks

    def at(k):
        return pl.BlockSpec((1, part, tile, cells_y), lambda o, j: (o, j, k, 0))

    return pl.pallas_call(
        functools.partial(rims_kernel, inner, outer),
        grid=(orbitals, chunks),
        in_specs=[at(cells_x // tile - 1), at(0), pl.BlockSpec(memory_space=pl.ANY)],
        out_specs=at(0),
        out_shape=jax.ShapeDtypeStruct((orbitals, length, 2 * (outer - inner), cells_y), BF16),
        compiler_params=params(2, 8),
        name="own_rims",
    )(c, c, after)


def density_kernel(
    first_steps,
    pitch,
    occ_ref,
    slot_ref,
    c_ref,
    h_ref,
    my_ref,
    ax_ref,
    mz_ref,
    dht_ref,
    psi_ref,
    q_ref,
    peak,
    mid,
    waves,
    level,
):
    step = pl.program_id(0)
    cells_z, cells_x, cells_y = c_ref.shape[1], c_ref.shape[2], c_ref.shape[3]
    rim = h_ref.shape[2]
    orbitals, some_x, length = psi_ref.shape[0], psi_ref.shape[1], psi_ref.shape[2]
    block = 64
    many = 8
    group = 8

    @pl.when(step < first_steps)
    def _():
        my = my_ref[...]
        ax = ax_ref[...]

        def planes(i, carry):
            z0 = i * block
            own = dot(c_ref[0, pl.ds(z0, block)].reshape(block * cells_x, cells_y), my)
            own = own.astype(BF16).reshape(block, cells_x, cells_y)
            far = dot(h_ref[0, pl.ds(z0, block)].reshape(block * rim, cells_y), my)
            far = far.astype(BF16).reshape(block, rim, cells_y)
            for p in range(0, block, many):
                some = range(p, p + many)
                flat = jnp.concatenate(
                    [
                        jnp.concatenate([own[z] for z in some], axis=1),
                        jnp.concatenate([far[z] for z in some], axis=1),
                    ],
                    axis=0,
                )
                crossed = dot(ax, flat)
                for k in range(many):
                    row = pl.multiple_of((step * cells_z + z0 + p + k) * pitch, 8)
                    mid[pl.ds(row, cells_x), :] = crossed[:, k * cells_y : (k + 1) * cells_y]
            return carry

        lax.fori_loop(0, cells_z // block, planes, 0)

    def grid_values(x, count):
        first = lax.axis_index("orb") * orbitals
        columns = [
            mid[pl.ds(o * length * pitch + x + k, length, stride=pitch), :].astype(BF16)
            for o in range(orbitals)
            for k in range(count)
        ]
        values = dot(mz_ref[...], jnp.concatenate(columns, axis=1)).astype(BF16)
        total = None
        for o in range(orbitals):
            weight = occ_ref[slot_ref[first + o]].astype(F32) / slot_ref.shape[0]
            wide = values[:, o * count * cells_y : (o + 1) * count * cells_y].astype(F32)
            part = weight * (wide * wide)
            total = part if total is None else total + part
        return values, total

    @pl.when(step == first_steps)
    def _():
        _, total = grid_values(0, 2)
        code, fine, top = scale_of(jnp.sum(total) / total.size)
        level[0] = code
        level[1] = fine
        level[2] = top
        peak[...] = jnp.zeros_like(peak)

    @pl.when(step >= first_steps)
    def _():
        x0 = (step - first_steps) * some_x
        mean = level[2]
        table = dht_ref[...]
        largest = peak[...]
        for local in range(0, some_x, group):
            values, total = grid_values(x0 + local, group)
            for o in range(orbitals):
                for k in range(group):
                    at = (o * group + k) * cells_y
                    psi_ref[o, local + k] = values[:, at : at + cells_y]
            result = hartley_pair(table, total - mean)
            for k in range(group):
                part = result[:, k * cells_y : (k + 1) * cells_y]
                waves[pl.ds(x0 + local + k, length, stride=pitch), :] = part
                size = jnp.abs(part).reshape(length // 8, 8, cells_y)
                largest = jnp.maximum(largest, jnp.max(size, axis=0))
        peak[...] = largest

    @pl.when(step == pl.num_programs(0) - 1)
    def _():
        code, fine, top = scale_of(jnp.max(peak[...]))
        factor = LEVELS / top
        code_rows = coded_rows(cells_y, (code, fine, level[0], level[1], LEVELS))
        per = length // q_ref.shape[0]
        rows = per * cells_x

        def quantise(i, carry):
            for k in range(per):
                row = pl.multiple_of((i * per + k) * pitch, 8)
                values = jnp.round(waves[pl.ds(row, cells_x), :] * factor)
                at = pl.ds(k * cells_x, cells_x)
                q_ref[i, at, :] = values.astype(jnp.int32).astype(jnp.int16)
            q_ref[i, rows : rows + 16, :] = code_rows
            return carry

        lax.fori_loop(0, q_ref.shape[0], quantise, 0, unroll=4)


def density(occupations, slot_orbital, c, halo, my, ax, mz, dht, owners):
    orbitals, length, cells_x, cells_y = c.shape
    chunks = 2
    part = length // chunks
    first_steps = orbitals * chunks
    some_x = 8
    pitch = cells_x + 8
    smem = pl.BlockSpec(memory_space=pltpu.SMEM)
    rows = (length // owners) * cells_x + 16

    def at_first(s):
        s = jnp.minimum(s, first_steps - 1)
        return (s // chunks, s % chunks, 0, 0)

    return pl.pallas_call(
        functools.partial(density_kernel, first_steps, pitch),
        grid=(first_steps + cells_x // some_x,),
        in_specs=[
            smem,
            smem,
            pl.BlockSpec((1, part, cells_x, cells_y), at_first),
            pl.BlockSpec((1, part, halo.shape[2], cells_y), at_first),
            whole(my),
            whole(ax),
            whole(mz),
            whole(dht),
        ],
        out_specs=[
            pl.BlockSpec(
                (orbitals, some_x, length, cells_y),
                lambda s: (0, jnp.maximum(s - first_steps, 0), 0, 0),
            ),
            pl.BlockSpec((owners, rows, cells_y), lambda s: (0, 0, 0)),
            pl.BlockSpec((8, cells_y), lambda s: (0, 0)),
        ],
        out_shape=[
            pltpu.HBM((orbitals, cells_x, length, cells_y), BF16),
            pltpu.HBM((owners, rows, cells_y), jnp.int16),
            jax.ShapeDtypeStruct((8, cells_y), F32),
        ],
        scratch_shapes=[
            pltpu.VMEM((orbitals * length * pitch, cells_y), F32),
            pltpu.VMEM((length * pitch, cells_y), F32),
            pltpu.SMEM((3,), F32),
        ],
        compiler_params=params(1, 30),
        name="density",
    )(occupations, slot_orbital, c, halo, my, ax, mz, dht)


def kinetic_kernel(
    pitch, c_ref, near_ref, far_ref, dy_ref, dx_ref, dz_ref, after_ref, kin_ref, sums_ref, wide, acc
):
    length, cells_x, cells_y = c_ref.shape[1], c_ref.shape[2], c_ref.shape[3]
    block = 8

    def widen(z, carry):
        row = pl.multiple_of(z * pitch, 8)
        wide[pl.ds(row, cells_x), :] = c_ref[0, z].astype(F32)
        return carry

    lax.fori_loop(0, length, widen, 0, unroll=8)

    def columns(i, carry):
        x = 2 * i
        pair = side_by_side(
            wide[pl.ds(x, length, stride=pitch), :].astype(BF16),
            wide[pl.ds(x + 1, length, stride=pitch), :].astype(BF16),
        )
        values = dot(dz_ref[...], pair)
        acc[pl.ds(x, length, stride=pitch), :] = values[:, :cells_y]
        acc[pl.ds(x + 1, length, stride=pitch), :] = values[:, cells_y:]
        return carry

    lax.fori_loop(0, cells_x // 2, columns, 0, unroll=4)

    def planes(i, carry):
        energy, norm = carry
        z0 = i * block
        own = c_ref[0, pl.ds(z0, block)]
        along_y = dot(own.reshape(block * cells_x, cells_y), dy_ref[...])
        for p in range(0, block, 2):
            z = z0 + p
            pair = jnp.concatenate(
                [
                    side_by_side(c_ref[0, z], c_ref[0, z + 1]),
                    side_by_side(near_ref[0, z], near_ref[0, z + 1]),
                    side_by_side(far_ref[0, z], far_ref[0, z + 1]),
                ],
                axis=0,
            )
            along_x = dot(dx_ref[...], pair)
            for k in range(2):
                at = pl.ds(pl.multiple_of((z + k) * pitch, 8), cells_x)
                value = (
                    acc[at, :]
                    + along_x[:, k * cells_y : (k + 1) * cells_y]
                    + along_y[(p + k) * cells_x : (p + k + 1) * cells_x]
                )
                kin_ref[0, z + k] = value
                coeff = own[p + k].astype(F32)
                tiles = (cells_x // 8, 8, cells_y)
                energy = energy + jnp.sum((coeff * value).reshape(tiles), axis=0)
                norm = norm + jnp.sum((coeff * coeff).reshape(tiles), axis=0)
        return energy, norm

    zeros = jnp.zeros((8, cells_y), F32)
    energy, norm = lax.fori_loop(0, length // block, planes, (zeros, zeros), unroll=2)
    sums_ref[0, 0:8] = energy
    sums_ref[0, 8:16] = norm


def kinetic(c, near, far, dy, dx, dz, after):
    orbitals, length, cells_x, cells_y = c.shape
    cells = orbitals * length * cells_x * cells_y
    pitch = cells_x + 8

    def block(array):
        return pl.BlockSpec((1, *array.shape[1:]), lambda o: (o, 0, 0, 0))

    return pl.pallas_call(
        functools.partial(kinetic_kernel, pitch),
        grid=(orbitals,),
        in_specs=[
            block(c),
            block(near),
            block(far),
            whole(dy),
            whole(dx),
            whole(dz),
            pl.BlockSpec(memory_space=pl.ANY),
        ],
        out_specs=[block(c), pl.BlockSpec((1, 16, cells_y), lambda o: (o, 0, 0))],
        out_shape=[
            pltpu.HBM(c.shape, F32),
            jax.ShapeDtypeStruct((orbitals, 16, cells_y), F32),
        ],
        scratch_shapes=[
            pltpu.VMEM((length * pitch, cells_y), F32),
            pltpu.VMEM((length * pitch, cells_y), F32),
        ],
        compiler_params=params(1, 26),
        cost_estimate=pl.CostEstimate(
            flops=cells * 768 * 4, bytes_accessed=cells * 7, transcendentals=0
        ),
        name="kinetic",
    )(c, near, far, dy, dx, dz, after)


def unpacked(ref, source, rows):
    codes = ref[source, rows : rows + 16, :].astype(jnp.int32).astype(F32)
    powers = jnp.exp2(codes) * (1.0 / (LEVELS * FINE))
    step = codes[1:2] * powers[0:1]
    mean = codes[4:5] * (codes[3:4] * powers[2:3])
    return ref[source, 0:rows, :].astype(jnp.int32).astype(F32) * step, mean


def sum_kernel(per, got_ref, after_ref, out_ref):
    rows = out_ref.shape[0]
    cells_y = out_ref.shape[1]

    def body(source, carry):
        total, means = carry
        values, mean = unpacked(got_ref, source, rows)
        return total + values, means + mean

    total, means = lax.fori_loop(
        0,
        got_ref.shape[0],
        body,
        (jnp.zeros((rows, cells_y), F32), jnp.zeros((1, cells_y), F32)),
        unroll=2,
    )
    length = got_ref.shape[0] * per
    row = lax.broadcasted_iota(jnp.int32, (rows, cells_y), 0)
    flat = (lax.axis_index("orb") == 0) & (row < rows // per)
    out_ref[...] = total + jnp.where(flat, means * math.sqrt(length), 0.0)


def slab_sum(got, rows, per, after):
    return pl.pallas_call(
        functools.partial(sum_kernel, per),
        in_specs=[pl.BlockSpec(memory_space=pltpu.VMEM), pl.BlockSpec(memory_space=pl.ANY)],
        out_shape=jax.ShapeDtypeStruct((rows, got.shape[2]), F32),
        compiler_params=params(0, 12),
        name="slab_sum",
    )(got, after)


def solve_kernel(curve_z_ref, slab_ref, dht_ref, curve_ref, q_ref):
    per, length, cells_y = slab_ref.shape
    cells_x = length // 2
    orb = lax.axis_index("orb")
    corner = pl.multiple_of(lax.axis_index("grid") * cells_x, cells_x)
    dht = dht_ref[...]
    own = dht_ref[pl.ds(corner, cells_x), :]
    row = lax.broadcasted_iota(jnp.int32, (length, cells_y), 0)
    col = lax.broadcasted_iota(jnp.int32, (length, cells_y), 1)
    waves = dot_exact(jnp.concatenate([slab_ref[k] for k in range(per)], axis=0), dht)
    waves = jnp.concatenate(
        [waves[k * length : (k + 1) * length] for k in range(per)], axis=1
    )
    waves = dot_exact(dht, waves)
    parts = []
    for k in range(per):
        wave = orb * per + k
        anchor = (row == 0) & (col == 0) & (wave == 0)
        bent = curve_ref[...] + curve_z_ref[wave]
        factor = jnp.where(anchor, 0.0, COULOMB / jnp.where(anchor, 1.0, bent))
        parts.append(waves[:, k * cells_y : (k + 1) * cells_y] * factor)
    field = dot_exact(own, jnp.concatenate(parts, axis=1))
    field = jnp.concatenate(
        [field[:, k * cells_y : (k + 1) * cells_y] for k in range(per)], axis=0
    )
    field = dot_exact(field, dht)
    code, fine, top = scale_of(jnp.max(jnp.abs(field)))
    coded = jnp.round(field * (LEVELS / top)).astype(jnp.int32).astype(jnp.int16)
    code_rows = coded_rows(cells_y, (code, fine))
    rows = per * cells_x

    def spread(i, carry):
        q_ref[i, 0:rows, :] = coded
        q_ref[i, rows : rows + 16, :] = code_rows
        return carry

    lax.fori_loop(0, q_ref.shape[0], spread, 0, unroll=4)


def solve(curve_z, slab, dht, plane_curve, owners):
    per, length, cells_y = slab.shape
    vmem = pl.BlockSpec(memory_space=pltpu.VMEM)
    return pl.pallas_call(
        solve_kernel,
        in_specs=[pl.BlockSpec(memory_space=pltpu.SMEM), vmem, vmem, vmem],
        out_shape=jax.ShapeDtypeStruct((owners, per * (length // 2) + 16, cells_y), jnp.int16),
        compiler_params=params(0, 12),
        name="solve",
    )(curve_z, slab, dht, plane_curve)


def field_kernel(
    pitch,
    turn_pitch,
    got_ref,
    psi_ref,
    kin_ref,
    dht_ref,
    tz_ref,
    back_ref,
    rim_ref,
    slab_ref,
    sums_ref,
    waves,
    turn,
    head,
    values,
):
    step = pl.program_id(0)
    orbitals, some_x, length, cells_y = psi_ref.shape
    owners = got_ref.shape[0]
    per = length // owners
    cells_x = some_x * pl.num_programs(0)
    rim = rim_ref.shape[2] // 2
    first = pl.multiple_of((lax.axis_index("orb") * per) // 8 * 8, 8)

    @pl.when(step == 0)
    def _():
        def unpack(source, carry):
            found, _ = unpacked(got_ref, source, per * cells_x)
            for k in range(per):
                at = pl.ds(pl.multiple_of((source * per + k) * pitch, 8), cells_x)
                waves[at, :] = found[k * cells_x : (k + 1) * cells_x]
            return carry

        lax.fori_loop(0, owners, unpack, 0, unroll=4)
        sums_ref[...] = kin_ref[...]

    group = 8
    energy = [jnp.zeros((8, cells_y), F32) for _ in range(orbitals)]
    for local in range(0, some_x, group):
        x = step * some_x + local
        field = hartley_pair(
            dht_ref[...],
            jnp.concatenate(
                [waves[pl.ds(x + k, length, stride=pitch), :] for k in range(group)], axis=1
            ),
        )
        values[local // group] = field
        own = values[local // group, pl.ds(first, 8), :]
        for k in range(group):
            slab_ref[local + k] = own[:, k * cells_y : (k + 1) * cells_y]
        products = []
        for o in range(orbitals):
            psi = jnp.concatenate([psi_ref[o, local + k] for k in range(group)], axis=1)
            psi = psi.astype(F32)
            product = field * psi
            products.append(product.astype(BF16))
            squares = product * psi
            for k in range(group):
                part = squares[:, k * cells_y : (k + 1) * cells_y]
                part = part.reshape(length // 8, 8, cells_y)
                energy[o] = energy[o] + jnp.sum(part, axis=0)
        back = dot(tz_ref[...], jnp.concatenate(products, axis=1))
        for o in range(orbitals):
            for k in range(group):
                at = (o * group + k) * cells_y
                row = o * length * turn_pitch + local + k
                turn[pl.ds(row, length, stride=turn_pitch), :] = back[:, at : at + cells_y]

    for o in range(orbitals):
        sums_ref[o, 0:8] = sums_ref[o, 0:8] + energy[o]

    def turned(o, z, start, count):
        row = pl.multiple_of((o * length + z) * turn_pitch, 8) + start
        return turn[pl.ds(row, count), :]

    def rows(z, carry):
        for o in range(orbitals):
            back_ref[o, z] = turned(o, z, 0, some_x).astype(BF16)
        return carry

    lax.fori_loop(0, length, rows, 0, unroll=8)

    @pl.when(step == 0)
    def _():
        def keep(z, carry):
            for o in range(orbitals):
                head[o, z] = turned(o, z, 0, rim)
            return carry

        lax.fori_loop(0, length, keep, 0, unroll=8)

    @pl.when(step == pl.num_programs(0) - 1)
    def _():
        def send(z, carry):
            for o in range(orbitals):
                both = jnp.concatenate([turned(o, z, some_x - rim, rim), head[o, z]], axis=0)
                rim_ref[o, z] = both.astype(BF16)
            return carry

        lax.fori_loop(0, length, send, 0, unroll=8)


def field(got, psi, kin_sums, dht, tz):
    orbitals, cells_x, length, cells_y = psi.shape
    some_x = 16
    pitch = cells_x + 8
    turn_pitch = some_x + 8
    rim = 8
    return pl.pallas_call(
        functools.partial(field_kernel, pitch, turn_pitch),
        grid=(cells_x // some_x,),
        in_specs=[
            pl.BlockSpec(memory_space=pltpu.VMEM),
            pl.BlockSpec((orbitals, some_x, length, cells_y), lambda i: (0, i, 0, 0)),
            whole(kin_sums),
            whole(dht),
            whole(tz),
        ],
        out_specs=[
            pl.BlockSpec((orbitals, length, some_x, cells_y), lambda i: (0, 0, i, 0)),
            pl.BlockSpec((orbitals, length, 2 * rim, cells_y), lambda i: (0, 0, 0, 0)),
            pl.BlockSpec((some_x, 8, cells_y), lambda i: (i, 0, 0)),
            whole(kin_sums),
        ],
        out_shape=[
            pltpu.HBM((orbitals, length, cells_x, cells_y), BF16),
            jax.ShapeDtypeStruct((orbitals, length, 2 * rim, cells_y), BF16),
            jax.ShapeDtypeStruct((cells_x, 8, cells_y), F32),
            jax.ShapeDtypeStruct(kin_sums.shape, F32),
        ],
        scratch_shapes=[
            pltpu.VMEM((length * pitch, cells_y), F32),
            pltpu.VMEM((orbitals * length * turn_pitch, cells_y), F32),
            pltpu.VMEM((orbitals, length, rim, cells_y), F32),
            pltpu.VMEM((2, length, 8 * cells_y), F32),
        ],
        compiler_params=params(1, 26),
        name="field",
    )(got, psi, kin_sums, dht, tz)


def update_kernel(
    sums_ref, other_ref, back_ref, rim_ref, c_ref, kin_ref, tx_ref, ty_ref, out_ref, energy_ref
):
    orbital = pl.program_id(0)

    @pl.when(pl.program_id(1) == 0)
    def _():
        both = sums_ref[orbital] + other_ref[orbital]
        energy_ref[orbital] = jnp.sum(both[0:8]) / jnp.sum(both[8:16])

    energy = energy_ref[orbital]
    some_z, cells_x, cells_y = back_ref.shape[1], back_ref.shape[2], back_ref.shape[3]
    tx = tx_ref[...]
    ty = ty_ref[...]
    block = 16
    many = 8

    def planes(i, carry):
        z0 = i * block
        crossed = []
        for p in range(0, block, many):
            some = range(p, p + many)
            flat = jnp.concatenate(
                [
                    jnp.concatenate([back_ref[0, z0 + k] for k in some], axis=1),
                    jnp.concatenate([rim_ref[0, z0 + k] for k in some], axis=1),
                ],
                axis=0,
            )
            both = dot(tx, flat).astype(BF16)
            crossed += [both[:, k * cells_y : (k + 1) * cells_y] for k in range(many)]
        potential = dot(jnp.concatenate(crossed, axis=0), ty)
        for p in range(block):
            z = z0 + p
            applied = potential[p * cells_x : (p + 1) * cells_x] + kin_ref[0, z]
            coeff = c_ref[0, z].astype(F32)
            out_ref[0, z] = (coeff - STEP_SIZE * (applied - energy * coeff)).astype(BF16)
        return carry

    lax.fori_loop(0, some_z // block, planes, 0, unroll=4)


def update(sums, other_sums, back, rim, c, kin, tx, ty):
    orbitals, length, cells_x, cells_y = c.shape
    chunks = 2
    part = length // chunks
    block = pl.BlockSpec((1, part, cells_x, cells_y), lambda o, j: (o, j, 0, 0))
    return pl.pallas_call(
        update_kernel,
        grid=(orbitals, chunks),
        in_specs=[
            whole(sums),
            whole(other_sums),
            block,
            pl.BlockSpec((1, part, rim.shape[2], cells_y), lambda o, j: (o, j, 0, 0)),
            block,
            block,
            whole(tx),
            whole(ty),
        ],
        out_specs=[block, pl.BlockSpec(memory_space=pltpu.SMEM)],
        out_shape=[
            jax.ShapeDtypeStruct(c.shape, BF16),
            jax.ShapeDtypeStruct((orbitals,), F32),
        ],
        compiler_params=params(2, 12),
        name="update",
    )(sums, other_sums, back, rim, c, kin, tx, ty)


def to_other(array):
    return lax.ppermute(array, "grid", [(0, 1), (1, 0)])


def in_hbm(array):
    return pltpu.with_memory_space_constraint(array, pltpu.HBM)


def to_all(blocks):
    return lax.all_to_all(blocks, "orb", split_axis=0, concat_axis=0, tiled=True)


def on_device(coefficients, occupations, slot_orbital):
    orbitals, length, cells_x, cells_y = coefficients.shape
    owners = slot_orbital.shape[0] // orbitals
    per = length // owners
    magic, trans, kin_taps = magic_pairs(), transposed_pairs(), kinetic_pairs()
    magic_line = band_periodic(length, magic)
    trans_line = band_periodic(length, trans)
    kin_line = band_periodic(length, kin_taps, -0.5)
    inside = list(range(cells_x))
    near_cells = inside + with_rims(cells_x, 0, 8)
    all_cells = near_cells + with_rims(cells_x, 8, 16)
    dht = hartley(length)
    table = jnp.asarray(split_table(dht))
    waves = curve(length)

    own_near = own_rims(coefficients, 0, 8, occupations)
    near = to_other(own_near)
    far = to_other(own_rims(coefficients, 8, 16, own_near))
    psi, coded, peak = density(
        occupations,
        slot_orbital,
        coefficients,
        near,
        jnp.asarray(magic_line.T),
        jnp.asarray(band_columns(cells_x, near_cells, magic)),
        jnp.asarray(magic_line),
        table,
        owners,
    )
    got = to_all(coded)
    kin, kin_sums = kinetic(
        in_hbm(coefficients),
        near,
        far,
        jnp.asarray(kin_line.T),
        jnp.asarray(band_columns(cells_x, all_cells, kin_taps, -0.5)),
        jnp.asarray(kin_line),
        peak,
    )
    half = slab_sum(got, per * cells_x, per, kin_sums).reshape(per, cells_x, cells_y)
    slab = lax.all_gather(half, "grid", axis=1, tiled=True)
    spread = solve(
        jnp.asarray(waves.astype(np.float32)),
        slab,
        jnp.asarray(dht),
        jnp.asarray((waves[:, None] + waves[None, :]).astype(np.float32)),
        owners,
    )
    back, back_rims, slab_field, sums = field(
        to_all(spread), psi, kin_sums, table, jnp.asarray(trans_line)
    )
    updated, energies = update(
        sums,
        to_other(sums),
        in_hbm(back),
        to_other(back_rims),
        in_hbm(coefficients),
        in_hbm(kin),
        jnp.asarray(band_columns(cells_x, near_cells, trans)),
        jnp.asarray(trans_line.T),
    )
    first = lax.rem(lax.axis_index("orb") * per, 8)
    potential = lax.dynamic_slice_in_dim(slab_field, first, per, 1).transpose(1, 0, 2)
    return (updated, energies, potential)


def solution(mesh):
    return jax.shard_map(
        on_device,
        mesh=mesh,
        in_specs=(P("orb", None, "grid", None), P(), P()),
        out_specs=(P("orb", None, "grid", None), P("orb"), P("orb", "grid", None)),
        check_vma=False,
    )
```

```python
import functools
import math

import jax
import jax.numpy as jnp
import ml_dtypes
import numpy as np
from jax import lax
from jax.experimental import pallas as pl
from jax.experimental.pallas import tpu as pltpu
from jax.sharding import PartitionSpec as P

MAGIC = (
    8.433424733352934e-07,
    -1.290557201342061e-05,
    8.76298447621056e-05,
    -0.00030158038132690465,
    0.001747237136729939,
    -0.009420470302010804,
    0.023738214637249424,
    0.0612625895831208,
    0.9940415697834004,
    -0.06048952891969835,
    -0.021030251609303816,
    0.013372634148547948,
    -0.0034412814449349387,
    0.0004944322768868992,
    -5.185986881173433e-05,
    2.7273449291197967e-06,
)
STEP_SIZE = 0.1
COULOMB = 4.0 * math.pi
LEVELS = 32000.0
FINE = 16384.0
F32 = jnp.float32
BF16 = jnp.bfloat16
HIGHEST = lax.Precision.HIGHEST
MIB = 1024 * 1024


def magic_pairs():
    return [(position - 8, MAGIC[position]) for position in range(16)]


def transposed_pairs():
    return [(8 - position, MAGIC[position]) for position in range(16)]


def kinetic_pairs():
    spread = 14
    weights = []
    for distance in range(1, spread + 1):
        numerator = 2.0 * (-1.0) ** (distance + 1) * math.factorial(spread) ** 2
        weights.append(
            numerator
            / (
                distance
                * distance
                * math.factorial(spread - distance)
                * math.factorial(spread + distance)
            )
        )
    result = [(0, -2.0 * sum(weights))]
    for distance in range(1, spread + 1):
        result.append((distance, weights[distance - 1]))
        result.append((-distance, weights[distance - 1]))
    return result


def rounded(weight):
    return np.float32(np.float32(weight).astype(ml_dtypes.bfloat16))


def band_periodic(length, pairs, scale=1.0):
    matrix = np.zeros((length, length), np.float32)
    for offset, weight in pairs:
        for i in range(length):
            matrix[i, (i + offset) % length] += scale * rounded(weight)
    return matrix.astype(ml_dtypes.bfloat16)


def band_columns(length, columns, pairs, scale=1.0):
    matrix = np.zeros((length, len(columns)), np.float32)
    place = {cell: k for k, cell in enumerate(columns)}
    for offset, weight in pairs:
        for i in range(length):
            matrix[i, place[i + offset]] += scale * rounded(weight)
    return matrix.astype(ml_dtypes.bfloat16)


def with_rims(length, inner, outer):
    return [*range(-outer, -inner), *range(length + inner, length + outer)]


def hartley(length):
    index = np.arange(length)
    angle = 2.0 * np.pi * ((index[:, None] * index[None, :]) % length) / length
    return ((np.cos(angle) + np.sin(angle)) / math.sqrt(length)).astype(np.float32)


def split_table(table):
    high = table.astype(ml_dtypes.bfloat16)
    low = (table - high.astype(np.float32)).astype(ml_dtypes.bfloat16)
    return np.concatenate([high, low, high], axis=1)


def curve(length):
    return 2.0 - 2.0 * np.cos(2.0 * np.pi * np.arange(length) / length)


def dot(a, b):
    return jnp.dot(a, b, preferred_element_type=F32)


def dot_exact(a, b):
    return jnp.dot(a, b, preferred_element_type=F32, precision=HIGHEST)


def params(count, mebibytes):
    return pltpu.CompilerParams(
        dimension_semantics=("arbitrary",) * count, vmem_limit_bytes=mebibytes * MIB
    )


def cost(cells, bytes_each):
    return pl.CostEstimate(
        flops=cells * 256, bytes_accessed=cells * bytes_each, transcendentals=0
    )


def whole(array):
    zeros = (0,) * array.ndim
    return pl.BlockSpec(array.shape, lambda *_: zeros)


def scale_of(largest):
    largest = jnp.maximum(largest, 1e-30)
    code = jnp.ceil(jnp.log2(largest))
    power = jnp.exp2(code)
    units = jnp.ceil(largest / power * FINE) + 1.0
    return code, units, units * (1.0 / FINE) * power


def coded_rows(cells_y, codes):
    row = lax.broadcasted_iota(jnp.int32, (16, cells_y), 0)
    values = jnp.zeros((16, cells_y), F32)
    for k, code in enumerate(codes):
        values = jnp.where(row == k, code, values)
    return values.astype(jnp.int32).astype(jnp.int16)


def side_by_side(first, second):
    return jnp.concatenate([first, second], axis=1)


def hartley_pair(table, pair):
    high = pair.astype(BF16)
    low = (pair - high.astype(F32)).astype(BF16)
    return dot(table, jnp.concatenate([high, high, low], axis=0))


def rims_kernel(inner, outer, low_ref, high_ref, *rest):
    out_ref, mark_ref = rest[-2:]
    tile = low_ref.shape[2]
    low = low_ref[...].astype(F32)[:, :, tile - outer : tile - inner]
    high = high_ref[...].astype(F32)[:, :, inner:outer]
    out_ref[...] = jnp.concatenate([low, high], axis=2).astype(BF16)
    mark_ref[...] = jnp.zeros_like(mark_ref)


def own_rims(c, inner, outer, *after):
    orbitals, length, cells_x, cells_y = c.shape
    tile = 16

    def at(k):
        return pl.BlockSpec((orbitals, length, tile, cells_y), lambda o: (0, 0, k, 0))

    return pl.pallas_call(
        functools.partial(rims_kernel, inner, outer),
        grid=(1,),
        in_specs=[at(cells_x // tile - 1), at(0)]
        + [pl.BlockSpec(memory_space=pl.ANY) for _ in after],
        out_specs=[at(0), pl.BlockSpec((8, cells_y), lambda o: (0, 0))],
        out_shape=[
            jax.ShapeDtypeStruct((orbitals, length, 2 * (outer - inner), cells_y), BF16),
            jax.ShapeDtypeStruct((8, cells_y), F32),
        ],
        compiler_params=params(1, 16),
        name="own_rims",
    )(c, c, *after)


def density_kernel(
    first_steps,
    pitch,
    occ_ref,
    slot_ref,
    c_ref,
    h_ref,
    my_ref,
    ax_ref,
    mz_ref,
    dht_ref,
    psi_ref,
    q_ref,
    peak,
    mid,
    waves,
    level,
):
    step = pl.program_id(0)
    cells_z, cells_x, cells_y = c_ref.shape[1], c_ref.shape[2], c_ref.shape[3]
    rim = h_ref.shape[2]
    orbitals, some_x, length = psi_ref.shape[0], psi_ref.shape[1], psi_ref.shape[2]
    block = 64
    many = 8
    group = 8

    @pl.when(step < first_steps)
    def _():
        my = my_ref[...]
        ax = ax_ref[...]

        def planes(i, carry):
            z0 = i * block
            own = dot(c_ref[0, pl.ds(z0, block)].reshape(block * cells_x, cells_y), my)
            own = own.astype(BF16).reshape(block, cells_x, cells_y)
            far = dot(h_ref[0, pl.ds(z0, block)].reshape(block * rim, cells_y), my)
            far = far.astype(BF16).reshape(block, rim, cells_y)
            for p in range(0, block, many):
                some = range(p, p + many)
                flat = jnp.concatenate(
                    [
                        jnp.concatenate([own[z] for z in some], axis=1),
                        jnp.concatenate([far[z] for z in some], axis=1),
                    ],
                    axis=0,
                )
                crossed = dot(ax, flat)
                for k in range(many):
                    row = pl.multiple_of((step * cells_z + z0 + p + k) * pitch, 8)
                    mid[pl.ds(row, cells_x), :] = crossed[:, k * cells_y : (k + 1) * cells_y]
            return carry

        lax.fori_loop(0, cells_z // block, planes, 0)

    def grid_values(x, count):
        first = lax.axis_index("orb") * orbitals
        columns = [
            mid[pl.ds(o * length * pitch + x + k, length, stride=pitch), :].astype(BF16)
            for o in range(orbitals)
            for k in range(count)
        ]
        values = dot(mz_ref[...], jnp.concatenate(columns, axis=1)).astype(BF16)
        total = None
        for o in range(orbitals):
            weight = occ_ref[slot_ref[first + o]].astype(F32) / slot_ref.shape[0]
            wide = values[:, o * count * cells_y : (o + 1) * count * cells_y].astype(F32)
            part = weight * (wide * wide)
            total = part if total is None else total + part
        return values, total

    @pl.when(step == first_steps)
    def _():
        _, total = grid_values(0, 2)
        code, fine, top = scale_of(jnp.sum(total) / total.size)
        level[0] = code
        level[1] = fine
        level[2] = top
        peak[...] = jnp.zeros_like(peak)

    @pl.when(step >= first_steps)
    def _():
        x0 = (step - first_steps) * some_x
        mean = level[2]
        table = dht_ref[...]
        largest = peak[...]
        for local in range(0, some_x, group):
            values, total = grid_values(x0 + local, group)
            for o in range(orbitals):
                for k in range(group):
                    at = (o * group + k) * cells_y
                    psi_ref[o, local + k] = values[:, at : at + cells_y]
            result = hartley_pair(table, total - mean)
            for k in range(group):
                part = result[:, k * cells_y : (k + 1) * cells_y]
                waves[pl.ds(x0 + local + k, length, stride=pitch), :] = part
                size = jnp.abs(part).reshape(length // 8, 8, cells_y)
                largest = jnp.maximum(largest, jnp.max(size, axis=0))
        peak[...] = largest

    @pl.when(step == pl.num_programs(0) - 1)
    def _():
        code, fine, top = scale_of(jnp.max(peak[...]))
        factor = LEVELS / top
        code_rows = coded_rows(cells_y, (code, fine, level[0], level[1], LEVELS))
        per = length // q_ref.shape[0]
        rows = per * cells_x

        def quantise(i, carry):
            for k in range(per):
                row = pl.multiple_of((i * per + k) * pitch, 8)
                values = jnp.round(waves[pl.ds(row, cells_x), :] * factor)
                at = pl.ds(k * cells_x, cells_x)
                q_ref[i, at, :] = values.astype(jnp.int32).astype(jnp.int16)
            q_ref[i, rows : rows + 16, :] = code_rows
            return carry

        lax.fori_loop(0, q_ref.shape[0], quantise, 0, unroll=4)


def density(occupations, slot_orbital, c, halo, my, ax, mz, dht, owners):
    orbitals, length, cells_x, cells_y = c.shape
    chunks = 2
    part = length // chunks
    first_steps = orbitals * chunks
    some_x = 8
    pitch = cells_x + 8
    smem = pl.BlockSpec(memory_space=pltpu.SMEM)
    rows = (length // owners) * cells_x + 16

    def at_first(s):
        s = jnp.minimum(s, first_steps - 1)
        return (s // chunks, s % chunks, 0, 0)

    return pl.pallas_call(
        functools.partial(density_kernel, first_steps, pitch),
        grid=(first_steps + cells_x // some_x,),
        in_specs=[
            smem,
            smem,
            pl.BlockSpec((1, part, cells_x, cells_y), at_first),
            pl.BlockSpec((1, part, halo.shape[2], cells_y), at_first),
            whole(my),
            whole(ax),
            whole(mz),
            whole(dht),
        ],
        out_specs=[
            pl.BlockSpec(
                (orbitals, some_x, length, cells_y),
                lambda s: (0, jnp.maximum(s - first_steps, 0), 0, 0),
            ),
            pl.BlockSpec((owners, rows, cells_y), lambda s: (0, 0, 0)),
            pl.BlockSpec((8, cells_y), lambda s: (0, 0)),
        ],
        out_shape=[
            pltpu.HBM((orbitals, cells_x, length, cells_y), BF16),
            pltpu.HBM((owners, rows, cells_y), jnp.int16),
            jax.ShapeDtypeStruct((8, cells_y), F32),
        ],
        scratch_shapes=[
            pltpu.VMEM((orbitals * length * pitch, cells_y), F32),
            pltpu.VMEM((length * pitch, cells_y), F32),
            pltpu.SMEM((3,), F32),
        ],
        compiler_params=params(1, 30),
        name="density",
    )(occupations, slot_orbital, c, halo, my, ax, mz, dht)


def kinetic_kernel(
    pitch, c_ref, near_ref, far_ref, dy_ref, dx_ref, dz_ref, after_ref, kin_ref, step_ref, sums_ref, wide, acc
):
    length, cells_x, cells_y = c_ref.shape[1], c_ref.shape[2], c_ref.shape[3]
    block = 8

    def widen(z, carry):
        row = pl.multiple_of(z * pitch, 8)
        wide[pl.ds(row, cells_x), :] = c_ref[0, z].astype(F32)
        return carry

    lax.fori_loop(0, length, widen, 0, unroll=8)

    def columns(i, carry):
        x = 2 * i
        pair = side_by_side(
            wide[pl.ds(x, length, stride=pitch), :].astype(BF16),
            wide[pl.ds(x + 1, length, stride=pitch), :].astype(BF16),
        )
        values = dot(dz_ref[...], pair)
        acc[pl.ds(x, length, stride=pitch), :] = values[:, :cells_y]
        acc[pl.ds(x + 1, length, stride=pitch), :] = values[:, cells_y:]
        return carry

    lax.fori_loop(0, cells_x // 2, columns, 0, unroll=4)

    def planes(i, carry):
        energy, norm = carry
        z0 = i * block
        own = c_ref[0, pl.ds(z0, block)]
        along_y = dot(own.reshape(block * cells_x, cells_y), dy_ref[...])
        steps = []
        for p in range(0, block, 2):
            z = z0 + p
            pair = jnp.concatenate(
                [
                    side_by_side(c_ref[0, z], c_ref[0, z + 1]),
                    side_by_side(near_ref[0, z], near_ref[0, z + 1]),
                    side_by_side(far_ref[0, z], far_ref[0, z + 1]),
                ],
                axis=0,
            )
            along_x = dot(dx_ref[...], pair)
            for k in range(2):
                at = pl.ds(pl.multiple_of((z + k) * pitch, 8), cells_x)
                value = (
                    acc[at, :]
                    + along_x[:, k * cells_y : (k + 1) * cells_y]
                    + along_y[(p + k) * cells_x : (p + k + 1) * cells_x]
                )
                tiles = (cells_x // 8, 8, cells_y)
                largest = jnp.max(jnp.max(jnp.abs(value).reshape(tiles), axis=0), axis=0)
                largest = jnp.maximum(largest, 1e-30).reshape(1, cells_y)
                coded = jnp.round(value * (LEVELS / largest))
                kin_ref[0, z + k] = coded.astype(jnp.int32).astype(jnp.int16)
                steps.append(largest * (1.0 / LEVELS))
                coeff = own[p + k].astype(F32)
                energy = energy + jnp.sum((coeff * value).reshape(tiles), axis=0)
                norm = norm + jnp.sum((coeff * coeff).reshape(tiles), axis=0)
        step_ref[0, pl.ds(pl.multiple_of(z0, block), block), :] = jnp.concatenate(steps, axis=0)
        return energy, norm

    zeros = jnp.zeros((8, cells_y), F32)
    energy, norm = lax.fori_loop(0, length // block, planes, (zeros, zeros), unroll=2)
    sums_ref[0, 0:8] = energy
    sums_ref[0, 8:16] = norm


def kinetic(c, near, far, dy, dx, dz, after):
    orbitals, length, cells_x, cells_y = c.shape
    cells = orbitals * length * cells_x * cells_y
    pitch = cells_x + 8

    def block(array):
        return pl.BlockSpec((1, *array.shape[1:]), lambda o: (o, 0, 0, 0))

    return pl.pallas_call(
        functools.partial(kinetic_kernel, pitch),
        grid=(orbitals,),
        in_specs=[
            block(c),
            block(near),
            block(far),
            whole(dy),
            whole(dx),
            whole(dz),
            pl.BlockSpec(memory_space=pl.ANY),
        ],
        out_specs=[
            block(c),
            pl.BlockSpec((1, length, cells_y), lambda o: (o, 0, 0)),
            pl.BlockSpec((1, 16, cells_y), lambda o: (o, 0, 0)),
        ],
        out_shape=[
            pltpu.HBM(c.shape, jnp.int16),
            jax.ShapeDtypeStruct((orbitals, length, cells_y), F32),
            jax.ShapeDtypeStruct((orbitals, 16, cells_y), F32),
        ],
        scratch_shapes=[
            pltpu.VMEM((length * pitch, cells_y), F32),
            pltpu.VMEM((length * pitch, cells_y), F32),
        ],
        compiler_params=params(1, 26),
        cost_estimate=pl.CostEstimate(
            flops=cells * 768 * 4, bytes_accessed=cells * 7, transcendentals=0
        ),
        name="kinetic",
    )(c, near, far, dy, dx, dz, after)


def unpacked(ref, source, rows):
    codes = ref[source, rows : rows + 16, :].astype(jnp.int32).astype(F32)
    powers = jnp.exp2(codes) * (1.0 / (LEVELS * FINE))
    step = codes[1:2] * powers[0:1]
    mean = codes[4:5] * (codes[3:4] * powers[2:3])
    return ref[source, 0:rows, :].astype(jnp.int32).astype(F32) * step, mean


def sum_kernel(per, got_ref, after_ref, out_ref):
    rows = out_ref.shape[0]
    cells_y = out_ref.shape[1]

    def body(source, carry):
        total, means = carry
        values, mean = unpacked(got_ref, source, rows)
        return total + values, means + mean

    total, means = lax.fori_loop(
        0,
        got_ref.shape[0],
        body,
        (jnp.zeros((rows, cells_y), F32), jnp.zeros((1, cells_y), F32)),
        unroll=2,
    )
    length = got_ref.shape[0] * per
    row = lax.broadcasted_iota(jnp.int32, (rows, cells_y), 0)
    flat = (lax.axis_index("orb") == 0) & (row < rows // per)
    out_ref[...] = total + jnp.where(flat, means * math.sqrt(length), 0.0)


def slab_sum(got, rows, per, after):
    return pl.pallas_call(
        functools.partial(sum_kernel, per),
        in_specs=[pl.BlockSpec(memory_space=pltpu.VMEM), pl.BlockSpec(memory_space=pl.ANY)],
        out_shape=jax.ShapeDtypeStruct((rows, got.shape[2]), F32),
        compiler_params=params(0, 12),
        name="slab_sum",
    )(got, after)


def solve_kernel(curve_z_ref, slab_ref, dht_ref, curve_ref, q_ref):
    per, length, cells_y = slab_ref.shape
    cells_x = length // 2
    orb = lax.axis_index("orb")
    corner = pl.multiple_of(lax.axis_index("grid") * cells_x, cells_x)
    dht = dht_ref[...]
    own = dht_ref[pl.ds(corner, cells_x), :]
    row = lax.broadcasted_iota(jnp.int32, (length, cells_y), 0)
    col = lax.broadcasted_iota(jnp.int32, (length, cells_y), 1)
    waves = dot_exact(jnp.concatenate([slab_ref[k] for k in range(per)], axis=0), dht)
    waves = jnp.concatenate(
        [waves[k * length : (k + 1) * length] for k in range(per)], axis=1
    )
    waves = dot_exact(dht, waves)
    parts = []
    for k in range(per):
        wave = orb * per + k
        anchor = (row == 0) & (col == 0) & (wave == 0)
        bent = curve_ref[...] + curve_z_ref[wave]
        factor = jnp.where(anchor, 0.0, COULOMB / jnp.where(anchor, 1.0, bent))
        parts.append(waves[:, k * cells_y : (k + 1) * cells_y] * factor)
    field = dot_exact(own, jnp.concatenate(parts, axis=1))
    field = jnp.concatenate(
        [field[:, k * cells_y : (k + 1) * cells_y] for k in range(per)], axis=0
    )
    field = dot_exact(field, dht)
    code, fine, top = scale_of(jnp.max(jnp.abs(field)))
    coded = jnp.round(field * (LEVELS / top)).astype(jnp.int32).astype(jnp.int16)
    code_rows = coded_rows(cells_y, (code, fine))
    rows = per * cells_x

    def spread(i, carry):
        q_ref[i, 0:rows, :] = coded
        q_ref[i, rows : rows + 16, :] = code_rows
        return carry

    lax.fori_loop(0, q_ref.shape[0], spread, 0, unroll=4)


def solve(curve_z, slab, dht, plane_curve, owners):
    per, length, cells_y = slab.shape
    vmem = pl.BlockSpec(memory_space=pltpu.VMEM)
    return pl.pallas_call(
        solve_kernel,
        in_specs=[pl.BlockSpec(memory_space=pltpu.SMEM), vmem, vmem, vmem],
        out_shape=jax.ShapeDtypeStruct((owners, per * (length // 2) + 16, cells_y), jnp.int16),
        compiler_params=params(0, 12),
        name="solve",
    )(curve_z, slab, dht, plane_curve)


def field_kernel(
    pitch,
    turn_pitch,
    got_ref,
    psi_ref,
    kin_ref,
    dht_ref,
    tz_ref,
    back_ref,
    rim_ref,
    slab_ref,
    sums_ref,
    waves,
    turn,
    head,
    values,
):
    step = pl.program_id(0)
    orbitals, some_x, length, cells_y = psi_ref.shape
    owners = got_ref.shape[0]
    per = length // owners
    cells_x = some_x * pl.num_programs(0)
    rim = rim_ref.shape[2] // 2
    first = pl.multiple_of((lax.axis_index("orb") * per) // 8 * 8, 8)

    @pl.when(step == 0)
    def _():
        def unpack(source, carry):
            found, _ = unpacked(got_ref, source, per * cells_x)
            for k in range(per):
                at = pl.ds(pl.multiple_of((source * per + k) * pitch, 8), cells_x)
                waves[at, :] = found[k * cells_x : (k + 1) * cells_x]
            return carry

        lax.fori_loop(0, owners, unpack, 0, unroll=4)
        sums_ref[...] = kin_ref[...]

    group = 8
    energy = [jnp.zeros((8, cells_y), F32) for _ in range(orbitals)]
    for local in range(0, some_x, group):
        x = step * some_x + local
        field = hartley_pair(
            dht_ref[...],
            jnp.concatenate(
                [waves[pl.ds(x + k, length, stride=pitch), :] for k in range(group)], axis=1
            ),
        )
        values[local // group] = field
        own = values[local // group, pl.ds(first, 8), :]
        for k in range(group):
            slab_ref[local + k] = own[:, k * cells_y : (k + 1) * cells_y]
        products = []
        for o in range(orbitals):
            psi = jnp.concatenate([psi_ref[o, local + k] for k in range(group)], axis=1)
            psi = psi.astype(F32)
            product = field * psi
            products.append(product.astype(BF16))
            squares = product * psi
            for k in range(group):
                part = squares[:, k * cells_y : (k + 1) * cells_y]
                part = part.reshape(length // 8, 8, cells_y)
                energy[o] = energy[o] + jnp.sum(part, axis=0)
        back = dot(tz_ref[...], jnp.concatenate(products, axis=1))
        for o in range(orbitals):
            for k in range(group):
                at = (o * group + k) * cells_y
                row = o * length * turn_pitch + local + k
                turn[pl.ds(row, length, stride=turn_pitch), :] = back[:, at : at + cells_y]

    for o in range(orbitals):
        sums_ref[o, 0:8] = sums_ref[o, 0:8] + energy[o]

    def turned(o, z, start, count):
        row = pl.multiple_of((o * length + z) * turn_pitch, 8) + start
        return turn[pl.ds(row, count), :]

    def rows(z, carry):
        for o in range(orbitals):
            back_ref[o, z] = turned(o, z, 0, some_x).astype(BF16)
        return carry

    lax.fori_loop(0, length, rows, 0, unroll=8)

    @pl.when(step == 0)
    def _():
        def keep(z, carry):
            for o in range(orbitals):
                head[o, z] = turned(o, z, 0, rim)
            return carry

        lax.fori_loop(0, length, keep, 0, unroll=8)

    @pl.when(step == pl.num_programs(0) - 1)
    def _():
        def send(z, carry):
            for o in range(orbitals):
                both = jnp.concatenate([turned(o, z, some_x - rim, rim), head[o, z]], axis=0)
                rim_ref[o, z] = both.astype(BF16)
            return carry

        lax.fori_loop(0, length, send, 0, unroll=8)


def field(got, psi, kin_sums, dht, tz):
    orbitals, cells_x, length, cells_y = psi.shape
    some_x = 16
    pitch = cells_x + 8
    turn_pitch = some_x + 8
    rim = 8
    return pl.pallas_call(
        functools.partial(field_kernel, pitch, turn_pitch),
        grid=(cells_x // some_x,),
        in_specs=[
            pl.BlockSpec(memory_space=pltpu.VMEM),
            pl.BlockSpec((orbitals, some_x, length, cells_y), lambda i: (0, i, 0, 0)),
            whole(kin_sums),
            whole(dht),
            whole(tz),
        ],
        out_specs=[
            pl.BlockSpec((orbitals, length, some_x, cells_y), lambda i: (0, 0, i, 0)),
            pl.BlockSpec((orbitals, length, 2 * rim, cells_y), lambda i: (0, 0, 0, 0)),
            pl.BlockSpec((some_x, 8, cells_y), lambda i: (i, 0, 0)),
            whole(kin_sums),
        ],
        out_shape=[
            pltpu.HBM((orbitals, length, cells_x, cells_y), BF16),
            jax.ShapeDtypeStruct((orbitals, length, 2 * rim, cells_y), BF16),
            jax.ShapeDtypeStruct((cells_x, 8, cells_y), F32),
            jax.ShapeDtypeStruct(kin_sums.shape, F32),
        ],
        scratch_shapes=[
            pltpu.VMEM((length * pitch, cells_y), F32),
            pltpu.VMEM((orbitals * length * turn_pitch, cells_y), F32),
            pltpu.VMEM((orbitals, length, rim, cells_y), F32),
            pltpu.VMEM((2, length, 8 * cells_y), F32),
        ],
        compiler_params=params(1, 26),
        name="field",
    )(got, psi, kin_sums, dht, tz)


def update_kernel(
    sums_ref,
    other_ref,
    back_ref,
    rim_ref,
    c_ref,
    kin_ref,
    step_ref,
    tx_ref,
    ty_ref,
    out_ref,
    energy_ref,
):
    orbital = pl.program_id(0)

    @pl.when(pl.program_id(1) == 0)
    def _():
        both = sums_ref[orbital] + other_ref[orbital]
        energy_ref[orbital] = jnp.sum(both[0:8]) / jnp.sum(both[8:16])

    energy = energy_ref[orbital]
    some_z, cells_x, cells_y = back_ref.shape[1], back_ref.shape[2], back_ref.shape[3]
    tx = tx_ref[...]
    ty = ty_ref[...]
    block = 16
    many = 8

    def planes(i, carry):
        z0 = i * block
        crossed = []
        for p in range(0, block, many):
            some = range(p, p + many)
            flat = jnp.concatenate(
                [
                    jnp.concatenate([back_ref[0, z0 + k] for k in some], axis=1),
                    jnp.concatenate([rim_ref[0, z0 + k] for k in some], axis=1),
                ],
                axis=0,
            )
            both = dot(tx, flat).astype(BF16)
            crossed += [both[:, k * cells_y : (k + 1) * cells_y] for k in range(many)]
        potential = dot(jnp.concatenate(crossed, axis=0), ty)
        steps = step_ref[0, pl.ds(pl.multiple_of(z0, block), block), :]
        for p in range(block):
            z = z0 + p
            kin = kin_ref[0, z].astype(jnp.int32).astype(F32) * steps[p : p + 1]
            applied = potential[p * cells_x : (p + 1) * cells_x] + kin
            coeff = c_ref[0, z].astype(F32)
            out_ref[0, z] = (coeff - STEP_SIZE * (applied - energy * coeff)).astype(BF16)
        return carry

    lax.fori_loop(0, some_z // block, planes, 0, unroll=4)


def update(sums, other_sums, back, rim, c, kin, steps, tx, ty):
    orbitals, length, cells_x, cells_y = c.shape
    chunks = 2
    part = length // chunks
    block = pl.BlockSpec((1, part, cells_x, cells_y), lambda o, j: (o, j, 0, 0))
    return pl.pallas_call(
        update_kernel,
        grid=(orbitals, chunks),
        in_specs=[
            whole(sums),
            whole(other_sums),
            block,
            pl.BlockSpec((1, part, rim.shape[2], cells_y), lambda o, j: (o, j, 0, 0)),
            block,
            block,
            pl.BlockSpec((1, part, cells_y), lambda o, j: (o, j, 0)),
            whole(tx),
            whole(ty),
        ],
        out_specs=[block, pl.BlockSpec(memory_space=pltpu.SMEM)],
        out_shape=[
            jax.ShapeDtypeStruct(c.shape, BF16),
            jax.ShapeDtypeStruct((orbitals,), F32),
        ],
        compiler_params=params(2, 12),
        name="update",
    )(sums, other_sums, back, rim, c, kin, steps, tx, ty)


def to_other(array):
    return lax.ppermute(array, "grid", [(0, 1), (1, 0)])


def in_hbm(array):
    return pltpu.with_memory_space_constraint(array, pltpu.HBM)


def to_all(blocks):
    return lax.all_to_all(blocks, "orb", split_axis=0, concat_axis=0, tiled=True)


def on_device(coefficients, occupations, slot_orbital):
    orbitals, length, cells_x, cells_y = coefficients.shape
    owners = slot_orbital.shape[0] // orbitals
    per = length // owners
    magic, trans, kin_taps = magic_pairs(), transposed_pairs(), kinetic_pairs()
    magic_line = band_periodic(length, magic)
    trans_line = band_periodic(length, trans)
    kin_line = band_periodic(length, kin_taps, -0.5)
    inside = list(range(cells_x))
    near_cells = inside + with_rims(cells_x, 0, 8)
    all_cells = near_cells + with_rims(cells_x, 8, 16)
    dht = hartley(length)
    table = jnp.asarray(split_table(dht))
    waves = curve(length)

    c = in_hbm(coefficients)
    own_near, mark = own_rims(c, 0, 8)
    near = to_other(own_near)
    far = to_other(own_rims(c, 8, 16, mark)[0])
    psi, coded, peak = density(
        occupations,
        slot_orbital,
        coefficients,
        near,
        jnp.asarray(magic_line.T),
        jnp.asarray(band_columns(cells_x, near_cells, magic)),
        jnp.asarray(magic_line),
        table,
        owners,
    )
    got = to_all(coded)
    kin, steps, kin_sums = kinetic(
        c,
        near,
        far,
        jnp.asarray(kin_line.T),
        jnp.asarray(band_columns(cells_x, all_cells, kin_taps, -0.5)),
        jnp.asarray(kin_line),
        peak,
    )
    half = slab_sum(got, per * cells_x, per, kin_sums).reshape(per, cells_x, cells_y)
    slab = lax.all_gather(half, "grid", axis=1, tiled=True)
    spread = solve(
        jnp.asarray(waves.astype(np.float32)),
        slab,
        jnp.asarray(dht),
        jnp.asarray((waves[:, None] + waves[None, :]).astype(np.float32)),
        owners,
    )
    back, back_rims, slab_field, sums = field(
        to_all(spread), psi, kin_sums, table, jnp.asarray(trans_line)
    )
    updated, energies = update(
        sums,
        to_other(sums),
        in_hbm(back),
        to_other(back_rims),
        c,
        in_hbm(kin),
        steps,
        jnp.asarray(band_columns(cells_x, near_cells, trans)),
        jnp.asarray(trans_line.T),
    )
    first = lax.rem(lax.axis_index("orb") * per, 8)
    potential = lax.dynamic_slice_in_dim(slab_field, first, per, 1).transpose(1, 0, 2)
    return (updated, energies, potential)


def solution(mesh):
    return jax.shard_map(
        on_device,
        mesh=mesh,
        in_specs=(P("orb", None, "grid", None), P(), P()),
        out_specs=(P("orb", None, "grid", None), P("orb"), P("orb", "grid", None)),
        check_vma=False,
    )
```

```python
import functools
import math

import jax
import jax.numpy as jnp
import ml_dtypes
import numpy as np
from jax import lax
from jax.experimental import pallas as pl
from jax.experimental.pallas import tpu as pltpu
from jax.sharding import PartitionSpec as P

MAGIC = (
    8.433424733352934e-07,
    -1.290557201342061e-05,
    8.76298447621056e-05,
    -0.00030158038132690465,
    0.001747237136729939,
    -0.009420470302010804,
    0.023738214637249424,
    0.0612625895831208,
    0.9940415697834004,
    -0.06048952891969835,
    -0.021030251609303816,
    0.013372634148547948,
    -0.0034412814449349387,
    0.0004944322768868992,
    -5.185986881173433e-05,
    2.7273449291197967e-06,
)
STEP_SIZE = 0.1
COULOMB = 4.0 * math.pi
LEVELS = 32000.0
CODE_ROWS = 8
FINE = 16384.0
F32 = jnp.float32
BF16 = jnp.bfloat16
HIGHEST = lax.Precision.HIGHEST
MIB = 1024 * 1024


def magic_pairs():
    return [(position - 8, MAGIC[position]) for position in range(16)]


def transposed_pairs():
    return [(8 - position, MAGIC[position]) for position in range(16)]


def kinetic_pairs():
    spread = 14
    weights = []
    for distance in range(1, spread + 1):
        numerator = 2.0 * (-1.0) ** (distance + 1) * math.factorial(spread) ** 2
        weights.append(
            numerator
            / (
                distance
                * distance
                * math.factorial(spread - distance)
                * math.factorial(spread + distance)
            )
        )
    result = [(0, -2.0 * sum(weights))]
    for distance in range(1, spread + 1):
        result.append((distance, weights[distance - 1]))
        result.append((-distance, weights[distance - 1]))
    return result


def rounded(weight):
    return np.float32(np.float32(weight).astype(ml_dtypes.bfloat16))


def band_periodic(length, pairs, scale=1.0):
    matrix = np.zeros((length, length), np.float32)
    for offset, weight in pairs:
        for i in range(length):
            matrix[i, (i + offset) % length] += scale * rounded(weight)
    return matrix.astype(ml_dtypes.bfloat16)


def band_columns(length, columns, pairs, scale=1.0):
    matrix = np.zeros((length, len(columns)), np.float32)
    place = {cell: k for k, cell in enumerate(columns)}
    for offset, weight in pairs:
        for i in range(length):
            matrix[i, place[i + offset]] += scale * rounded(weight)
    return matrix.astype(ml_dtypes.bfloat16)


def with_rims(length, inner, outer):
    return [*range(-outer, -inner), *range(length + inner, length + outer)]


def hartley(length):
    index = np.arange(length)
    angle = 2.0 * np.pi * ((index[:, None] * index[None, :]) % length) / length
    return ((np.cos(angle) + np.sin(angle)) / math.sqrt(length)).astype(np.float32)


def split_table(table):
    high = table.astype(ml_dtypes.bfloat16)
    low = (table - high.astype(np.float32)).astype(ml_dtypes.bfloat16)
    return np.concatenate([high, low, high], axis=1)


def curve(length):
    return 2.0 - 2.0 * np.cos(2.0 * np.pi * np.arange(length) / length)


def dot(a, b):
    return jnp.dot(a, b, preferred_element_type=F32)


def dot_exact(a, b):
    return jnp.dot(a, b, preferred_element_type=F32, precision=HIGHEST)


def params(count, mebibytes):
    return pltpu.CompilerParams(
        dimension_semantics=("arbitrary",) * count, vmem_limit_bytes=mebibytes * MIB
    )


def cost(cells, bytes_each):
    return pl.CostEstimate(
        flops=cells * 256, bytes_accessed=cells * bytes_each, transcendentals=0
    )


def whole(array):
    zeros = (0,) * array.ndim
    return pl.BlockSpec(array.shape, lambda *_: zeros)


def scale_of(largest):
    largest = jnp.maximum(largest, 1e-30)
    code = jnp.ceil(jnp.log2(largest))
    power = jnp.exp2(code)
    units = jnp.ceil(largest / power * FINE) + 1.0
    return code, units, units * (1.0 / FINE) * power


def coded_rows(cells_y, codes):
    row = lax.broadcasted_iota(jnp.int32, (CODE_ROWS, cells_y), 0)
    values = jnp.zeros((CODE_ROWS, cells_y), F32)
    for k, code in enumerate(codes):
        values = jnp.where(row == k, code, values)
    return values.astype(jnp.int32).astype(jnp.int16)


def side_by_side(first, second):
    return jnp.concatenate([first, second], axis=1)


def hartley_pair(table, pair):
    high = pair.astype(BF16)
    low = (pair - high.astype(F32)).astype(BF16)
    return dot(table, jnp.concatenate([high, high, low], axis=0))


def rims_kernel(inner, outer, low_ref, high_ref, *rest):
    out_ref, mark_ref = rest[-2:]
    tile = low_ref.shape[2]
    low = low_ref[...].astype(F32)[:, :, tile - outer : tile - inner]
    high = high_ref[...].astype(F32)[:, :, inner:outer]
    out_ref[...] = jnp.concatenate([low, high], axis=2).astype(BF16)
    mark_ref[...] = jnp.zeros_like(mark_ref)


def own_rims(c, inner, outer, *after):
    orbitals, length, cells_x, cells_y = c.shape
    tile = 16

    def at(k):
        return pl.BlockSpec((orbitals, length, tile, cells_y), lambda o: (0, 0, k, 0))

    return pl.pallas_call(
        functools.partial(rims_kernel, inner, outer),
        grid=(1,),
        in_specs=[at(cells_x // tile - 1), at(0)]
        + [pl.BlockSpec(memory_space=pl.ANY) for _ in after],
        out_specs=[at(0), pl.BlockSpec((8, cells_y), lambda o: (0, 0))],
        out_shape=[
            jax.ShapeDtypeStruct((orbitals, length, 2 * (outer - inner), cells_y), BF16),
            jax.ShapeDtypeStruct((8, cells_y), F32),
        ],
        compiler_params=params(1, 16),
        name="own_rims",
    )(c, c, *after)


def density_kernel(
    first_steps,
    pitch,
    occ_ref,
    slot_ref,
    c_ref,
    h_ref,
    my_ref,
    ax_ref,
    mz_ref,
    dht_ref,
    psi_ref,
    q_ref,
    peak,
    mid,
    waves,
    level,
):
    step = pl.program_id(0)
    cells_z, cells_x, cells_y = c_ref.shape[1], c_ref.shape[2], c_ref.shape[3]
    rim = h_ref.shape[2]
    orbitals, some_x, length = psi_ref.shape[0], psi_ref.shape[1], psi_ref.shape[2]
    block = 64
    many = 8
    group = 8

    @pl.when(step < first_steps)
    def _():
        my = my_ref[...]
        ax = ax_ref[...]

        def planes(i, carry):
            z0 = i * block
            own = dot(c_ref[0, pl.ds(z0, block)].reshape(block * cells_x, cells_y), my)
            own = own.astype(BF16).reshape(block, cells_x, cells_y)
            far = dot(h_ref[0, pl.ds(z0, block)].reshape(block * rim, cells_y), my)
            far = far.astype(BF16).reshape(block, rim, cells_y)
            for p in range(0, block, many):
                some = range(p, p + many)
                flat = jnp.concatenate(
                    [
                        jnp.concatenate([own[z] for z in some], axis=1),
                        jnp.concatenate([far[z] for z in some], axis=1),
                    ],
                    axis=0,
                )
                crossed = dot(ax, flat)
                for k in range(many):
                    row = pl.multiple_of((step * cells_z + z0 + p + k) * pitch, 8)
                    mid[pl.ds(row, cells_x), :] = crossed[:, k * cells_y : (k + 1) * cells_y]
            return carry

        lax.fori_loop(0, cells_z // block, planes, 0)

    def grid_values(x, count):
        first = lax.axis_index("orb") * orbitals
        columns = [
            mid[pl.ds(o * length * pitch + x + k, length, stride=pitch), :].astype(BF16)
            for o in range(orbitals)
            for k in range(count)
        ]
        values = dot(mz_ref[...], jnp.concatenate(columns, axis=1)).astype(BF16)
        total = None
        for o in range(orbitals):
            weight = occ_ref[slot_ref[first + o]].astype(F32) / slot_ref.shape[0]
            wide = values[:, o * count * cells_y : (o + 1) * count * cells_y].astype(F32)
            part = weight * (wide * wide)
            total = part if total is None else total + part
        return values, total

    @pl.when(step == first_steps)
    def _():
        _, total = grid_values(0, 2)
        code, fine, top = scale_of(jnp.sum(total) / total.size)
        level[0] = code
        level[1] = fine
        level[2] = top
        peak[...] = jnp.zeros_like(peak)

    @pl.when(step >= first_steps)
    def _():
        x0 = (step - first_steps) * some_x
        mean = level[2]
        table = dht_ref[...]
        largest = peak[...]
        for local in range(0, some_x, group):
            values, total = grid_values(x0 + local, group)
            for o in range(orbitals):
                for k in range(group):
                    at = (o * group + k) * cells_y
                    psi_ref[o, local + k] = values[:, at : at + cells_y]
            result = hartley_pair(table, total - mean)
            for k in range(group):
                part = result[:, k * cells_y : (k + 1) * cells_y]
                waves[pl.ds(x0 + local + k, length, stride=pitch), :] = part
                size = jnp.abs(part).reshape(length // 8, 8, cells_y)
                largest = jnp.maximum(largest, jnp.max(size, axis=0))
        peak[...] = largest

    @pl.when(step == pl.num_programs(0) - 1)
    def _():
        code, fine, top = scale_of(jnp.max(peak[...]))
        factor = LEVELS / top
        code_rows = coded_rows(cells_y, (code, fine, level[0], level[1], LEVELS))
        per = length // q_ref.shape[0]
        rows = per * cells_x

        def quantise(i, carry):
            for k in range(per):
                row = pl.multiple_of((i * per + k) * pitch, 8)
                values = jnp.round(waves[pl.ds(row, cells_x), :] * factor)
                at = pl.ds(k * cells_x, cells_x)
                q_ref[i, at, :] = values.astype(jnp.int32).astype(jnp.int16)
            q_ref[i, rows : rows + CODE_ROWS, :] = code_rows
            return carry

        lax.fori_loop(0, q_ref.shape[0], quantise, 0, unroll=4)


def density(occupations, slot_orbital, c, halo, my, ax, mz, dht, owners):
    orbitals, length, cells_x, cells_y = c.shape
    chunks = 2
    part = length // chunks
    first_steps = orbitals * chunks
    some_x = 8
    pitch = cells_x + 8
    smem = pl.BlockSpec(memory_space=pltpu.SMEM)
    rows = (length // owners) * cells_x + CODE_ROWS

    def at_first(s):
        s = jnp.minimum(s, first_steps - 1)
        return (s // chunks, s % chunks, 0, 0)

    return pl.pallas_call(
        functools.partial(density_kernel, first_steps, pitch),
        grid=(first_steps + cells_x // some_x,),
        in_specs=[
            smem,
            smem,
            pl.BlockSpec((1, part, cells_x, cells_y), at_first),
            pl.BlockSpec((1, part, halo.shape[2], cells_y), at_first),
            whole(my),
            whole(ax),
            whole(mz),
            whole(dht),
        ],
        out_specs=[
            pl.BlockSpec(
                (orbitals, some_x, length, cells_y),
                lambda s: (0, jnp.maximum(s - first_steps, 0), 0, 0),
            ),
            pl.BlockSpec((owners, rows, cells_y), lambda s: (0, 0, 0)),
            pl.BlockSpec((8, cells_y), lambda s: (0, 0)),
        ],
        out_shape=[
            pltpu.HBM((orbitals, cells_x, length, cells_y), BF16),
            pltpu.HBM((owners, rows, cells_y), jnp.int16),
            jax.ShapeDtypeStruct((8, cells_y), F32),
        ],
        scratch_shapes=[
            pltpu.VMEM((orbitals * length * pitch, cells_y), F32),
            pltpu.VMEM((length * pitch, cells_y), F32),
            pltpu.SMEM((3,), F32),
        ],
        compiler_params=params(1, 30),
        name="density",
    )(occupations, slot_orbital, c, halo, my, ax, mz, dht)


def kinetic_kernel(
    pitch, c_ref, near_ref, far_ref, dy_ref, dx_ref, dz_ref, after_ref, kin_ref, step_ref, sums_ref, wide, acc
):
    length, cells_x, cells_y = c_ref.shape[1], c_ref.shape[2], c_ref.shape[3]
    block = 8

    def widen(z, carry):
        row = pl.multiple_of(z * pitch, 8)
        wide[pl.ds(row, cells_x), :] = c_ref[0, z].astype(F32)
        return carry

    lax.fori_loop(0, length, widen, 0, unroll=8)

    def columns(i, carry):
        x = 2 * i
        pair = side_by_side(
            wide[pl.ds(x, length, stride=pitch), :].astype(BF16),
            wide[pl.ds(x + 1, length, stride=pitch), :].astype(BF16),
        )
        values = dot(dz_ref[...], pair)
        acc[pl.ds(x, length, stride=pitch), :] = values[:, :cells_y]
        acc[pl.ds(x + 1, length, stride=pitch), :] = values[:, cells_y:]
        return carry

    lax.fori_loop(0, cells_x // 2, columns, 0, unroll=4)

    def planes(i, carry):
        energy, norm = carry
        z0 = i * block
        own = c_ref[0, pl.ds(z0, block)]
        along_y = dot(own.reshape(block * cells_x, cells_y), dy_ref[...])
        steps = []
        for p in range(0, block, 2):
            z = z0 + p
            pair = jnp.concatenate(
                [
                    side_by_side(c_ref[0, z], c_ref[0, z + 1]),
                    side_by_side(near_ref[0, z], near_ref[0, z + 1]),
                    side_by_side(far_ref[0, z], far_ref[0, z + 1]),
                ],
                axis=0,
            )
            along_x = dot(dx_ref[...], pair)
            for k in range(2):
                at = pl.ds(pl.multiple_of((z + k) * pitch, 8), cells_x)
                value = (
                    acc[at, :]
                    + along_x[:, k * cells_y : (k + 1) * cells_y]
                    + along_y[(p + k) * cells_x : (p + k + 1) * cells_x]
                )
                tiles = (cells_x // 8, 8, cells_y)
                largest = jnp.max(jnp.max(jnp.abs(value).reshape(tiles), axis=0), axis=0)
                largest = jnp.maximum(largest, 1e-30).reshape(1, cells_y)
                coded = jnp.round(value * (LEVELS / largest))
                kin_ref[0, z + k] = coded.astype(jnp.int32).astype(jnp.int16)
                steps.append(largest * (1.0 / LEVELS))
                coeff = own[p + k].astype(F32)
                energy = energy + jnp.sum((coeff * value).reshape(tiles), axis=0)
                norm = norm + jnp.sum((coeff * coeff).reshape(tiles), axis=0)
        step_ref[0, pl.ds(pl.multiple_of(z0, block), block), :] = jnp.concatenate(steps, axis=0)
        return energy, norm

    zeros = jnp.zeros((8, cells_y), F32)
    energy, norm = lax.fori_loop(0, length // block, planes, (zeros, zeros), unroll=2)
    sums_ref[0, 0:8] = energy
    sums_ref[0, 8:16] = norm


def kinetic(c, near, far, dy, dx, dz, after):
    orbitals, length, cells_x, cells_y = c.shape
    cells = orbitals * length * cells_x * cells_y
    pitch = cells_x + 8

    def block(array):
        return pl.BlockSpec((1, *array.shape[1:]), lambda o: (o, 0, 0, 0))

    return pl.pallas_call(
        functools.partial(kinetic_kernel, pitch),
        grid=(orbitals,),
        in_specs=[
            block(c),
            block(near),
            block(far),
            whole(dy),
            whole(dx),
            whole(dz),
            pl.BlockSpec(memory_space=pl.ANY),
        ],
        out_specs=[
            block(c),
            pl.BlockSpec((1, length, cells_y), lambda o: (o, 0, 0)),
            pl.BlockSpec((1, 16, cells_y), lambda o: (o, 0, 0)),
        ],
        out_shape=[
            pltpu.HBM(c.shape, jnp.int16),
            jax.ShapeDtypeStruct((orbitals, length, cells_y), F32),
            jax.ShapeDtypeStruct((orbitals, 16, cells_y), F32),
        ],
        scratch_shapes=[
            pltpu.VMEM((length * pitch, cells_y), F32),
            pltpu.VMEM((length * pitch, cells_y), F32),
        ],
        compiler_params=params(1, 26),
        cost_estimate=pl.CostEstimate(
            flops=cells * 768 * 4, bytes_accessed=cells * 7, transcendentals=0
        ),
        name="kinetic",
    )(c, near, far, dy, dx, dz, after)


def unpacked(ref, source, rows):
    codes = ref[source, rows : rows + CODE_ROWS, :].astype(jnp.int32).astype(F32)
    powers = jnp.exp2(codes) * (1.0 / (LEVELS * FINE))
    step = codes[1:2] * powers[0:1]
    mean = codes[4:5] * (codes[3:4] * powers[2:3])
    return ref[source, 0:rows, :].astype(jnp.int32).astype(F32) * step, mean


def sum_kernel(per, got_ref, after_ref, out_ref):
    rows = out_ref.shape[0]
    cells_y = out_ref.shape[1]

    def body(source, carry):
        total, means = carry
        values, mean = unpacked(got_ref, source, rows)
        return total + values, means + mean

    total, means = lax.fori_loop(
        0,
        got_ref.shape[0],
        body,
        (jnp.zeros((rows, cells_y), F32), jnp.zeros((1, cells_y), F32)),
        unroll=2,
    )
    length = got_ref.shape[0] * per
    row = lax.broadcasted_iota(jnp.int32, (rows, cells_y), 0)
    flat = (lax.axis_index("orb") == 0) & (row < rows // per)
    out_ref[...] = total + jnp.where(flat, means * math.sqrt(length), 0.0)


def slab_sum(got, rows, per, after):
    return pl.pallas_call(
        functools.partial(sum_kernel, per),
        in_specs=[pl.BlockSpec(memory_space=pltpu.VMEM), pl.BlockSpec(memory_space=pl.ANY)],
        out_shape=jax.ShapeDtypeStruct((rows, got.shape[2]), F32),
        compiler_params=params(0, 12),
        name="slab_sum",
    )(got, after)


def solve_kernel(curve_z_ref, slab_ref, dht_ref, curve_ref, q_ref):
    per, length, cells_y = slab_ref.shape
    cells_x = length // 2
    orb = lax.axis_index("orb")
    corner = pl.multiple_of(lax.axis_index("grid") * cells_x, cells_x)
    dht = dht_ref[...]
    own = dht_ref[pl.ds(corner, cells_x), :]
    row = lax.broadcasted_iota(jnp.int32, (length, cells_y), 0)
    col = lax.broadcasted_iota(jnp.int32, (length, cells_y), 1)
    waves = dot_exact(jnp.concatenate([slab_ref[k] for k in range(per)], axis=0), dht)
    waves = jnp.concatenate(
        [waves[k * length : (k + 1) * length] for k in range(per)], axis=1
    )
    waves = dot_exact(dht, waves)
    parts = []
    for k in range(per):
        wave = orb * per + k
        anchor = (row == 0) & (col == 0) & (wave == 0)
        bent = curve_ref[...] + curve_z_ref[wave]
        factor = jnp.where(anchor, 0.0, COULOMB / jnp.where(anchor, 1.0, bent))
        parts.append(waves[:, k * cells_y : (k + 1) * cells_y] * factor)
    field = dot_exact(own, jnp.concatenate(parts, axis=1))
    field = jnp.concatenate(
        [field[:, k * cells_y : (k + 1) * cells_y] for k in range(per)], axis=0
    )
    field = dot_exact(field, dht)
    code, fine, top = scale_of(jnp.max(jnp.abs(field)))
    coded = jnp.round(field * (LEVELS / top)).astype(jnp.int32).astype(jnp.int16)
    code_rows = coded_rows(cells_y, (code, fine))
    rows = per * cells_x

    def spread(i, carry):
        q_ref[i, 0:rows, :] = coded
        q_ref[i, rows : rows + CODE_ROWS, :] = code_rows
        return carry

    lax.fori_loop(0, q_ref.shape[0], spread, 0, unroll=4)


def solve(curve_z, slab, dht, plane_curve, owners):
    per, length, cells_y = slab.shape
    vmem = pl.BlockSpec(memory_space=pltpu.VMEM)
    return pl.pallas_call(
        solve_kernel,
        in_specs=[pl.BlockSpec(memory_space=pltpu.SMEM), vmem, vmem, vmem],
        out_shape=jax.ShapeDtypeStruct((owners, per * (length // 2) + CODE_ROWS, cells_y), jnp.int16),
        compiler_params=params(0, 12),
        name="solve",
    )(curve_z, slab, dht, plane_curve)


def field_kernel(
    pitch,
    turn_pitch,
    got_ref,
    psi_ref,
    kin_ref,
    dht_ref,
    tz_ref,
    back_ref,
    rim_ref,
    slab_ref,
    sums_ref,
    waves,
    turn,
    head,
    values,
):
    step = pl.program_id(0)
    orbitals, some_x, length, cells_y = psi_ref.shape
    owners = got_ref.shape[0]
    per = length // owners
    cells_x = some_x * pl.num_programs(0)
    rim = rim_ref.shape[2] // 2
    first = pl.multiple_of((lax.axis_index("orb") * per) // 8 * 8, 8)

    @pl.when(step == 0)
    def _():
        def unpack(source, carry):
            found, _ = unpacked(got_ref, source, per * cells_x)
            for k in range(per):
                at = pl.ds(pl.multiple_of((source * per + k) * pitch, 8), cells_x)
                waves[at, :] = found[k * cells_x : (k + 1) * cells_x]
            return carry

        lax.fori_loop(0, owners, unpack, 0, unroll=4)
        sums_ref[...] = kin_ref[...]

    group = 8
    energy = [jnp.zeros((8, cells_y), F32) for _ in range(orbitals)]
    for local in range(0, some_x, group):
        x = step * some_x + local
        field = hartley_pair(
            dht_ref[...],
            jnp.concatenate(
                [waves[pl.ds(x + k, length, stride=pitch), :] for k in range(group)], axis=1
            ),
        )
        values[local // group] = field
        own = values[local // group, pl.ds(first, 8), :]
        for k in range(group):
            slab_ref[local + k] = own[:, k * cells_y : (k + 1) * cells_y]
        products = []
        for o in range(orbitals):
            psi = jnp.concatenate([psi_ref[o, local + k] for k in range(group)], axis=1)
            psi = psi.astype(F32)
            product = field * psi
            products.append(product.astype(BF16))
            squares = product * psi
            for k in range(group):
                part = squares[:, k * cells_y : (k + 1) * cells_y]
                part = part.reshape(length // 8, 8, cells_y)
                energy[o] = energy[o] + jnp.sum(part, axis=0)
        back = dot(tz_ref[...], jnp.concatenate(products, axis=1))
        for o in range(orbitals):
            for k in range(group):
                at = (o * group + k) * cells_y
                row = o * length * turn_pitch + local + k
                turn[pl.ds(row, length, stride=turn_pitch), :] = back[:, at : at + cells_y]

    for o in range(orbitals):
        sums_ref[o, 0:8] = sums_ref[o, 0:8] + energy[o]

    def turned(o, z, start, count):
        row = pl.multiple_of((o * length + z) * turn_pitch, 8) + start
        return turn[pl.ds(row, count), :]

    def rows(z, carry):
        for o in range(orbitals):
            back_ref[o, z] = turned(o, z, 0, some_x).astype(BF16)
        return carry

    lax.fori_loop(0, length, rows, 0, unroll=8)

    @pl.when(step == 0)
    def _():
        def keep(z, carry):
            for o in range(orbitals):
                head[o, z] = turned(o, z, 0, rim)
            return carry

        lax.fori_loop(0, length, keep, 0, unroll=8)

    @pl.when(step == pl.num_programs(0) - 1)
    def _():
        def send(z, carry):
            for o in range(orbitals):
                both = jnp.concatenate([turned(o, z, some_x - rim, rim), head[o, z]], axis=0)
                rim_ref[o, z] = both.astype(BF16)
            return carry

        lax.fori_loop(0, length, send, 0, unroll=8)


def field(got, psi, kin_sums, dht, tz):
    orbitals, cells_x, length, cells_y = psi.shape
    some_x = 16
    pitch = cells_x + 8
    turn_pitch = some_x + 8
    rim = 8
    return pl.pallas_call(
        functools.partial(field_kernel, pitch, turn_pitch),
        grid=(cells_x // some_x,),
        in_specs=[
            pl.BlockSpec(memory_space=pltpu.VMEM),
            pl.BlockSpec((orbitals, some_x, length, cells_y), lambda i: (0, i, 0, 0)),
            whole(kin_sums),
            whole(dht),
            whole(tz),
        ],
        out_specs=[
            pl.BlockSpec((orbitals, length, some_x, cells_y), lambda i: (0, 0, i, 0)),
            pl.BlockSpec((orbitals, length, 2 * rim, cells_y), lambda i: (0, 0, 0, 0)),
            pl.BlockSpec((some_x, 8, cells_y), lambda i: (i, 0, 0)),
            whole(kin_sums),
        ],
        out_shape=[
            pltpu.HBM((orbitals, length, cells_x, cells_y), BF16),
            jax.ShapeDtypeStruct((orbitals, length, 2 * rim, cells_y), BF16),
            jax.ShapeDtypeStruct((cells_x, 8, cells_y), F32),
            jax.ShapeDtypeStruct(kin_sums.shape, F32),
        ],
        scratch_shapes=[
            pltpu.VMEM((length * pitch, cells_y), F32),
            pltpu.VMEM((orbitals * length * turn_pitch, cells_y), F32),
            pltpu.VMEM((orbitals, length, rim, cells_y), F32),
            pltpu.VMEM((2, length, 8 * cells_y), F32),
        ],
        compiler_params=params(1, 26),
        name="field",
    )(got, psi, kin_sums, dht, tz)


def update_kernel(
    sums_ref,
    other_ref,
    back_ref,
    rim_ref,
    c_ref,
    kin_ref,
    step_ref,
    tx_ref,
    ty_ref,
    out_ref,
    energy_ref,
):
    orbital = pl.program_id(0)

    @pl.when(pl.program_id(1) == 0)
    def _():
        both = sums_ref[orbital] + other_ref[orbital]
        energy_ref[orbital] = jnp.sum(both[0:8]) / jnp.sum(both[8:16])

    energy = energy_ref[orbital]
    some_z, cells_x, cells_y = back_ref.shape[1], back_ref.shape[2], back_ref.shape[3]
    tx = tx_ref[...]
    ty = ty_ref[...]
    block = 16
    many = 8

    def planes(i, carry):
        z0 = i * block
        crossed = []
        for p in range(0, block, many):
            some = range(p, p + many)
            flat = jnp.concatenate(
                [
                    jnp.concatenate([back_ref[0, z0 + k] for k in some], axis=1),
                    jnp.concatenate([rim_ref[0, z0 + k] for k in some], axis=1),
                ],
                axis=0,
            )
            both = dot(tx, flat).astype(BF16)
            crossed += [both[:, k * cells_y : (k + 1) * cells_y] for k in range(many)]
        potential = dot(jnp.concatenate(crossed, axis=0), ty)
        steps = step_ref[0, pl.ds(pl.multiple_of(z0, block), block), :]
        for p in range(block):
            z = z0 + p
            kin = kin_ref[0, z].astype(jnp.int32).astype(F32) * steps[p : p + 1]
            applied = potential[p * cells_x : (p + 1) * cells_x] + kin
            coeff = c_ref[0, z].astype(F32)
            out_ref[0, z] = (coeff - STEP_SIZE * (applied - energy * coeff)).astype(BF16)
        return carry

    lax.fori_loop(0, some_z // block, planes, 0, unroll=4)


def update(sums, other_sums, back, rim, c, kin, steps, tx, ty):
    orbitals, length, cells_x, cells_y = c.shape
    chunks = 2
    part = length // chunks
    block = pl.BlockSpec((1, part, cells_x, cells_y), lambda o, j: (o, j, 0, 0))
    return pl.pallas_call(
        update_kernel,
        grid=(orbitals, chunks),
        in_specs=[
            whole(sums),
            whole(other_sums),
            block,
            pl.BlockSpec((1, part, rim.shape[2], cells_y), lambda o, j: (o, j, 0, 0)),
            block,
            block,
            pl.BlockSpec((1, part, cells_y), lambda o, j: (o, j, 0)),
            whole(tx),
            whole(ty),
        ],
        out_specs=[block, pl.BlockSpec(memory_space=pltpu.SMEM)],
        out_shape=[
            jax.ShapeDtypeStruct(c.shape, BF16),
            jax.ShapeDtypeStruct((orbitals,), F32),
        ],
        compiler_params=params(2, 12),
        name="update",
    )(sums, other_sums, back, rim, c, kin, steps, tx, ty)


def to_other(array):
    return lax.ppermute(array, "grid", [(0, 1), (1, 0)])


def in_hbm(array):
    return pltpu.with_memory_space_constraint(array, pltpu.HBM)


def to_all(blocks):
    return lax.all_to_all(blocks, "orb", split_axis=0, concat_axis=0, tiled=True)


def on_device(coefficients, occupations, slot_orbital):
    orbitals, length, cells_x, cells_y = coefficients.shape
    owners = slot_orbital.shape[0] // orbitals
    per = length // owners
    magic, trans, kin_taps = magic_pairs(), transposed_pairs(), kinetic_pairs()
    magic_line = band_periodic(length, magic)
    trans_line = band_periodic(length, trans)
    kin_line = band_periodic(length, kin_taps, -0.5)
    inside = list(range(cells_x))
    near_cells = inside + with_rims(cells_x, 0, 8)
    all_cells = near_cells + with_rims(cells_x, 8, 16)
    dht = hartley(length)
    table = jnp.asarray(split_table(dht))
    waves = curve(length)

    c = in_hbm(coefficients)
    own_near, mark = own_rims(c, 0, 8)
    near = to_other(own_near)
    far = to_other(own_rims(c, 8, 16, mark)[0])
    psi, coded, peak = density(
        occupations,
        slot_orbital,
        coefficients,
        near,
        jnp.asarray(magic_line.T),
        jnp.asarray(band_columns(cells_x, near_cells, magic)),
        jnp.asarray(magic_line),
        table,
        owners,
    )
    got = to_all(coded)
    kin, steps, kin_sums = kinetic(
        c,
        near,
        far,
        jnp.asarray(kin_line.T),
        jnp.asarray(band_columns(cells_x, all_cells, kin_taps, -0.5)),
        jnp.asarray(kin_line),
        peak,
    )
    half = slab_sum(got, per * cells_x, per, kin_sums).reshape(per, cells_x, cells_y)
    slab = lax.all_gather(half, "grid", axis=1, tiled=True)
    spread = solve(
        jnp.asarray(waves.astype(np.float32)),
        slab,
        jnp.asarray(dht),
        jnp.asarray((waves[:, None] + waves[None, :]).astype(np.float32)),
        owners,
    )
    back, back_rims, slab_field, sums = field(
        to_all(spread), psi, kin_sums, table, jnp.asarray(trans_line)
    )
    updated, energies = update(
        sums,
        to_other(sums),
        in_hbm(back),
        to_other(back_rims),
        c,
        in_hbm(kin),
        steps,
        jnp.asarray(band_columns(cells_x, near_cells, trans)),
        jnp.asarray(trans_line.T),
    )
    first = lax.rem(lax.axis_index("orb") * per, 8)
    potential = lax.dynamic_slice_in_dim(slab_field, first, per, 1).transpose(1, 0, 2)
    return (updated, energies, potential)


def solution(mesh):
    return jax.shard_map(
        on_device,
        mesh=mesh,
        in_specs=(P("orb", None, "grid", None), P(), P()),
        out_specs=(P("orb", None, "grid", None), P("orb"), P("orb", "grid", None)),
        check_vma=False,
    )
```

```python
import functools
import math

import jax
import jax.numpy as jnp
import ml_dtypes
import numpy as np
from jax import lax
from jax.experimental import pallas as pl
from jax.experimental.pallas import tpu as pltpu
from jax.sharding import PartitionSpec as P

MAGIC = (
    8.433424733352934e-07,
    -1.290557201342061e-05,
    8.76298447621056e-05,
    -0.00030158038132690465,
    0.001747237136729939,
    -0.009420470302010804,
    0.023738214637249424,
    0.0612625895831208,
    0.9940415697834004,
    -0.06048952891969835,
    -0.021030251609303816,
    0.013372634148547948,
    -0.0034412814449349387,
    0.0004944322768868992,
    -5.185986881173433e-05,
    2.7273449291197967e-06,
)
STEP_SIZE = 0.1
COULOMB = 4.0 * math.pi
LEVELS = 32000.0
CODE_ROWS = 8
FINE = 16384.0
F32 = jnp.float32
BF16 = jnp.bfloat16
HIGHEST = lax.Precision.HIGHEST
MIB = 1024 * 1024


def magic_pairs():
    return [(position - 8, MAGIC[position]) for position in range(16)]


def transposed_pairs():
    return [(8 - position, MAGIC[position]) for position in range(16)]


def kinetic_pairs():
    spread = 14
    weights = []
    for distance in range(1, spread + 1):
        numerator = 2.0 * (-1.0) ** (distance + 1) * math.factorial(spread) ** 2
        weights.append(
            numerator
            / (
                distance
                * distance
                * math.factorial(spread - distance)
                * math.factorial(spread + distance)
            )
        )
    result = [(0, -2.0 * sum(weights))]
    for distance in range(1, spread + 1):
        result.append((distance, weights[distance - 1]))
        result.append((-distance, weights[distance - 1]))
    return result


def rounded(weight):
    return np.float32(np.float32(weight).astype(ml_dtypes.bfloat16))


def band_periodic(length, pairs, scale=1.0):
    matrix = np.zeros((length, length), np.float32)
    for offset, weight in pairs:
        for i in range(length):
            matrix[i, (i + offset) % length] += scale * rounded(weight)
    return matrix.astype(ml_dtypes.bfloat16)


def band_columns(length, columns, pairs, scale=1.0):
    matrix = np.zeros((length, len(columns)), np.float32)
    place = {cell: k for k, cell in enumerate(columns)}
    for offset, weight in pairs:
        for i in range(length):
            matrix[i, place[i + offset]] += scale * rounded(weight)
    return matrix.astype(ml_dtypes.bfloat16)


def with_rims(length, inner, outer):
    return [*range(-outer, -inner), *range(length + inner, length + outer)]


def hartley(length):
    index = np.arange(length)
    angle = 2.0 * np.pi * ((index[:, None] * index[None, :]) % length) / length
    return ((np.cos(angle) + np.sin(angle)) / math.sqrt(length)).astype(np.float32)


def split_table(table):
    high = table.astype(ml_dtypes.bfloat16)
    low = (table - high.astype(np.float32)).astype(ml_dtypes.bfloat16)
    return np.concatenate([high, low, high], axis=1)


def curve(length):
    return 2.0 - 2.0 * np.cos(2.0 * np.pi * np.arange(length) / length)


def dot(a, b):
    return jnp.dot(a, b, preferred_element_type=F32)


def dot_exact(a, b):
    return jnp.dot(a, b, preferred_element_type=F32, precision=HIGHEST)


def params(count, mebibytes):
    return pltpu.CompilerParams(
        dimension_semantics=("arbitrary",) * count, vmem_limit_bytes=mebibytes * MIB
    )


def cost(cells, bytes_each):
    return pl.CostEstimate(
        flops=cells * 256, bytes_accessed=cells * bytes_each, transcendentals=0
    )


def whole(array):
    zeros = (0,) * array.ndim
    return pl.BlockSpec(array.shape, lambda *_: zeros)


def scale_of(largest):
    largest = jnp.maximum(largest, 1e-30)
    code = jnp.ceil(jnp.log2(largest))
    power = jnp.exp2(code)
    units = jnp.ceil(largest / power * FINE) + 1.0
    return code, units, units * (1.0 / FINE) * power


def coded_rows(cells_y, codes):
    row = lax.broadcasted_iota(jnp.int32, (CODE_ROWS, cells_y), 0)
    values = jnp.zeros((CODE_ROWS, cells_y), F32)
    for k, code in enumerate(codes):
        values = jnp.where(row == k, code, values)
    return values.astype(jnp.int32).astype(jnp.int16)


def side_by_side(first, second):
    return jnp.concatenate([first, second], axis=1)


def hartley_pair(table, pair):
    high = pair.astype(BF16)
    low = (pair - high.astype(F32)).astype(BF16)
    return dot(table, jnp.concatenate([high, high, low], axis=0))


def rims_kernel(inner, outer, low_ref, high_ref, *rest):
    out_ref, mark_ref = rest[-2:]
    tile = low_ref.shape[2]
    low = low_ref[...].astype(F32)[:, :, tile - outer : tile - inner]
    high = high_ref[...].astype(F32)[:, :, inner:outer]
    out_ref[...] = jnp.concatenate([low, high], axis=2).astype(BF16)
    mark_ref[...] = jnp.zeros_like(mark_ref)


def own_rims(c, inner, outer, *after):
    orbitals, length, cells_x, cells_y = c.shape
    tile = 16

    def at(k):
        return pl.BlockSpec((orbitals, length, tile, cells_y), lambda o: (0, 0, k, 0))

    return pl.pallas_call(
        functools.partial(rims_kernel, inner, outer),
        grid=(1,),
        in_specs=[at(cells_x // tile - 1), at(0)]
        + [pl.BlockSpec(memory_space=pl.ANY) for _ in after],
        out_specs=[at(0), pl.BlockSpec((8, cells_y), lambda o: (0, 0))],
        out_shape=[
            jax.ShapeDtypeStruct((orbitals, length, 2 * (outer - inner), cells_y), BF16),
            jax.ShapeDtypeStruct((8, cells_y), F32),
        ],
        compiler_params=params(1, 16),
        name="own_rims",
    )(c, c, *after)


def density_kernel(
    first_steps,
    pitch,
    occ_ref,
    slot_ref,
    c_ref,
    h_ref,
    my_ref,
    ax_ref,
    mz_ref,
    dht_ref,
    psi_ref,
    q_ref,
    peak,
    mid,
    waves,
    level,
):
    step = pl.program_id(0)
    cells_x, cells_y = c_ref.shape[2], c_ref.shape[3]
    cells_z = c_ref.shape[0] * c_ref.shape[1] // first_steps
    rim = h_ref.shape[2]
    orbitals, some_x, length = psi_ref.shape[0], psi_ref.shape[1], psi_ref.shape[2]
    block = 128
    many = 8
    group = 16

    @pl.when(step < first_steps)
    def _():
        my = my_ref[...]
        ax = ax_ref[...]

        def planes(i, carry):
            z0 = i * block
            own = dot(c_ref[step, pl.ds(z0, block)].reshape(block * cells_x, cells_y), my)
            own = own.astype(BF16).reshape(block, cells_x, cells_y)
            far = dot(h_ref[step, pl.ds(z0, block)].reshape(block * rim, cells_y), my)
            far = far.astype(BF16).reshape(block, rim, cells_y)
            for p in range(0, block, many):
                some = range(p, p + many)
                flat = jnp.concatenate(
                    [
                        jnp.concatenate([own[z] for z in some], axis=1),
                        jnp.concatenate([far[z] for z in some], axis=1),
                    ],
                    axis=0,
                )
                crossed = dot(ax, flat)
                for k in range(many):
                    row = pl.multiple_of((step * cells_z + z0 + p + k) * pitch, 8)
                    mid[pl.ds(row, cells_x), :] = crossed[:, k * cells_y : (k + 1) * cells_y]
            return carry

        lax.fori_loop(0, cells_z // block, planes, 0)

    def grid_values(x, count):
        first = lax.axis_index("orb") * orbitals
        columns = [
            mid[pl.ds(o * length * pitch + x + k, length, stride=pitch), :].astype(BF16)
            for o in range(orbitals)
            for k in range(count)
        ]
        values = dot(mz_ref[...], jnp.concatenate(columns, axis=1)).astype(BF16)
        total = None
        for o in range(orbitals):
            weight = occ_ref[slot_ref[first + o]].astype(F32) / slot_ref.shape[0]
            wide = values[:, o * count * cells_y : (o + 1) * count * cells_y].astype(F32)
            part = weight * (wide * wide)
            total = part if total is None else total + part
        return values, total

    @pl.when(step == first_steps)
    def _():
        _, total = grid_values(0, 2)
        code, fine, top = scale_of(jnp.sum(total) / total.size)
        level[0] = code
        level[1] = fine
        level[2] = top
        peak[...] = jnp.zeros_like(peak)

    @pl.when(step >= first_steps)
    def _():
        x0 = (step - first_steps) * some_x
        mean = level[2]
        table = dht_ref[...]
        largest = peak[...]
        for local in range(0, some_x, group):
            values, total = grid_values(x0 + local, group)
            for o in range(orbitals):
                for k in range(group):
                    at = (o * group + k) * cells_y
                    psi_ref[o, local + k] = values[:, at : at + cells_y]
            result = hartley_pair(table, total - mean)
            for k in range(group):
                part = result[:, k * cells_y : (k + 1) * cells_y]
                waves[pl.ds(x0 + local + k, length, stride=pitch), :] = part
                size = jnp.abs(part).reshape(length // 8, 8, cells_y)
                largest = jnp.maximum(largest, jnp.max(size, axis=0))
        peak[...] = largest

    @pl.when(step == pl.num_programs(0) - 1)
    def _():
        code, fine, top = scale_of(jnp.max(peak[...]))
        factor = LEVELS / top
        code_rows = coded_rows(cells_y, (code, fine, level[0], level[1], LEVELS))
        per = length // q_ref.shape[0]
        rows = per * cells_x

        def quantise(i, carry):
            for k in range(per):
                row = pl.multiple_of((i * per + k) * pitch, 8)
                values = jnp.round(waves[pl.ds(row, cells_x), :] * factor)
                at = pl.ds(k * cells_x, cells_x)
                q_ref[i, at, :] = values.astype(jnp.int32).astype(jnp.int16)
            q_ref[i, rows : rows + CODE_ROWS, :] = code_rows
            return carry

        lax.fori_loop(0, q_ref.shape[0], quantise, 0, unroll=16)


def density(occupations, slot_orbital, c, halo, my, ax, mz, dht, owners):
    orbitals, length, cells_x, cells_y = c.shape
    first_steps = orbitals
    some_x = 16
    pitch = cells_x + 8
    smem = pl.BlockSpec(memory_space=pltpu.SMEM)
    rows = (length // owners) * cells_x + CODE_ROWS

    return pl.pallas_call(
        functools.partial(density_kernel, first_steps, pitch),
        grid=(first_steps + cells_x // some_x,),
        in_specs=[
            smem,
            smem,
            pl.BlockSpec(memory_space=pltpu.VMEM),
            pl.BlockSpec(memory_space=pltpu.VMEM),
            whole(my),
            whole(ax),
            whole(mz),
            whole(dht),
        ],
        out_specs=[
            pl.BlockSpec(
                (orbitals, some_x, length, cells_y),
                lambda s: (0, jnp.maximum(s - first_steps, 0), 0, 0),
            ),
            pl.BlockSpec((owners, rows, cells_y), lambda s: (0, 0, 0)),
            pl.BlockSpec((8, cells_y), lambda s: (0, 0)),
        ],
        out_shape=[
            pltpu.HBM((orbitals, cells_x, length, cells_y), BF16),
            pltpu.HBM((owners, rows, cells_y), jnp.int16),
            jax.ShapeDtypeStruct((8, cells_y), F32),
        ],
        scratch_shapes=[
            pltpu.VMEM(((orbitals * length + 1) * pitch, cells_y), F32),
            pltpu.VMEM(((length + 1) * pitch, cells_y), F32),
            pltpu.SMEM((3,), F32),
        ],
        compiler_params=params(1, 36),
        name="density",
    )(occupations, slot_orbital, c, halo, my, ax, mz, dht)


def kinetic_kernel(
    pitch, c_ref, near_ref, far_ref, dy_ref, dx_ref, dz_ref, after_ref, kin_ref, step_ref, sums_ref, wide, acc
):
    length, cells_x, cells_y = c_ref.shape[1], c_ref.shape[2], c_ref.shape[3]
    block = 8

    def widen(z, carry):
        row = pl.multiple_of(z * pitch, 8)
        wide[pl.ds(row, cells_x), :] = c_ref[0, z].astype(F32)
        return carry

    lax.fori_loop(0, length, widen, 0, unroll=8)

    def columns(i, carry):
        x = 2 * i
        pair = side_by_side(
            wide[pl.ds(x, length, stride=pitch), :].astype(BF16),
            wide[pl.ds(x + 1, length, stride=pitch), :].astype(BF16),
        )
        values = dot(dz_ref[...], pair)
        acc[pl.ds(x, length, stride=pitch), :] = values[:, :cells_y]
        acc[pl.ds(x + 1, length, stride=pitch), :] = values[:, cells_y:]
        return carry

    lax.fori_loop(0, cells_x // 2, columns, 0, unroll=4)

    def planes(i, carry):
        energy, norm = carry
        z0 = i * block
        own = c_ref[0, pl.ds(z0, block)]
        along_y = dot(own.reshape(block * cells_x, cells_y), dy_ref[...])
        steps = []
        for p in range(0, block, 2):
            z = z0 + p
            pair = jnp.concatenate(
                [
                    side_by_side(c_ref[0, z], c_ref[0, z + 1]),
                    side_by_side(near_ref[0, z], near_ref[0, z + 1]),
                    side_by_side(far_ref[0, z], far_ref[0, z + 1]),
                ],
                axis=0,
            )
            along_x = dot(dx_ref[...], pair)
            for k in range(2):
                at = pl.ds(pl.multiple_of((z + k) * pitch, 8), cells_x)
                value = (
                    acc[at, :]
                    + along_x[:, k * cells_y : (k + 1) * cells_y]
                    + along_y[(p + k) * cells_x : (p + k + 1) * cells_x]
                )
                tiles = (cells_x // 8, 8, cells_y)
                largest = jnp.max(jnp.max(jnp.abs(value).reshape(tiles), axis=0), axis=0)
                largest = jnp.maximum(largest, 1e-30).reshape(1, cells_y)
                coded = jnp.round(value * (LEVELS / largest))
                kin_ref[0, z + k] = coded.astype(jnp.int32).astype(jnp.int16)
                steps.append(largest * (1.0 / LEVELS))
                coeff = own[p + k].astype(F32)
                energy = energy + jnp.sum((coeff * value).reshape(tiles), axis=0)
                norm = norm + jnp.sum((coeff * coeff).reshape(tiles), axis=0)
        step_ref[0, pl.ds(pl.multiple_of(z0, block), block), :] = jnp.concatenate(steps, axis=0)
        return energy, norm

    zeros = jnp.zeros((8, cells_y), F32)
    energy, norm = lax.fori_loop(0, length // block, planes, (zeros, zeros), unroll=2)
    sums_ref[0, 0:8] = energy
    sums_ref[0, 8:16] = norm


def kinetic(c, near, far, dy, dx, dz, after):
    orbitals, length, cells_x, cells_y = c.shape
    cells = orbitals * length * cells_x * cells_y
    pitch = cells_x + 8

    def block(array):
        return pl.BlockSpec((1, *array.shape[1:]), lambda o: (o, 0, 0, 0))

    return pl.pallas_call(
        functools.partial(kinetic_kernel, pitch),
        grid=(orbitals,),
        in_specs=[
            block(c),
            block(near),
            block(far),
            whole(dy),
            whole(dx),
            whole(dz),
            pl.BlockSpec(memory_space=pl.ANY),
        ],
        out_specs=[
            block(c),
            pl.BlockSpec((1, length, cells_y), lambda o: (o, 0, 0)),
            pl.BlockSpec((1, 16, cells_y), lambda o: (o, 0, 0)),
        ],
        out_shape=[
            pltpu.HBM(c.shape, jnp.int16),
            jax.ShapeDtypeStruct((orbitals, length, cells_y), F32),
            jax.ShapeDtypeStruct((orbitals, 16, cells_y), F32),
        ],
        scratch_shapes=[
            pltpu.VMEM(((length + 1) * pitch, cells_y), F32),
            pltpu.VMEM(((length + 1) * pitch, cells_y), F32),
        ],
        compiler_params=params(1, 26),
        cost_estimate=pl.CostEstimate(
            flops=cells * 768 * 4, bytes_accessed=cells * 7, transcendentals=0
        ),
        name="kinetic",
    )(c, near, far, dy, dx, dz, after)


def unpacked(ref, source, rows):
    codes = ref[source, rows : rows + CODE_ROWS, :].astype(jnp.int32).astype(F32)
    powers = jnp.exp2(codes) * (1.0 / (LEVELS * FINE))
    step = codes[1:2] * powers[0:1]
    mean = codes[4:5] * (codes[3:4] * powers[2:3])
    return ref[source, 0:rows, :].astype(jnp.int32).astype(F32) * step, mean


def sum_kernel(per, got_ref, after_ref, out_ref):
    rows = out_ref.shape[0]
    cells_y = out_ref.shape[1]

    def body(source, carry):
        total, means = carry
        values, mean = unpacked(got_ref, source, rows)
        return total + values, means + mean

    total, means = lax.fori_loop(
        0,
        got_ref.shape[0],
        body,
        (jnp.zeros((rows, cells_y), F32), jnp.zeros((1, cells_y), F32)),
        unroll=2,
    )
    length = got_ref.shape[0] * per
    row = lax.broadcasted_iota(jnp.int32, (rows, cells_y), 0)
    flat = (lax.axis_index("orb") == 0) & (row < rows // per)
    out_ref[...] = total + jnp.where(flat, means * math.sqrt(length), 0.0)


def slab_sum(got, rows, per, after):
    return pl.pallas_call(
        functools.partial(sum_kernel, per),
        in_specs=[pl.BlockSpec(memory_space=pltpu.VMEM), pl.BlockSpec(memory_space=pl.ANY)],
        out_shape=jax.ShapeDtypeStruct((rows, got.shape[2]), F32),
        compiler_params=params(0, 12),
        name="slab_sum",
    )(got, after)


def solve_kernel(curve_z_ref, slab_ref, dht_ref, curve_ref, q_ref):
    per, length, cells_y = slab_ref.shape
    cells_x = length // 2
    orb = lax.axis_index("orb")
    corner = pl.multiple_of(lax.axis_index("grid") * cells_x, cells_x)
    dht = dht_ref[...]
    own = dht_ref[pl.ds(corner, cells_x), :]
    row = lax.broadcasted_iota(jnp.int32, (length, cells_y), 0)
    col = lax.broadcasted_iota(jnp.int32, (length, cells_y), 1)
    waves = dot_exact(jnp.concatenate([slab_ref[k] for k in range(per)], axis=0), dht)
    waves = jnp.concatenate(
        [waves[k * length : (k + 1) * length] for k in range(per)], axis=1
    )
    waves = dot_exact(dht, waves)
    parts = []
    for k in range(per):
        wave = orb * per + k
        anchor = (row == 0) & (col == 0) & (wave == 0)
        bent = curve_ref[...] + curve_z_ref[wave]
        factor = jnp.where(anchor, 0.0, COULOMB / jnp.where(anchor, 1.0, bent))
        parts.append(waves[:, k * cells_y : (k + 1) * cells_y] * factor)
    field = dot_exact(own, jnp.concatenate(parts, axis=1))
    field = jnp.concatenate(
        [field[:, k * cells_y : (k + 1) * cells_y] for k in range(per)], axis=0
    )
    field = dot_exact(field, dht)
    code, fine, top = scale_of(jnp.max(jnp.abs(field)))
    coded = jnp.round(field * (LEVELS / top)).astype(jnp.int32).astype(jnp.int16)
    code_rows = coded_rows(cells_y, (code, fine))
    rows = per * cells_x

    def spread(i, carry):
        q_ref[i, 0:rows, :] = coded
        q_ref[i, rows : rows + CODE_ROWS, :] = code_rows
        return carry

    lax.fori_loop(0, q_ref.shape[0], spread, 0, unroll=4)


def solve(curve_z, slab, dht, plane_curve, owners):
    per, length, cells_y = slab.shape
    vmem = pl.BlockSpec(memory_space=pltpu.VMEM)
    return pl.pallas_call(
        solve_kernel,
        in_specs=[pl.BlockSpec(memory_space=pltpu.SMEM), vmem, vmem, vmem],
        out_shape=jax.ShapeDtypeStruct((owners, per * (length // 2) + CODE_ROWS, cells_y), jnp.int16),
        compiler_params=params(0, 12),
        name="solve",
    )(curve_z, slab, dht, plane_curve)


def field_kernel(
    pitch,
    turn_pitch,
    got_ref,
    psi_ref,
    kin_ref,
    dht_ref,
    tz_ref,
    back_ref,
    rim_ref,
    slab_ref,
    sums_ref,
    waves,
    turn,
    head,
    values,
):
    step = pl.program_id(0)
    orbitals, cells_x, length, cells_y = psi_ref.shape
    some_x = cells_x // pl.num_programs(0)
    owners = got_ref.shape[0]
    per = length // owners
    rim = rim_ref.shape[2] // 2
    first = pl.multiple_of((lax.axis_index("orb") * per) // 8 * 8, 8)

    @pl.when(step == 0)
    def _():
        def unpack(source, carry):
            found, _ = unpacked(got_ref, source, per * cells_x)
            for k in range(per):
                at = pl.ds(pl.multiple_of((source * per + k) * pitch, 8), cells_x)
                waves[at, :] = found[k * cells_x : (k + 1) * cells_x]
            return carry

        lax.fori_loop(0, owners, unpack, 0, unroll=16)
        sums_ref[...] = kin_ref[...]

    group = 16
    energy = [jnp.zeros((8, cells_y), F32) for _ in range(orbitals)]
    for local in range(0, some_x, group):
        x = step * some_x + local
        field = hartley_pair(
            dht_ref[...],
            jnp.concatenate(
                [waves[pl.ds(x + k, length, stride=pitch), :] for k in range(group)], axis=1
            ),
        )
        values[local // group] = field
        own = values[local // group, pl.ds(first, 8), :]
        for k in range(group):
            slab_ref[local + k] = own[:, k * cells_y : (k + 1) * cells_y]
        products = []
        for o in range(orbitals):
            psi = jnp.concatenate([psi_ref[o, x + k] for k in range(group)], axis=1)
            psi = psi.astype(F32)
            product = field * psi
            products.append(product.astype(BF16))
            squares = product * psi
            for k in range(group):
                part = squares[:, k * cells_y : (k + 1) * cells_y]
                part = part.reshape(length // 8, 8, cells_y)
                energy[o] = energy[o] + jnp.sum(part, axis=0)
        back = dot(tz_ref[...], jnp.concatenate(products, axis=1))
        for o in range(orbitals):
            for k in range(group):
                at = (o * group + k) * cells_y
                row = o * length * turn_pitch + local + k
                turn[pl.ds(row, length, stride=turn_pitch), :] = back[:, at : at + cells_y]

    for o in range(orbitals):
        sums_ref[o, 0:8] = sums_ref[o, 0:8] + energy[o]

    def turned(o, z, start, count):
        row = pl.multiple_of((o * length + z) * turn_pitch, 8) + start
        return turn[pl.ds(row, count), :]

    def rows(z, carry):
        for o in range(orbitals):
            back_ref[o, z] = turned(o, z, 0, some_x).astype(BF16)
        return carry

    lax.fori_loop(0, length, rows, 0, unroll=16)

    @pl.when(step == 0)
    def _():
        def keep(z, carry):
            for o in range(orbitals):
                head[o, z] = turned(o, z, 0, rim)
            return carry

        lax.fori_loop(0, length, keep, 0, unroll=16)

    @pl.when(step == pl.num_programs(0) - 1)
    def _():
        def send(z, carry):
            for o in range(orbitals):
                both = jnp.concatenate([turned(o, z, some_x - rim, rim), head[o, z]], axis=0)
                rim_ref[o, z] = both.astype(BF16)
            return carry

        lax.fori_loop(0, length, send, 0, unroll=16)


def field(got, psi, kin_sums, dht, tz):
    orbitals, cells_x, length, cells_y = psi.shape
    some_x = 16
    pitch = cells_x + 8
    turn_pitch = some_x + 8
    rim = 8
    return pl.pallas_call(
        functools.partial(field_kernel, pitch, turn_pitch),
        grid=(cells_x // some_x,),
        in_specs=[
            pl.BlockSpec(memory_space=pltpu.VMEM),
            pl.BlockSpec(memory_space=pltpu.VMEM),
            whole(kin_sums),
            whole(dht),
            whole(tz),
        ],
        out_specs=[
            pl.BlockSpec((orbitals, length, some_x, cells_y), lambda i: (0, 0, i, 0)),
            pl.BlockSpec((orbitals, length, 2 * rim, cells_y), lambda i: (0, 0, 0, 0)),
            pl.BlockSpec((some_x, 8, cells_y), lambda i: (i, 0, 0)),
            whole(kin_sums),
        ],
        out_shape=[
            pltpu.HBM((orbitals, length, cells_x, cells_y), BF16),
            jax.ShapeDtypeStruct((orbitals, length, 2 * rim, cells_y), BF16),
            jax.ShapeDtypeStruct((cells_x, 8, cells_y), F32),
            jax.ShapeDtypeStruct(kin_sums.shape, F32),
        ],
        scratch_shapes=[
            pltpu.VMEM(((length + 1) * pitch, cells_y), F32),
            pltpu.VMEM(((orbitals * length + 1) * turn_pitch, cells_y), F32),
            pltpu.VMEM((orbitals, length, rim, cells_y), F32),
            pltpu.VMEM((1, length, 16 * cells_y), F32),
        ],
        compiler_params=params(1, 30),
        name="field",
    )(got, psi, kin_sums, dht, tz)


def update_kernel(
    sums_ref,
    other_ref,
    back_ref,
    rim_ref,
    c_ref,
    kin_ref,
    step_ref,
    tx_ref,
    ty_ref,
    out_ref,
    energy_ref,
):
    orbital = pl.program_id(0)

    @pl.when(pl.program_id(1) == 0)
    def _():
        both = sums_ref[orbital] + other_ref[orbital]
        energy_ref[orbital] = jnp.sum(both[0:8]) / jnp.sum(both[8:16])

    energy = energy_ref[orbital]
    some_z, cells_x, cells_y = back_ref.shape[1], back_ref.shape[2], back_ref.shape[3]
    tx = tx_ref[...]
    ty = ty_ref[...]
    block = 16
    many = 8

    def planes(i, carry):
        z0 = i * block
        crossed = []
        for p in range(0, block, many):
            some = range(p, p + many)
            flat = jnp.concatenate(
                [
                    jnp.concatenate([back_ref[0, z0 + k] for k in some], axis=1),
                    jnp.concatenate([rim_ref[0, z0 + k] for k in some], axis=1),
                ],
                axis=0,
            )
            both = dot(tx, flat).astype(BF16)
            crossed += [both[:, k * cells_y : (k + 1) * cells_y] for k in range(many)]
        potential = dot(jnp.concatenate(crossed, axis=0), ty)
        steps = step_ref[0, pl.ds(pl.multiple_of(z0, block), block), :]
        for p in range(block):
            z = z0 + p
            kin = kin_ref[0, z].astype(jnp.int32).astype(F32) * steps[p : p + 1]
            applied = potential[p * cells_x : (p + 1) * cells_x] + kin
            coeff = c_ref[0, z].astype(F32)
            out_ref[0, z] = (coeff - STEP_SIZE * (applied - energy * coeff)).astype(BF16)
        return carry

    lax.fori_loop(0, some_z // block, planes, 0, unroll=4)


def update(sums, other_sums, back, rim, c, kin, steps, tx, ty):
    orbitals, length, cells_x, cells_y = c.shape
    chunks = 2
    part = length // chunks
    block = pl.BlockSpec((1, part, cells_x, cells_y), lambda o, j: (o, j, 0, 0))
    return pl.pallas_call(
        update_kernel,
        grid=(orbitals, chunks),
        in_specs=[
            whole(sums),
            whole(other_sums),
            block,
            pl.BlockSpec((1, part, rim.shape[2], cells_y), lambda o, j: (o, j, 0, 0)),
            block,
            block,
            pl.BlockSpec((1, part, cells_y), lambda o, j: (o, j, 0)),
            whole(tx),
            whole(ty),
        ],
        out_specs=[block, pl.BlockSpec(memory_space=pltpu.SMEM)],
        out_shape=[
            jax.ShapeDtypeStruct(c.shape, BF16),
            jax.ShapeDtypeStruct((orbitals,), F32),
        ],
        compiler_params=params(2, 12),
        name="update",
    )(sums, other_sums, back, rim, c, kin, steps, tx, ty)


def to_other(array):
    return lax.ppermute(array, "grid", [(0, 1), (1, 0)])


def in_hbm(array):
    return pltpu.with_memory_space_constraint(array, pltpu.HBM)


def to_all(blocks):
    return lax.all_to_all(blocks, "orb", split_axis=0, concat_axis=0, tiled=True)


def on_device(coefficients, occupations, slot_orbital):
    orbitals, length, cells_x, cells_y = coefficients.shape
    owners = slot_orbital.shape[0] // orbitals
    per = length // owners
    magic, trans, kin_taps = magic_pairs(), transposed_pairs(), kinetic_pairs()
    magic_line = band_periodic(length, magic)
    trans_line = band_periodic(length, trans)
    kin_line = band_periodic(length, kin_taps, -0.5)
    inside = list(range(cells_x))
    near_cells = inside + with_rims(cells_x, 0, 8)
    all_cells = near_cells + with_rims(cells_x, 8, 16)
    dht = hartley(length)
    table = jnp.asarray(split_table(dht))
    waves = curve(length)

    c = in_hbm(coefficients)
    own_near, mark = own_rims(c, 0, 8)
    near = to_other(own_near)
    far = to_other(own_rims(c, 8, 16, mark)[0])
    psi, coded, peak = density(
        occupations,
        slot_orbital,
        coefficients,
        near,
        jnp.asarray(magic_line.T),
        jnp.asarray(band_columns(cells_x, near_cells, magic)),
        jnp.asarray(magic_line),
        table,
        owners,
    )
    got = to_all(coded)
    kin, steps, kin_sums = kinetic(
        c,
        near,
        far,
        jnp.asarray(kin_line.T),
        jnp.asarray(band_columns(cells_x, all_cells, kin_taps, -0.5)),
        jnp.asarray(kin_line),
        peak,
    )
    half = slab_sum(got, per * cells_x, per, kin_sums).reshape(per, cells_x, cells_y)
    slab = lax.all_gather(half, "grid", axis=1, tiled=True)
    spread = solve(
        jnp.asarray(waves.astype(np.float32)),
        slab,
        jnp.asarray(dht),
        jnp.asarray((waves[:, None] + waves[None, :]).astype(np.float32)),
        owners,
    )
    back, back_rims, slab_field, sums = field(
        to_all(spread), psi, kin_sums, table, jnp.asarray(trans_line)
    )
    updated, energies = update(
        sums,
        to_other(sums),
        in_hbm(back),
        to_other(back_rims),
        c,
        in_hbm(kin),
        steps,
        jnp.asarray(band_columns(cells_x, near_cells, trans)),
        jnp.asarray(trans_line.T),
    )
    first = lax.rem(lax.axis_index("orb") * per, 8)
    potential = lax.dynamic_slice_in_dim(slab_field, first, per, 1).transpose(1, 0, 2)
    return (updated, energies, potential)


def solution(mesh):
    return jax.shard_map(
        on_device,
        mesh=mesh,
        in_specs=(P("orb", None, "grid", None), P(), P()),
        out_specs=(P("orb", None, "grid", None), P("orb"), P("orb", "grid", None)),
        check_vma=False,
    )
```

```python
import functools
import math

import jax
import jax.numpy as jnp
import ml_dtypes
import numpy as np
from jax import lax
from jax.experimental import pallas as pl
from jax.experimental.pallas import tpu as pltpu
from jax.sharding import PartitionSpec as P

MAGIC = (
    8.433424733352934e-07,
    -1.290557201342061e-05,
    8.76298447621056e-05,
    -0.00030158038132690465,
    0.001747237136729939,
    -0.009420470302010804,
    0.023738214637249424,
    0.0612625895831208,
    0.9940415697834004,
    -0.06048952891969835,
    -0.021030251609303816,
    0.013372634148547948,
    -0.0034412814449349387,
    0.0004944322768868992,
    -5.185986881173433e-05,
    2.7273449291197967e-06,
)
STEP_SIZE = 0.1
COULOMB = 4.0 * math.pi
LEVELS = 32000.0
CODE_ROWS = 8
FINE = 16384.0
F32 = jnp.float32
BF16 = jnp.bfloat16
HIGHEST = lax.Precision.HIGHEST
MIB = 1024 * 1024


def magic_pairs():
    return [(position - 8, MAGIC[position]) for position in range(16)]


def transposed_pairs():
    return [(8 - position, MAGIC[position]) for position in range(16)]


def kinetic_pairs():
    spread = 14
    weights = []
    for distance in range(1, spread + 1):
        numerator = 2.0 * (-1.0) ** (distance + 1) * math.factorial(spread) ** 2
        weights.append(
            numerator
            / (
                distance
                * distance
                * math.factorial(spread - distance)
                * math.factorial(spread + distance)
            )
        )
    result = [(0, -2.0 * sum(weights))]
    for distance in range(1, spread + 1):
        result.append((distance, weights[distance - 1]))
        result.append((-distance, weights[distance - 1]))
    return result


def rounded(weight):
    return np.float32(np.float32(weight).astype(ml_dtypes.bfloat16))


def band_periodic(length, pairs, scale=1.0):
    matrix = np.zeros((length, length), np.float32)
    for offset, weight in pairs:
        for i in range(length):
            matrix[i, (i + offset) % length] += scale * rounded(weight)
    return matrix.astype(ml_dtypes.bfloat16)


def band_columns(length, columns, pairs, scale=1.0):
    matrix = np.zeros((length, len(columns)), np.float32)
    place = {cell: k for k, cell in enumerate(columns)}
    for offset, weight in pairs:
        for i in range(length):
            matrix[i, place[i + offset]] += scale * rounded(weight)
    return matrix.astype(ml_dtypes.bfloat16)


def with_rims(length, inner, outer):
    return [*range(-outer, -inner), *range(length + inner, length + outer)]


def hartley(length):
    index = np.arange(length)
    angle = 2.0 * np.pi * ((index[:, None] * index[None, :]) % length) / length
    return ((np.cos(angle) + np.sin(angle)) / math.sqrt(length)).astype(np.float32)


def split_table(table):
    high = table.astype(ml_dtypes.bfloat16)
    low = (table - high.astype(np.float32)).astype(ml_dtypes.bfloat16)
    return np.concatenate([high, low, high], axis=1)


def curve(length):
    return 2.0 - 2.0 * np.cos(2.0 * np.pi * np.arange(length) / length)


def dot(a, b):
    return jnp.dot(a, b, preferred_element_type=F32)


def dot_exact(a, b):
    return jnp.dot(a, b, preferred_element_type=F32, precision=HIGHEST)


def params(count, mebibytes):
    return pltpu.CompilerParams(
        dimension_semantics=("arbitrary",) * count, vmem_limit_bytes=mebibytes * MIB
    )


def cost(cells, bytes_each):
    return pl.CostEstimate(
        flops=cells * 256, bytes_accessed=cells * bytes_each, transcendentals=0
    )


def whole(array):
    zeros = (0,) * array.ndim
    return pl.BlockSpec(array.shape, lambda *_: zeros)


def scale_of(largest):
    largest = jnp.maximum(largest, 1e-30)
    code = jnp.ceil(jnp.log2(largest))
    power = jnp.exp2(code)
    units = jnp.ceil(largest / power * FINE) + 1.0
    return code, units, units * (1.0 / FINE) * power


def coded_rows(cells_y, codes):
    row = lax.broadcasted_iota(jnp.int32, (CODE_ROWS, cells_y), 0)
    values = jnp.zeros((CODE_ROWS, cells_y), F32)
    for k, code in enumerate(codes):
        values = jnp.where(row == k, code, values)
    return values.astype(jnp.int32).astype(jnp.int16)


def side_by_side(first, second):
    return jnp.concatenate([first, second], axis=1)


def hartley_pair(table, pair):
    high = pair.astype(BF16)
    low = (pair - high.astype(F32)).astype(BF16)
    return dot(table, jnp.concatenate([high, high, low], axis=0))


def rims_kernel(inner, outer, low_ref, high_ref, *rest):
    out_ref, mark_ref = rest[-2:]
    tile = low_ref.shape[2]
    low = low_ref[...].astype(F32)[:, :, tile - outer : tile - inner]
    high = high_ref[...].astype(F32)[:, :, inner:outer]
    out_ref[...] = jnp.concatenate([low, high], axis=2).astype(BF16)
    mark_ref[...] = jnp.zeros_like(mark_ref)


def own_rims(c, inner, outer, *after):
    orbitals, length, cells_x, cells_y = c.shape
    tile = 16

    def at(k):
        return pl.BlockSpec((orbitals, length, tile, cells_y), lambda o: (0, 0, k, 0))

    return pl.pallas_call(
        functools.partial(rims_kernel, inner, outer),
        grid=(1,),
        in_specs=[at(cells_x // tile - 1), at(0)]
        + [pl.BlockSpec(memory_space=pl.ANY) for _ in after],
        out_specs=[at(0), pl.BlockSpec((8, cells_y), lambda o: (0, 0))],
        out_shape=[
            jax.ShapeDtypeStruct((orbitals, length, 2 * (outer - inner), cells_y), BF16),
            jax.ShapeDtypeStruct((8, cells_y), F32),
        ],
        compiler_params=params(1, 16),
        name="own_rims",
    )(c, c, *after)


def density_kernel(
    first_steps,
    pitch,
    occ_ref,
    slot_ref,
    c_ref,
    h_ref,
    my_ref,
    ax_ref,
    mz_ref,
    dht_ref,
    psi_ref,
    q_ref,
    rims_ref,
    peak,
    mid,
    waves,
    level,
):
    step = pl.program_id(0)
    cells_x, cells_y = c_ref.shape[2], c_ref.shape[3]
    cells_z = c_ref.shape[0] * c_ref.shape[1] // first_steps
    rim = h_ref.shape[2]
    orbitals, some_x, length = psi_ref.shape[0], psi_ref.shape[1], psi_ref.shape[2]
    block = 128
    many = 8
    group = 16

    @pl.when(step < first_steps)
    def _():
        my = my_ref[...]
        ax = ax_ref[...]
        low = c_ref[step, :, cells_x - 16 : cells_x].astype(F32)[:, 0:8]
        high = c_ref[step, :, 0:16].astype(F32)[:, 8:16]
        rims_ref[0] = jnp.concatenate([low, high], axis=1).astype(BF16)

        def planes(i, carry):
            z0 = i * block
            own = dot(c_ref[step, pl.ds(z0, block)].reshape(block * cells_x, cells_y), my)
            own = own.astype(BF16).reshape(block, cells_x, cells_y)
            far = dot(h_ref[step, pl.ds(z0, block)].reshape(block * rim, cells_y), my)
            far = far.astype(BF16).reshape(block, rim, cells_y)
            for p in range(0, block, many):
                some = range(p, p + many)
                flat = jnp.concatenate(
                    [
                        jnp.concatenate([own[z] for z in some], axis=1),
                        jnp.concatenate([far[z] for z in some], axis=1),
                    ],
                    axis=0,
                )
                crossed = dot(ax, flat)
                for k in range(many):
                    row = pl.multiple_of((step * cells_z + z0 + p + k) * pitch, 8)
                    mid[pl.ds(row, cells_x), :] = crossed[:, k * cells_y : (k + 1) * cells_y]
            return carry

        lax.fori_loop(0, cells_z // block, planes, 0)

    def grid_values(x, count):
        first = lax.axis_index("orb") * orbitals
        columns = [
            mid[pl.ds(o * length * pitch + x + k, length, stride=pitch), :].astype(BF16)
            for o in range(orbitals)
            for k in range(count)
        ]
        values = dot(mz_ref[...], jnp.concatenate(columns, axis=1)).astype(BF16)
        total = None
        for o in range(orbitals):
            weight = occ_ref[slot_ref[first + o]].astype(F32) / slot_ref.shape[0]
            wide = values[:, o * count * cells_y : (o + 1) * count * cells_y].astype(F32)
            part = weight * (wide * wide)
            total = part if total is None else total + part
        return values, total

    @pl.when(step == first_steps)
    def _():
        _, total = grid_values(0, 2)
        code, fine, top = scale_of(jnp.sum(total) / total.size)
        level[0] = code
        level[1] = fine
        level[2] = top
        peak[...] = jnp.zeros_like(peak)

    @pl.when(step >= first_steps)
    def _():
        x0 = (step - first_steps) * some_x
        mean = level[2]
        table = dht_ref[...]
        largest = peak[...]
        for local in range(0, some_x, group):
            values, total = grid_values(x0 + local, group)
            for o in range(orbitals):
                for k in range(group):
                    at = (o * group + k) * cells_y
                    psi_ref[o, local + k] = values[:, at : at + cells_y]
            result = hartley_pair(table, total - mean)
            for k in range(group):
                part = result[:, k * cells_y : (k + 1) * cells_y]
                waves[pl.ds(x0 + local + k, length, stride=pitch), :] = part
                size = jnp.abs(part).reshape(length // 8, 8, cells_y)
                largest = jnp.maximum(largest, jnp.max(size, axis=0))
        peak[...] = largest

    @pl.when(step == pl.num_programs(0) - 1)
    def _():
        code, fine, top = scale_of(jnp.max(peak[...]))
        factor = LEVELS / top
        code_rows = coded_rows(cells_y, (code, fine, level[0], level[1], LEVELS))
        per = length // q_ref.shape[0]
        rows = per * cells_x

        def quantise(i, carry):
            for k in range(per):
                row = pl.multiple_of((i * per + k) * pitch, 8)
                values = jnp.round(waves[pl.ds(row, cells_x), :] * factor)
                at = pl.ds(k * cells_x, cells_x)
                q_ref[i, at, :] = values.astype(jnp.int32).astype(jnp.int16)
            q_ref[i, rows : rows + CODE_ROWS, :] = code_rows
            return carry

        lax.fori_loop(0, q_ref.shape[0], quantise, 0, unroll=16)


def density(occupations, slot_orbital, c, halo, my, ax, mz, dht, owners):
    orbitals, length, cells_x, cells_y = c.shape
    first_steps = orbitals
    some_x = 16
    pitch = cells_x + 8
    smem = pl.BlockSpec(memory_space=pltpu.SMEM)
    rows = (length // owners) * cells_x + CODE_ROWS

    return pl.pallas_call(
        functools.partial(density_kernel, first_steps, pitch),
        grid=(first_steps + cells_x // some_x,),
        in_specs=[
            smem,
            smem,
            pl.BlockSpec(memory_space=pltpu.VMEM),
            pl.BlockSpec(memory_space=pltpu.VMEM),
            whole(my),
            whole(ax),
            whole(mz),
            whole(dht),
        ],
        out_specs=[
            pl.BlockSpec(
                (orbitals, some_x, length, cells_y),
                lambda s: (0, jnp.maximum(s - first_steps, 0), 0, 0),
            ),
            pl.BlockSpec((owners, rows, cells_y), lambda s: (0, 0, 0)),
            pl.BlockSpec(
                (1, *halo.shape[1:]), lambda s: (jnp.minimum(s, first_steps - 1), 0, 0, 0)
            ),
            pl.BlockSpec((8, cells_y), lambda s: (0, 0)),
        ],
        out_shape=[
            pltpu.HBM((orbitals, cells_x, length, cells_y), BF16),
            pltpu.HBM((owners, rows, cells_y), jnp.int16),
            pltpu.HBM(halo.shape, BF16),
            jax.ShapeDtypeStruct((8, cells_y), F32),
        ],
        scratch_shapes=[
            pltpu.VMEM(((orbitals * length + 1) * pitch, cells_y), F32),
            pltpu.VMEM(((length + 1) * pitch, cells_y), F32),
            pltpu.SMEM((3,), F32),
        ],
        compiler_params=params(1, 38),
        name="density",
    )(occupations, slot_orbital, c, halo, my, ax, mz, dht)


def kinetic_kernel(
    pitch, c_ref, near_ref, far_ref, dy_ref, dx_ref, dz_ref, after_ref, kin_ref, step_ref, sums_ref, wide, acc
):
    length, cells_x, cells_y = c_ref.shape[1], c_ref.shape[2], c_ref.shape[3]
    block = 8

    def widen(z, carry):
        row = pl.multiple_of(z * pitch, 8)
        wide[pl.ds(row, cells_x), :] = c_ref[0, z].astype(F32)
        return carry

    lax.fori_loop(0, length, widen, 0, unroll=8)

    def columns(i, carry):
        x = 2 * i
        pair = side_by_side(
            wide[pl.ds(x, length, stride=pitch), :].astype(BF16),
            wide[pl.ds(x + 1, length, stride=pitch), :].astype(BF16),
        )
        values = dot(dz_ref[...], pair)
        acc[pl.ds(x, length, stride=pitch), :] = values[:, :cells_y]
        acc[pl.ds(x + 1, length, stride=pitch), :] = values[:, cells_y:]
        return carry

    lax.fori_loop(0, cells_x // 2, columns, 0, unroll=4)

    def planes(i, carry):
        energy, norm = carry
        z0 = i * block
        own = c_ref[0, pl.ds(z0, block)]
        along_y = dot(own.reshape(block * cells_x, cells_y), dy_ref[...])
        steps = []
        for p in range(0, block, 2):
            z = z0 + p
            pair = jnp.concatenate(
                [
                    side_by_side(c_ref[0, z], c_ref[0, z + 1]),
                    side_by_side(near_ref[0, z], near_ref[0, z + 1]),
                    side_by_side(far_ref[0, z], far_ref[0, z + 1]),
                ],
                axis=0,
            )
            along_x = dot(dx_ref[...], pair)
            for k in range(2):
                at = pl.ds(pl.multiple_of((z + k) * pitch, 8), cells_x)
                value = (
                    acc[at, :]
                    + along_x[:, k * cells_y : (k + 1) * cells_y]
                    + along_y[(p + k) * cells_x : (p + k + 1) * cells_x]
                )
                tiles = (cells_x // 8, 8, cells_y)
                largest = jnp.max(jnp.max(jnp.abs(value).reshape(tiles), axis=0), axis=0)
                largest = jnp.maximum(largest, 1e-30).reshape(1, cells_y)
                coded = jnp.round(value * (LEVELS / largest))
                kin_ref[0, z + k] = coded.astype(jnp.int32).astype(jnp.int16)
                steps.append(largest * (1.0 / LEVELS))
                coeff = own[p + k].astype(F32)
                energy = energy + jnp.sum((coeff * value).reshape(tiles), axis=0)
                norm = norm + jnp.sum((coeff * coeff).reshape(tiles), axis=0)
        step_ref[0, pl.ds(pl.multiple_of(z0, block), block), :] = jnp.concatenate(steps, axis=0)
        return energy, norm

    zeros = jnp.zeros((8, cells_y), F32)
    energy, norm = lax.fori_loop(0, length // block, planes, (zeros, zeros), unroll=2)
    sums_ref[0, 0:8] = energy
    sums_ref[0, 8:16] = norm


def kinetic(c, near, far, dy, dx, dz, after):
    orbitals, length, cells_x, cells_y = c.shape
    cells = orbitals * length * cells_x * cells_y
    pitch = cells_x + 8

    def block(array):
        return pl.BlockSpec((1, *array.shape[1:]), lambda o: (o, 0, 0, 0))

    return pl.pallas_call(
        functools.partial(kinetic_kernel, pitch),
        grid=(orbitals,),
        in_specs=[
            block(c),
            block(near),
            block(far),
            whole(dy),
            whole(dx),
            whole(dz),
            pl.BlockSpec(memory_space=pl.ANY),
        ],
        out_specs=[
            block(c),
            pl.BlockSpec((1, length, cells_y), lambda o: (o, 0, 0)),
            pl.BlockSpec((1, 16, cells_y), lambda o: (o, 0, 0)),
        ],
        out_shape=[
            pltpu.HBM(c.shape, jnp.int16),
            jax.ShapeDtypeStruct((orbitals, length, cells_y), F32),
            jax.ShapeDtypeStruct((orbitals, 16, cells_y), F32),
        ],
        scratch_shapes=[
            pltpu.VMEM(((length + 1) * pitch, cells_y), F32),
            pltpu.VMEM(((length + 1) * pitch, cells_y), F32),
        ],
        compiler_params=params(1, 26),
        cost_estimate=pl.CostEstimate(
            flops=cells * 768 * 4, bytes_accessed=cells * 7, transcendentals=0
        ),
        name="kinetic",
    )(c, near, far, dy, dx, dz, after)


def unpacked(ref, source, rows):
    codes = ref[source, rows : rows + CODE_ROWS, :].astype(jnp.int32).astype(F32)
    powers = jnp.exp2(codes) * (1.0 / (LEVELS * FINE))
    step = codes[1:2] * powers[0:1]
    mean = codes[4:5] * (codes[3:4] * powers[2:3])
    return ref[source, 0:rows, :].astype(jnp.int32).astype(F32) * step, mean


def sum_kernel(per, got_ref, after_ref, out_ref):
    rows = out_ref.shape[0]
    cells_y = out_ref.shape[1]

    def body(source, carry):
        total, means = carry
        values, mean = unpacked(got_ref, source, rows)
        return total + values, means + mean

    total, means = lax.fori_loop(
        0,
        got_ref.shape[0],
        body,
        (jnp.zeros((rows, cells_y), F32), jnp.zeros((1, cells_y), F32)),
        unroll=2,
    )
    length = got_ref.shape[0] * per
    row = lax.broadcasted_iota(jnp.int32, (rows, cells_y), 0)
    flat = (lax.axis_index("orb") == 0) & (row < rows // per)
    out_ref[...] = total + jnp.where(flat, means * math.sqrt(length), 0.0)


def slab_sum(got, rows, per, after):
    return pl.pallas_call(
        functools.partial(sum_kernel, per),
        in_specs=[pl.BlockSpec(memory_space=pltpu.VMEM), pl.BlockSpec(memory_space=pl.ANY)],
        out_shape=jax.ShapeDtypeStruct((rows, got.shape[2]), F32),
        compiler_params=params(0, 12),
        name="slab_sum",
    )(got, after)


def solve_kernel(curve_z_ref, slab_ref, dht_ref, curve_ref, q_ref):
    per, length, cells_y = slab_ref.shape
    cells_x = length // 2
    orb = lax.axis_index("orb")
    corner = pl.multiple_of(lax.axis_index("grid") * cells_x, cells_x)
    dht = dht_ref[...]
    own = dht_ref[pl.ds(corner, cells_x), :]
    row = lax.broadcasted_iota(jnp.int32, (length, cells_y), 0)
    col = lax.broadcasted_iota(jnp.int32, (length, cells_y), 1)
    waves = dot_exact(jnp.concatenate([slab_ref[k] for k in range(per)], axis=0), dht)
    waves = jnp.concatenate(
        [waves[k * length : (k + 1) * length] for k in range(per)], axis=1
    )
    waves = dot_exact(dht, waves)
    parts = []
    for k in range(per):
        wave = orb * per + k
        anchor = (row == 0) & (col == 0) & (wave == 0)
        bent = curve_ref[...] + curve_z_ref[wave]
        factor = jnp.where(anchor, 0.0, COULOMB / jnp.where(anchor, 1.0, bent))
        parts.append(waves[:, k * cells_y : (k + 1) * cells_y] * factor)
    field = dot_exact(own, jnp.concatenate(parts, axis=1))
    field = jnp.concatenate(
        [field[:, k * cells_y : (k + 1) * cells_y] for k in range(per)], axis=0
    )
    field = dot_exact(field, dht)
    code, fine, top = scale_of(jnp.max(jnp.abs(field)))
    coded = jnp.round(field * (LEVELS / top)).astype(jnp.int32).astype(jnp.int16)
    code_rows = coded_rows(cells_y, (code, fine))
    rows = per * cells_x

    def spread(i, carry):
        q_ref[i, 0:rows, :] = coded
        q_ref[i, rows : rows + CODE_ROWS, :] = code_rows
        return carry

    lax.fori_loop(0, q_ref.shape[0], spread, 0, unroll=4)


def solve(curve_z, slab, dht, plane_curve, owners):
    per, length, cells_y = slab.shape
    vmem = pl.BlockSpec(memory_space=pltpu.VMEM)
    return pl.pallas_call(
        solve_kernel,
        in_specs=[pl.BlockSpec(memory_space=pltpu.SMEM), vmem, vmem, vmem],
        out_shape=jax.ShapeDtypeStruct((owners, per * (length // 2) + CODE_ROWS, cells_y), jnp.int16),
        compiler_params=params(0, 12),
        name="solve",
    )(curve_z, slab, dht, plane_curve)


def field_kernel(
    pitch,
    turn_pitch,
    got_ref,
    psi_ref,
    kin_ref,
    dht_ref,
    tz_ref,
    back_ref,
    rim_ref,
    slab_ref,
    sums_ref,
    waves,
    turn,
    head,
    values,
):
    step = pl.program_id(0)
    orbitals, cells_x, length, cells_y = psi_ref.shape
    some_x = cells_x // pl.num_programs(0)
    owners = got_ref.shape[0]
    per = length // owners
    rim = rim_ref.shape[2] // 2
    first = pl.multiple_of((lax.axis_index("orb") * per) // 8 * 8, 8)

    @pl.when(step == 0)
    def _():
        def unpack(source, carry):
            found, _ = unpacked(got_ref, source, per * cells_x)
            for k in range(per):
                at = pl.ds(pl.multiple_of((source * per + k) * pitch, 8), cells_x)
                waves[at, :] = found[k * cells_x : (k + 1) * cells_x]
            return carry

        lax.fori_loop(0, owners, unpack, 0, unroll=16)
        sums_ref[...] = kin_ref[...]

    group = 16
    energy = [jnp.zeros((8, cells_y), F32) for _ in range(orbitals)]
    for local in range(0, some_x, group):
        x = step * some_x + local
        field = hartley_pair(
            dht_ref[...],
            jnp.concatenate(
                [waves[pl.ds(x + k, length, stride=pitch), :] for k in range(group)], axis=1
            ),
        )
        values[local // group] = field
        own = values[local // group, pl.ds(first, 8), :]
        for k in range(group):
            slab_ref[local + k] = own[:, k * cells_y : (k + 1) * cells_y]
        products = []
        for o in range(orbitals):
            psi = jnp.concatenate([psi_ref[o, x + k] for k in range(group)], axis=1)
            psi = psi.astype(F32)
            product = field * psi
            products.append(product.astype(BF16))
            squares = product * psi
            for k in range(group):
                part = squares[:, k * cells_y : (k + 1) * cells_y]
                part = part.reshape(length // 8, 8, cells_y)
                energy[o] = energy[o] + jnp.sum(part, axis=0)
        back = dot(tz_ref[...], jnp.concatenate(products, axis=1))
        for o in range(orbitals):
            for k in range(group):
                at = (o * group + k) * cells_y
                row = o * length * turn_pitch + local + k
                turn[pl.ds(row, length, stride=turn_pitch), :] = back[:, at : at + cells_y]

    for o in range(orbitals):
        sums_ref[o, 0:8] = sums_ref[o, 0:8] + energy[o]

    def turned(o, z, start, count):
        row = pl.multiple_of((o * length + z) * turn_pitch, 8) + start
        return turn[pl.ds(row, count), :]

    def rows(z, carry):
        for o in range(orbitals):
            back_ref[o, z] = turned(o, z, 0, some_x).astype(BF16)
        return carry

    lax.fori_loop(0, length, rows, 0, unroll=16)

    @pl.when(step == 0)
    def _():
        def keep(z, carry):
            for o in range(orbitals):
                head[o, z] = turned(o, z, 0, rim)
            return carry

        lax.fori_loop(0, length, keep, 0, unroll=16)

    @pl.when(step == pl.num_programs(0) - 1)
    def _():
        def send(z, carry):
            for o in range(orbitals):
                both = jnp.concatenate([turned(o, z, some_x - rim, rim), head[o, z]], axis=0)
                rim_ref[o, z] = both.astype(BF16)
            return carry

        lax.fori_loop(0, length, send, 0, unroll=16)


def field(got, psi, kin_sums, dht, tz):
    orbitals, cells_x, length, cells_y = psi.shape
    some_x = 16
    pitch = cells_x + 8
    turn_pitch = some_x + 8
    rim = 8
    return pl.pallas_call(
        functools.partial(field_kernel, pitch, turn_pitch),
        grid=(cells_x // some_x,),
        in_specs=[
            pl.BlockSpec(memory_space=pltpu.VMEM),
            pl.BlockSpec(memory_space=pltpu.VMEM),
            whole(kin_sums),
            whole(dht),
            whole(tz),
        ],
        out_specs=[
            pl.BlockSpec((orbitals, length, some_x, cells_y), lambda i: (0, 0, i, 0)),
            pl.BlockSpec((orbitals, length, 2 * rim, cells_y), lambda i: (0, 0, 0, 0)),
            pl.BlockSpec((some_x, 8, cells_y), lambda i: (i, 0, 0)),
            whole(kin_sums),
        ],
        out_shape=[
            pltpu.HBM((orbitals, length, cells_x, cells_y), BF16),
            jax.ShapeDtypeStruct((orbitals, length, 2 * rim, cells_y), BF16),
            jax.ShapeDtypeStruct((cells_x, 8, cells_y), F32),
            jax.ShapeDtypeStruct(kin_sums.shape, F32),
        ],
        scratch_shapes=[
            pltpu.VMEM(((length + 1) * pitch, cells_y), F32),
            pltpu.VMEM(((orbitals * length + 1) * turn_pitch, cells_y), F32),
            pltpu.VMEM((orbitals, length, rim, cells_y), F32),
            pltpu.VMEM((1, length, 16 * cells_y), F32),
        ],
        compiler_params=params(1, 30),
        name="field",
    )(got, psi, kin_sums, dht, tz)


def update_kernel(
    sums_ref,
    other_ref,
    back_ref,
    rim_ref,
    c_ref,
    kin_ref,
    step_ref,
    tx_ref,
    ty_ref,
    out_ref,
    energy_ref,
):
    orbital = pl.program_id(0)

    @pl.when(pl.program_id(1) == 0)
    def _():
        both = sums_ref[orbital] + other_ref[orbital]
        energy_ref[orbital] = jnp.sum(both[0:8]) / jnp.sum(both[8:16])

    energy = energy_ref[orbital]
    some_z, cells_x, cells_y = back_ref.shape[1], back_ref.shape[2], back_ref.shape[3]
    tx = tx_ref[...]
    ty = ty_ref[...]
    block = 16
    many = 8

    def planes(i, carry):
        z0 = i * block
        crossed = []
        for p in range(0, block, many):
            some = range(p, p + many)
            flat = jnp.concatenate(
                [
                    jnp.concatenate([back_ref[0, z0 + k] for k in some], axis=1),
                    jnp.concatenate([rim_ref[0, z0 + k] for k in some], axis=1),
                ],
                axis=0,
            )
            both = dot(tx, flat).astype(BF16)
            crossed += [both[:, k * cells_y : (k + 1) * cells_y] for k in range(many)]
        potential = dot(jnp.concatenate(crossed, axis=0), ty)
        steps = step_ref[0, pl.ds(pl.multiple_of(z0, block), block), :]
        for p in range(block):
            z = z0 + p
            kin = kin_ref[0, z].astype(jnp.int32).astype(F32) * steps[p : p + 1]
            applied = potential[p * cells_x : (p + 1) * cells_x] + kin
            coeff = c_ref[0, z].astype(F32)
            out_ref[0, z] = (coeff - STEP_SIZE * (applied - energy * coeff)).astype(BF16)
        return carry

    lax.fori_loop(0, some_z // block, planes, 0, unroll=4)


def update(sums, other_sums, back, rim, c, kin, steps, tx, ty):
    orbitals, length, cells_x, cells_y = c.shape
    chunks = 2
    part = length // chunks
    block = pl.BlockSpec((1, part, cells_x, cells_y), lambda o, j: (o, j, 0, 0))
    return pl.pallas_call(
        update_kernel,
        grid=(orbitals, chunks),
        in_specs=[
            whole(sums),
            whole(other_sums),
            block,
            pl.BlockSpec((1, part, rim.shape[2], cells_y), lambda o, j: (o, j, 0, 0)),
            block,
            block,
            pl.BlockSpec((1, part, cells_y), lambda o, j: (o, j, 0)),
            whole(tx),
            whole(ty),
        ],
        out_specs=[block, pl.BlockSpec(memory_space=pltpu.SMEM)],
        out_shape=[
            jax.ShapeDtypeStruct(c.shape, BF16),
            jax.ShapeDtypeStruct((orbitals,), F32),
        ],
        compiler_params=params(2, 12),
        name="update",
    )(sums, other_sums, back, rim, c, kin, steps, tx, ty)


def to_other(array):
    return lax.ppermute(array, "grid", [(0, 1), (1, 0)])


def in_hbm(array):
    return pltpu.with_memory_space_constraint(array, pltpu.HBM)


def to_all(blocks):
    return lax.all_to_all(blocks, "orb", split_axis=0, concat_axis=0, tiled=True)


def on_device(coefficients, occupations, slot_orbital):
    orbitals, length, cells_x, cells_y = coefficients.shape
    owners = slot_orbital.shape[0] // orbitals
    per = length // owners
    magic, trans, kin_taps = magic_pairs(), transposed_pairs(), kinetic_pairs()
    magic_line = band_periodic(length, magic)
    trans_line = band_periodic(length, trans)
    kin_line = band_periodic(length, kin_taps, -0.5)
    inside = list(range(cells_x))
    near_cells = inside + with_rims(cells_x, 0, 8)
    all_cells = near_cells + with_rims(cells_x, 8, 16)
    dht = hartley(length)
    table = jnp.asarray(split_table(dht))
    waves = curve(length)

    c = in_hbm(coefficients)
    own_near, _ = own_rims(c, 0, 8)
    near = to_other(own_near)
    psi, coded, own_far, peak = density(
        occupations,
        slot_orbital,
        coefficients,
        near,
        jnp.asarray(magic_line.T),
        jnp.asarray(band_columns(cells_x, near_cells, magic)),
        jnp.asarray(magic_line),
        table,
        owners,
    )
    got = to_all(coded)
    far = to_other(own_far)
    kin, steps, kin_sums = kinetic(
        c,
        near,
        far,
        jnp.asarray(kin_line.T),
        jnp.asarray(band_columns(cells_x, all_cells, kin_taps, -0.5)),
        jnp.asarray(kin_line),
        peak,
    )
    half = slab_sum(got, per * cells_x, per, kin_sums).reshape(per, cells_x, cells_y)
    slab = lax.all_gather(half, "grid", axis=1, tiled=True)
    spread = solve(
        jnp.asarray(waves.astype(np.float32)),
        slab,
        jnp.asarray(dht),
        jnp.asarray((waves[:, None] + waves[None, :]).astype(np.float32)),
        owners,
    )
    back, back_rims, slab_field, sums = field(
        to_all(spread), psi, kin_sums, table, jnp.asarray(trans_line)
    )
    updated, energies = update(
        sums,
        to_other(sums),
        in_hbm(back),
        to_other(back_rims),
        c,
        in_hbm(kin),
        steps,
        jnp.asarray(band_columns(cells_x, near_cells, trans)),
        jnp.asarray(trans_line.T),
    )
    first = lax.rem(lax.axis_index("orb") * per, 8)
    potential = lax.dynamic_slice_in_dim(slab_field, first, per, 1).transpose(1, 0, 2)
    return (updated, energies, potential)


def solution(mesh):
    return jax.shard_map(
        on_device,
        mesh=mesh,
        in_specs=(P("orb", None, "grid", None), P(), P()),
        out_specs=(P("orb", None, "grid", None), P("orb"), P("orb", "grid", None)),
        check_vma=False,
    )
```

```python
import functools
import math

import jax
import jax.numpy as jnp
import ml_dtypes
import numpy as np
from jax import lax
from jax.experimental import pallas as pl
from jax.experimental.pallas import tpu as pltpu
from jax.sharding import PartitionSpec as P

MAGIC = (
    8.433424733352934e-07,
    -1.290557201342061e-05,
    8.76298447621056e-05,
    -0.00030158038132690465,
    0.001747237136729939,
    -0.009420470302010804,
    0.023738214637249424,
    0.0612625895831208,
    0.9940415697834004,
    -0.06048952891969835,
    -0.021030251609303816,
    0.013372634148547948,
    -0.0034412814449349387,
    0.0004944322768868992,
    -5.185986881173433e-05,
    2.7273449291197967e-06,
)
STEP_SIZE = 0.1
COULOMB = 4.0 * math.pi
LEVELS = 32000.0
CODE_ROWS = 8
FINE = 16384.0
F32 = jnp.float32
BF16 = jnp.bfloat16
HIGHEST = lax.Precision.HIGHEST
MIB = 1024 * 1024


def magic_pairs():
    return [(position - 8, MAGIC[position]) for position in range(16)]


def transposed_pairs():
    return [(8 - position, MAGIC[position]) for position in range(16)]


def kinetic_pairs():
    spread = 14
    weights = []
    for distance in range(1, spread + 1):
        numerator = 2.0 * (-1.0) ** (distance + 1) * math.factorial(spread) ** 2
        weights.append(
            numerator
            / (
                distance
                * distance
                * math.factorial(spread - distance)
                * math.factorial(spread + distance)
            )
        )
    result = [(0, -2.0 * sum(weights))]
    for distance in range(1, spread + 1):
        result.append((distance, weights[distance - 1]))
        result.append((-distance, weights[distance - 1]))
    return result


def rounded(weight):
    return np.float32(np.float32(weight).astype(ml_dtypes.bfloat16))


def band_periodic(length, pairs, scale=1.0):
    matrix = np.zeros((length, length), np.float32)
    for offset, weight in pairs:
        for i in range(length):
            matrix[i, (i + offset) % length] += scale * rounded(weight)
    return matrix.astype(ml_dtypes.bfloat16)


def band_columns(length, columns, pairs, scale=1.0):
    matrix = np.zeros((length, len(columns)), np.float32)
    place = {cell: k for k, cell in enumerate(columns)}
    for offset, weight in pairs:
        for i in range(length):
            matrix[i, place[i + offset]] += scale * rounded(weight)
    return matrix.astype(ml_dtypes.bfloat16)


def with_rims(length, inner, outer):
    return [*range(-outer, -inner), *range(length + inner, length + outer)]


def hartley(length):
    index = np.arange(length)
    angle = 2.0 * np.pi * ((index[:, None] * index[None, :]) % length) / length
    return ((np.cos(angle) + np.sin(angle)) / math.sqrt(length)).astype(np.float32)


def split_table(table):
    high = table.astype(ml_dtypes.bfloat16)
    low = (table - high.astype(np.float32)).astype(ml_dtypes.bfloat16)
    return np.concatenate([high, low, high], axis=1)


def curve(length):
    return 2.0 - 2.0 * np.cos(2.0 * np.pi * np.arange(length) / length)


def dot(a, b):
    return jnp.dot(a, b, preferred_element_type=F32)


def dot_exact(a, b):
    return jnp.dot(a, b, preferred_element_type=F32, precision=HIGHEST)


def params(count, mebibytes):
    return pltpu.CompilerParams(
        dimension_semantics=("arbitrary",) * count, vmem_limit_bytes=mebibytes * MIB
    )


def cost(cells, bytes_each):
    return pl.CostEstimate(
        flops=cells * 256, bytes_accessed=cells * bytes_each, transcendentals=0
    )


def whole(array):
    zeros = (0,) * array.ndim
    return pl.BlockSpec(array.shape, lambda *_: zeros)


def scale_of(largest):
    largest = jnp.maximum(largest, 1e-30)
    code = jnp.ceil(jnp.log2(largest))
    power = jnp.exp2(code)
    units = jnp.ceil(largest / power * FINE) + 1.0
    return code, units, units * (1.0 / FINE) * power


def coded_rows(cells_y, codes):
    row = lax.broadcasted_iota(jnp.int32, (CODE_ROWS, cells_y), 0)
    values = jnp.zeros((CODE_ROWS, cells_y), F32)
    for k, code in enumerate(codes):
        values = jnp.where(row == k, code, values)
    return values.astype(jnp.int32).astype(jnp.int16)


def side_by_side(first, second):
    return jnp.concatenate([first, second], axis=1)


def hartley_pair(table, pair):
    high = pair.astype(BF16)
    low = (pair - high.astype(F32)).astype(BF16)
    return dot(table, jnp.concatenate([high, high, low], axis=0))


def rims_kernel(low_ref, high_ref, out_ref):
    half = low_ref.shape[2] // 2
    low = low_ref[...].astype(F32)[:, :, half:]
    high = high_ref[...].astype(F32)[:, :, :half]
    out_ref[...] = jnp.concatenate([low, high], axis=2).astype(BF16)


def own_rims(c):
    orbitals, length, cells_x, cells_y = c.shape
    tile = 16

    def at(k):
        return pl.BlockSpec((1, length, tile, cells_y), lambda o: (o, 0, k, 0))

    return pl.pallas_call(
        rims_kernel,
        grid=(orbitals,),
        in_specs=[at(cells_x // tile - 1), at(0)],
        out_specs=at(0),
        out_shape=jax.ShapeDtypeStruct((orbitals, length, tile, cells_y), BF16),
        compiler_params=params(1, 8),
        name="own_rims",
    )(c, c)


def density_kernel(
    first_steps,
    pitch,
    occ_ref,
    slot_ref,
    c_ref,
    h_ref,
    my_ref,
    ax_ref,
    mz_ref,
    dht_ref,
    psi_ref,
    q_ref,
    rims_ref,
    peak,
    mid,
    waves,
    level,
):
    step = pl.program_id(0)
    cells_x, cells_y = c_ref.shape[2], c_ref.shape[3]
    cells_z = c_ref.shape[0] * c_ref.shape[1] // first_steps
    rim = h_ref.shape[2]
    orbitals, some_x, length = psi_ref.shape[0], psi_ref.shape[1], psi_ref.shape[2]
    block = 128
    many = 8
    group = 16

    @pl.when(step < first_steps)
    def _():
        my = my_ref[...]
        ax = ax_ref[...]
        low = c_ref[step, :, cells_x - 16 : cells_x].astype(F32)[:, 0:8]
        high = c_ref[step, :, 0:16].astype(F32)[:, 8:16]
        rims_ref[0] = jnp.concatenate([low, high], axis=1).astype(BF16)

        def planes(i, carry):
            z0 = i * block
            own = dot(c_ref[step, pl.ds(z0, block)].reshape(block * cells_x, cells_y), my)
            own = own.astype(BF16).reshape(block, cells_x, cells_y)
            far = dot(h_ref[step, pl.ds(z0, block)].reshape(block * rim, cells_y), my)
            far = far.astype(BF16).reshape(block, rim, cells_y)
            for p in range(0, block, many):
                some = range(p, p + many)
                flat = jnp.concatenate(
                    [
                        jnp.concatenate([own[z] for z in some], axis=1),
                        jnp.concatenate([far[z] for z in some], axis=1),
                    ],
                    axis=0,
                )
                crossed = dot(ax, flat)
                for k in range(many):
                    row = pl.multiple_of((step * cells_z + z0 + p + k) * pitch, 8)
                    mid[pl.ds(row, cells_x), :] = crossed[:, k * cells_y : (k + 1) * cells_y]
            return carry

        lax.fori_loop(0, cells_z // block, planes, 0)

    def grid_values(x, count):
        first = lax.axis_index("orb") * orbitals
        columns = [
            mid[pl.ds(o * length * pitch + x + k, length, stride=pitch), :].astype(BF16)
            for o in range(orbitals)
            for k in range(count)
        ]
        values = dot(mz_ref[...], jnp.concatenate(columns, axis=1)).astype(BF16)
        total = None
        for o in range(orbitals):
            weight = occ_ref[slot_ref[first + o]].astype(F32) / slot_ref.shape[0]
            wide = values[:, o * count * cells_y : (o + 1) * count * cells_y].astype(F32)
            part = weight * (wide * wide)
            total = part if total is None else total + part
        return values, total

    @pl.when(step == first_steps)
    def _():
        _, total = grid_values(0, 2)
        code, fine, top = scale_of(jnp.sum(total) / total.size)
        level[0] = code
        level[1] = fine
        level[2] = top
        peak[...] = jnp.zeros_like(peak)

    @pl.when(step >= first_steps)
    def _():
        x0 = (step - first_steps) * some_x
        mean = level[2]
        table = dht_ref[...]
        largest = peak[...]
        for local in range(0, some_x, group):
            values, total = grid_values(x0 + local, group)
            for o in range(orbitals):
                for k in range(group):
                    at = (o * group + k) * cells_y
                    psi_ref[o, local + k] = values[:, at : at + cells_y]
            result = hartley_pair(table, total - mean)
            for k in range(group):
                part = result[:, k * cells_y : (k + 1) * cells_y]
                waves[pl.ds(x0 + local + k, length, stride=pitch), :] = part
                size = jnp.abs(part).reshape(length // 8, 8, cells_y)
                largest = jnp.maximum(largest, jnp.max(size, axis=0))
        peak[...] = largest

    @pl.when(step == pl.num_programs(0) - 1)
    def _():
        code, fine, top = scale_of(jnp.max(peak[...]))
        factor = LEVELS / top
        code_rows = coded_rows(cells_y, (code, fine, level[0], level[1], LEVELS))
        per = length // q_ref.shape[0]
        rows = per * cells_x

        def quantise(i, carry):
            for k in range(per):
                row = pl.multiple_of((i * per + k) * pitch, 8)
                values = jnp.round(waves[pl.ds(row, cells_x), :] * factor)
                at = pl.ds(k * cells_x, cells_x)
                q_ref[i, at, :] = values.astype(jnp.int32).astype(jnp.int16)
            q_ref[i, rows : rows + CODE_ROWS, :] = code_rows
            return carry

        lax.fori_loop(0, q_ref.shape[0], quantise, 0, unroll=16)


def density(occupations, slot_orbital, c, halo, my, ax, mz, dht, owners):
    orbitals, length, cells_x, cells_y = c.shape
    first_steps = orbitals
    some_x = 16
    pitch = cells_x + 8
    smem = pl.BlockSpec(memory_space=pltpu.SMEM)
    rows = (length // owners) * cells_x + CODE_ROWS

    return pl.pallas_call(
        functools.partial(density_kernel, first_steps, pitch),
        grid=(first_steps + cells_x // some_x,),
        in_specs=[
            smem,
            smem,
            pl.BlockSpec(memory_space=pltpu.VMEM),
            pl.BlockSpec(memory_space=pltpu.VMEM),
            whole(my),
            whole(ax),
            whole(mz),
            whole(dht),
        ],
        out_specs=[
            pl.BlockSpec(
                (orbitals, some_x, length, cells_y),
                lambda s: (0, jnp.maximum(s - first_steps, 0), 0, 0),
            ),
            pl.BlockSpec((owners, rows, cells_y), lambda s: (0, 0, 0)),
            pl.BlockSpec(
                (1, *halo.shape[1:]), lambda s: (jnp.minimum(s, first_steps - 1), 0, 0, 0)
            ),
            pl.BlockSpec((8, cells_y), lambda s: (0, 0)),
        ],
        out_shape=[
            pltpu.HBM((orbitals, cells_x, length, cells_y), BF16),
            pltpu.HBM((owners, rows, cells_y), jnp.int16),
            pltpu.HBM(halo.shape, BF16),
            jax.ShapeDtypeStruct((8, cells_y), F32),
        ],
        scratch_shapes=[
            pltpu.VMEM(((orbitals * length + 1) * pitch, cells_y), F32),
            pltpu.VMEM(((length + 1) * pitch, cells_y), F32),
            pltpu.SMEM((3,), F32),
        ],
        compiler_params=params(1, 38),
        name="density",
    )(occupations, slot_orbital, c, halo, my, ax, mz, dht)


def kinetic_kernel(
    pitch, c_ref, near_ref, far_ref, dy_ref, dx_ref, dz_ref, after_ref, kin_ref, step_ref, sums_ref, wide, acc
):
    length, cells_x, cells_y = c_ref.shape[1], c_ref.shape[2], c_ref.shape[3]
    block = 8

    def widen(z, carry):
        row = pl.multiple_of(z * pitch, 8)
        wide[pl.ds(row, cells_x), :] = c_ref[0, z].astype(F32)
        return carry

    lax.fori_loop(0, length, widen, 0, unroll=8)

    def columns(i, carry):
        x = 2 * i
        pair = side_by_side(
            wide[pl.ds(x, length, stride=pitch), :].astype(BF16),
            wide[pl.ds(x + 1, length, stride=pitch), :].astype(BF16),
        )
        values = dot(dz_ref[...], pair)
        acc[pl.ds(x, length, stride=pitch), :] = values[:, :cells_y]
        acc[pl.ds(x + 1, length, stride=pitch), :] = values[:, cells_y:]
        return carry

    lax.fori_loop(0, cells_x // 2, columns, 0, unroll=4)

    def planes(i, carry):
        energy, norm = carry
        z0 = i * block
        own = c_ref[0, pl.ds(z0, block)]
        along_y = dot(own.reshape(block * cells_x, cells_y), dy_ref[...])
        steps = []
        for p in range(0, block, 2):
            z = z0 + p
            pair = jnp.concatenate(
                [
                    side_by_side(c_ref[0, z], c_ref[0, z + 1]),
                    side_by_side(near_ref[0, z], near_ref[0, z + 1]),
                    side_by_side(far_ref[0, z], far_ref[0, z + 1]),
                ],
                axis=0,
            )
            along_x = dot(dx_ref[...], pair)
            for k in range(2):
                at = pl.ds(pl.multiple_of((z + k) * pitch, 8), cells_x)
                value = (
                    acc[at, :]
                    + along_x[:, k * cells_y : (k + 1) * cells_y]
                    + along_y[(p + k) * cells_x : (p + k + 1) * cells_x]
                )
                tiles = (cells_x // 8, 8, cells_y)
                largest = jnp.max(jnp.max(jnp.abs(value).reshape(tiles), axis=0), axis=0)
                largest = jnp.maximum(largest, 1e-30).reshape(1, cells_y)
                coded = jnp.round(value * (LEVELS / largest))
                kin_ref[0, z + k] = coded.astype(jnp.int32).astype(jnp.int16)
                steps.append(largest * (1.0 / LEVELS))
                coeff = own[p + k].astype(F32)
                energy = energy + jnp.sum((coeff * value).reshape(tiles), axis=0)
                norm = norm + jnp.sum((coeff * coeff).reshape(tiles), axis=0)
        step_ref[0, pl.ds(pl.multiple_of(z0, block), block), :] = jnp.concatenate(steps, axis=0)
        return energy, norm

    zeros = jnp.zeros((8, cells_y), F32)
    energy, norm = lax.fori_loop(0, length // block, planes, (zeros, zeros), unroll=2)
    sums_ref[0, 0:8] = energy
    sums_ref[0, 8:16] = norm


def kinetic(c, near, far, dy, dx, dz, after):
    orbitals, length, cells_x, cells_y = c.shape
    cells = orbitals * length * cells_x * cells_y
    pitch = cells_x + 8

    def block(array):
        return pl.BlockSpec((1, *array.shape[1:]), lambda o: (o, 0, 0, 0))

    return pl.pallas_call(
        functools.partial(kinetic_kernel, pitch),
        grid=(orbitals,),
        in_specs=[
            block(c),
            block(near),
            block(far),
            whole(dy),
            whole(dx),
            whole(dz),
            pl.BlockSpec(memory_space=pl.ANY),
        ],
        out_specs=[
            block(c),
            pl.BlockSpec((1, length, cells_y), lambda o: (o, 0, 0)),
            pl.BlockSpec((1, 16, cells_y), lambda o: (o, 0, 0)),
        ],
        out_shape=[
            pltpu.HBM(c.shape, jnp.int16),
            jax.ShapeDtypeStruct((orbitals, length, cells_y), F32),
            jax.ShapeDtypeStruct((orbitals, 16, cells_y), F32),
        ],
        scratch_shapes=[
            pltpu.VMEM(((length + 1) * pitch, cells_y), F32),
            pltpu.VMEM(((length + 1) * pitch, cells_y), F32),
        ],
        compiler_params=params(1, 26),
        cost_estimate=pl.CostEstimate(
            flops=cells * 768 * 4, bytes_accessed=cells * 7, transcendentals=0
        ),
        name="kinetic",
    )(c, near, far, dy, dx, dz, after)


def unpacked(ref, source, rows):
    codes = ref[source, rows : rows + CODE_ROWS, :].astype(jnp.int32).astype(F32)
    powers = jnp.exp2(codes) * (1.0 / (LEVELS * FINE))
    step = codes[1:2] * powers[0:1]
    mean = codes[4:5] * (codes[3:4] * powers[2:3])
    return ref[source, 0:rows, :].astype(jnp.int32).astype(F32) * step, mean


def sum_kernel(per, got_ref, after_ref, out_ref):
    rows = out_ref.shape[0]
    cells_y = out_ref.shape[1]

    def body(source, carry):
        total, means = carry
        values, mean = unpacked(got_ref, source, rows)
        return total + values, means + mean

    total, means = lax.fori_loop(
        0,
        got_ref.shape[0],
        body,
        (jnp.zeros((rows, cells_y), F32), jnp.zeros((1, cells_y), F32)),
        unroll=8,
    )
    length = got_ref.shape[0] * per
    row = lax.broadcasted_iota(jnp.int32, (rows, cells_y), 0)
    flat = (lax.axis_index("orb") == 0) & (row < rows // per)
    out_ref[...] = total + jnp.where(flat, means * math.sqrt(length), 0.0)


def slab_sum(got, rows, per, after):
    return pl.pallas_call(
        functools.partial(sum_kernel, per),
        in_specs=[pl.BlockSpec(memory_space=pltpu.VMEM), pl.BlockSpec(memory_space=pl.ANY)],
        out_shape=jax.ShapeDtypeStruct((rows, got.shape[2]), F32),
        compiler_params=params(0, 12),
        name="slab_sum",
    )(got, after)


def solve_kernel(curve_z_ref, slab_ref, dht_ref, curve_ref, q_ref):
    per, length, cells_y = slab_ref.shape
    cells_x = length // 2
    orb = lax.axis_index("orb")
    corner = pl.multiple_of(lax.axis_index("grid") * cells_x, cells_x)
    dht = dht_ref[...]
    own = dht_ref[pl.ds(corner, cells_x), :]
    row = lax.broadcasted_iota(jnp.int32, (length, cells_y), 0)
    col = lax.broadcasted_iota(jnp.int32, (length, cells_y), 1)
    waves = dot_exact(jnp.concatenate([slab_ref[k] for k in range(per)], axis=0), dht)
    waves = jnp.concatenate(
        [waves[k * length : (k + 1) * length] for k in range(per)], axis=1
    )
    waves = dot_exact(dht, waves)
    parts = []
    for k in range(per):
        wave = orb * per + k
        anchor = (row == 0) & (col == 0) & (wave == 0)
        bent = curve_ref[...] + curve_z_ref[wave]
        factor = jnp.where(anchor, 0.0, COULOMB / jnp.where(anchor, 1.0, bent))
        parts.append(waves[:, k * cells_y : (k + 1) * cells_y] * factor)
    field = dot_exact(own, jnp.concatenate(parts, axis=1))
    field = jnp.concatenate(
        [field[:, k * cells_y : (k + 1) * cells_y] for k in range(per)], axis=0
    )
    field = dot_exact(field, dht)
    code, fine, top = scale_of(jnp.max(jnp.abs(field)))
    coded = jnp.round(field * (LEVELS / top)).astype(jnp.int32).astype(jnp.int16)
    code_rows = coded_rows(cells_y, (code, fine))
    rows = per * cells_x

    def spread(i, carry):
        q_ref[i, 0:rows, :] = coded
        q_ref[i, rows : rows + CODE_ROWS, :] = code_rows
        return carry

    lax.fori_loop(0, q_ref.shape[0], spread, 0, unroll=4)


def solve(curve_z, slab, dht, plane_curve, owners):
    per, length, cells_y = slab.shape
    vmem = pl.BlockSpec(memory_space=pltpu.VMEM)
    return pl.pallas_call(
        solve_kernel,
        in_specs=[pl.BlockSpec(memory_space=pltpu.SMEM), vmem, vmem, vmem],
        out_shape=jax.ShapeDtypeStruct((owners, per * (length // 2) + CODE_ROWS, cells_y), jnp.int16),
        compiler_params=params(0, 12),
        name="solve",
    )(curve_z, slab, dht, plane_curve)


def field_kernel(
    pitch,
    turn_pitch,
    got_ref,
    psi_ref,
    kin_ref,
    dht_ref,
    tz_ref,
    back_ref,
    rim_ref,
    slab_ref,
    sums_ref,
    waves,
    turn,
    head,
    values,
):
    step = pl.program_id(0)
    orbitals, cells_x, length, cells_y = psi_ref.shape
    some_x = cells_x // pl.num_programs(0)
    owners = got_ref.shape[0]
    per = length // owners
    rim = rim_ref.shape[2] // 2
    first = pl.multiple_of((lax.axis_index("orb") * per) // 8 * 8, 8)

    @pl.when(step == 0)
    def _():
        def unpack(source, carry):
            found, _ = unpacked(got_ref, source, per * cells_x)
            for k in range(per):
                at = pl.ds(pl.multiple_of((source * per + k) * pitch, 8), cells_x)
                waves[at, :] = found[k * cells_x : (k + 1) * cells_x]
            return carry

        lax.fori_loop(0, owners, unpack, 0, unroll=16)
        sums_ref[...] = kin_ref[...]

    group = 16
    energy = [jnp.zeros((8, cells_y), F32) for _ in range(orbitals)]
    for local in range(0, some_x, group):
        x = step * some_x + local
        field = hartley_pair(
            dht_ref[...],
            jnp.concatenate(
                [waves[pl.ds(x + k, length, stride=pitch), :] for k in range(group)], axis=1
            ),
        )
        values[local // group] = field
        own = values[local // group, pl.ds(first, 8), :]
        for k in range(group):
            slab_ref[local + k] = own[:, k * cells_y : (k + 1) * cells_y]
        products = []
        for o in range(orbitals):
            psi = jnp.concatenate([psi_ref[o, x + k] for k in range(group)], axis=1)
            psi = psi.astype(F32)
            product = field * psi
            products.append(product.astype(BF16))
            squares = product * psi
            for k in range(group):
                part = squares[:, k * cells_y : (k + 1) * cells_y]
                part = part.reshape(length // 8, 8, cells_y)
                energy[o] = energy[o] + jnp.sum(part, axis=0)
        back = dot(tz_ref[...], jnp.concatenate(products, axis=1))
        for o in range(orbitals):
            for k in range(group):
                at = (o * group + k) * cells_y
                row = o * length * turn_pitch + local + k
                turn[pl.ds(row, length, stride=turn_pitch), :] = back[:, at : at + cells_y]

    for o in range(orbitals):
        sums_ref[o, 0:8] = sums_ref[o, 0:8] + energy[o]

    def turned(o, z, start, count):
        row = pl.multiple_of((o * length + z) * turn_pitch, 8) + start
        return turn[pl.ds(row, count), :]

    def rows(z, carry):
        for o in range(orbitals):
            back_ref[o, z] = turned(o, z, 0, some_x).astype(BF16)
        return carry

    lax.fori_loop(0, length, rows, 0, unroll=16)

    @pl.when(step == 0)
    def _():
        def keep(z, carry):
            for o in range(orbitals):
                head[o, z] = turned(o, z, 0, rim)
            return carry

        lax.fori_loop(0, length, keep, 0, unroll=16)

    @pl.when(step == pl.num_programs(0) - 1)
    def _():
        def send(z, carry):
            for o in range(orbitals):
                both = jnp.concatenate([turned(o, z, some_x - rim, rim), head[o, z]], axis=0)
                rim_ref[o, z] = both.astype(BF16)
            return carry

        lax.fori_loop(0, length, send, 0, unroll=16)


def field(got, psi, kin_sums, dht, tz):
    orbitals, cells_x, length, cells_y = psi.shape
    some_x = 16
    pitch = cells_x + 8
    turn_pitch = some_x + 8
    rim = 8
    return pl.pallas_call(
        functools.partial(field_kernel, pitch, turn_pitch),
        grid=(cells_x // some_x,),
        in_specs=[
            pl.BlockSpec(memory_space=pltpu.VMEM),
            pl.BlockSpec(memory_space=pltpu.VMEM),
            whole(kin_sums),
            whole(dht),
            whole(tz),
        ],
        out_specs=[
            pl.BlockSpec((orbitals, length, some_x, cells_y), lambda i: (0, 0, i, 0)),
            pl.BlockSpec((orbitals, length, 2 * rim, cells_y), lambda i: (0, 0, 0, 0)),
            pl.BlockSpec((some_x, 8, cells_y), lambda i: (i, 0, 0)),
            whole(kin_sums),
        ],
        out_shape=[
            pltpu.HBM((orbitals, length, cells_x, cells_y), BF16),
            jax.ShapeDtypeStruct((orbitals, length, 2 * rim, cells_y), BF16),
            jax.ShapeDtypeStruct((cells_x, 8, cells_y), F32),
            jax.ShapeDtypeStruct(kin_sums.shape, F32),
        ],
        scratch_shapes=[
            pltpu.VMEM(((length + 1) * pitch, cells_y), F32),
            pltpu.VMEM(((orbitals * length + 1) * turn_pitch, cells_y), F32),
            pltpu.VMEM((orbitals, length, rim, cells_y), F32),
            pltpu.VMEM((1, length, 16 * cells_y), F32),
        ],
        compiler_params=params(1, 30),
        name="field",
    )(got, psi, kin_sums, dht, tz)


def update_kernel(
    sums_ref,
    other_ref,
    back_ref,
    rim_ref,
    c_ref,
    kin_ref,
    step_ref,
    tx_ref,
    ty_ref,
    out_ref,
    energy_ref,
):
    orbital = pl.program_id(0)

    @pl.when(pl.program_id(1) == 0)
    def _():
        both = sums_ref[orbital] + other_ref[orbital]
        energy_ref[orbital] = jnp.sum(both[0:8]) / jnp.sum(both[8:16])

    energy = energy_ref[orbital]
    some_z, cells_x, cells_y = back_ref.shape[1], back_ref.shape[2], back_ref.shape[3]
    tx = tx_ref[...]
    ty = ty_ref[...]
    block = 16
    many = 8

    def planes(i, carry):
        z0 = i * block
        crossed = []
        for p in range(0, block, many):
            some = range(p, p + many)
            flat = jnp.concatenate(
                [
                    jnp.concatenate([back_ref[0, z0 + k] for k in some], axis=1),
                    jnp.concatenate([rim_ref[0, z0 + k] for k in some], axis=1),
                ],
                axis=0,
            )
            both = dot(tx, flat).astype(BF16)
            crossed += [both[:, k * cells_y : (k + 1) * cells_y] for k in range(many)]
        potential = dot(jnp.concatenate(crossed, axis=0), ty)
        steps = step_ref[0, pl.ds(pl.multiple_of(z0, block), block), :]
        for p in range(block):
            z = z0 + p
            kin = kin_ref[0, z].astype(jnp.int32).astype(F32) * steps[p : p + 1]
            applied = potential[p * cells_x : (p + 1) * cells_x] + kin
            coeff = c_ref[0, z].astype(F32)
            out_ref[0, z] = (coeff - STEP_SIZE * (applied - energy * coeff)).astype(BF16)
        return carry

    lax.fori_loop(0, some_z // block, planes, 0, unroll=4)


def update(sums, other_sums, back, rim, c, kin, steps, tx, ty):
    orbitals, length, cells_x, cells_y = c.shape
    chunks = 2
    part = length // chunks
    block = pl.BlockSpec((1, part, cells_x, cells_y), lambda o, j: (o, j, 0, 0))
    return pl.pallas_call(
        update_kernel,
        grid=(orbitals, chunks),
        in_specs=[
            whole(sums),
            whole(other_sums),
            block,
            pl.BlockSpec((1, part, rim.shape[2], cells_y), lambda o, j: (o, j, 0, 0)),
            block,
            block,
            pl.BlockSpec((1, part, cells_y), lambda o, j: (o, j, 0)),
            whole(tx),
            whole(ty),
        ],
        out_specs=[block, pl.BlockSpec(memory_space=pltpu.SMEM)],
        out_shape=[
            jax.ShapeDtypeStruct(c.shape, BF16),
            jax.ShapeDtypeStruct((orbitals,), F32),
        ],
        compiler_params=params(2, 12),
        name="update",
    )(sums, other_sums, back, rim, c, kin, steps, tx, ty)


def to_other(array):
    return lax.ppermute(array, "grid", [(0, 1), (1, 0)])


def in_hbm(array):
    return pltpu.with_memory_space_constraint(array, pltpu.HBM)


def to_all(blocks):
    return lax.all_to_all(blocks, "orb", split_axis=0, concat_axis=0, tiled=True)


def on_device(coefficients, occupations, slot_orbital):
    orbitals, length, cells_x, cells_y = coefficients.shape
    owners = slot_orbital.shape[0] // orbitals
    per = length // owners
    magic, trans, kin_taps = magic_pairs(), transposed_pairs(), kinetic_pairs()
    magic_line = band_periodic(length, magic)
    trans_line = band_periodic(length, trans)
    kin_line = band_periodic(length, kin_taps, -0.5)
    inside = list(range(cells_x))
    near_cells = inside + with_rims(cells_x, 0, 8)
    all_cells = near_cells + with_rims(cells_x, 8, 16)
    dht = hartley(length)
    table = jnp.asarray(split_table(dht))
    waves = curve(length)

    c = in_hbm(coefficients)
    near = to_other(own_rims(c))
    psi, coded, own_far, peak = density(
        occupations,
        slot_orbital,
        coefficients,
        near,
        jnp.asarray(magic_line.T),
        jnp.asarray(band_columns(cells_x, near_cells, magic)),
        jnp.asarray(magic_line),
        table,
        owners,
    )
    got = to_all(coded)
    far = to_other(own_far)
    kin, steps, kin_sums = kinetic(
        c,
        near,
        far,
        jnp.asarray(kin_line.T),
        jnp.asarray(band_columns(cells_x, all_cells, kin_taps, -0.5)),
        jnp.asarray(kin_line),
        peak,
    )
    half = slab_sum(got, per * cells_x, per, kin_sums).reshape(per, cells_x, cells_y)
    slab = lax.all_gather(half, "grid", axis=1, tiled=True)
    spread = solve(
        jnp.asarray(waves.astype(np.float32)),
        slab,
        jnp.asarray(dht),
        jnp.asarray((waves[:, None] + waves[None, :]).astype(np.float32)),
        owners,
    )
    back, back_rims, slab_field, sums = field(
        to_all(spread), psi, kin_sums, table, jnp.asarray(trans_line)
    )
    updated, energies = update(
        sums,
        to_other(sums),
        in_hbm(back),
        to_other(back_rims),
        c,
        in_hbm(kin),
        steps,
        jnp.asarray(band_columns(cells_x, near_cells, trans)),
        jnp.asarray(trans_line.T),
    )
    first = lax.rem(lax.axis_index("orb") * per, 8)
    potential = lax.dynamic_slice_in_dim(slab_field, first, per, 1).transpose(1, 0, 2)
    return (updated, energies, potential)


def solution(mesh):
    return jax.shard_map(
        on_device,
        mesh=mesh,
        in_specs=(P("orb", None, "grid", None), P(), P()),
        out_specs=(P("orb", None, "grid", None), P("orb"), P("orb", "grid", None)),
        check_vma=False,
    )
```
